128 devices in a mesh: segment: 8 (over x, core), wide: 16 (over z, y).
Axes of the slice: x: 4, y: 4, z: 4, core: 2. Of those that a mesh axis runs over, the one named last changes fastest.
Arguments:
- prompt_states: bfloat16 [4, 256, 8192], P(None, None, 'wide')
- norm_gain: bfloat16 [8, 8192], P('segment', 'wide'), may hold values from 0.29882812 to 3
- w_latent: bfloat16 [8, 8192, 512], P('segment', 'wide'), may hold values from -0.0625 to 0.0625
- w_back: bfloat16 [8, 512, 8192], P('segment', None, 'wide'), may hold values from -0.25 to 0.25
- page_lists: int32 [8, 8, 1], replicated, may hold values from 0 to 7; in each aligned block of 8 rows (0 to 7, 8 to 15, ..., all dimensions but the last counted through in order) at most 2 rows name the same one
- queries: bfloat16 [128, 8, 64, 512], P('segment', None, 'wide'), may hold values from -64 to 64
- new_latent: bfloat16 [128, 8, 512], P('segment'), may hold values from -6 to 6
- context_lengths: int32 [128, 8], P('segment'), may hold values from 0 to 256
Outputs:
- attended: bfloat16 [128, 8, 64, 512], P('segment', None, 'wide')
The draws below stay inside these ranges and needn't reach their ends.
Inputs may be any that keep to these rules, and one draw needn't show every extreme that they name: Page p of layer l is sent to decode owner page_lists[l, p, 0]; no owner receives more than 2 pages of one layer, and exactly 2 in some layers.
All inputs are finite; a program needn't handle non-finite values.
Results may differ from the reference program's by a relative error of at most 0.03.
Values may be sent and summed in bfloat16 or wider, within the bound.
No kernel may reach another device: no remote copies, remote signals or barrier semaphores. Data moves between devices by JAX's collectives and lax.ppermute only.
A program may use at most 64 MiB of HBM per device.

```python
import math
import jax
import jax.numpy as jnp
import numpy as np
from jax import lax

D = 8192
LAT = 512
HEADS = 64
MB = 4
TOK_MB = 256
PAGE = 128
REQ_DEV = 16
LAYERS = 8
PAGES = 8
CAP = 2
REQ = 128
N_SEGMENT = 8
N_WIDE = 16


def shared_latent(key):
    values = jax.random.normal(jax.random.fold_in(key, 5), (REQ, LAYERS, LAT), jnp.float32)
    return jnp.clip(values, -6.0, 6.0)


def draw_prompt_states(key, part):
    key = jax.random.fold_in(key, 11)
    key_base = jax.random.fold_in(key, 0)
    columns = jnp.arange(D, dtype=jnp.float32) / (D - 1)
    rising = jnp.exp(jnp.log(3.0) * columns)
    values = jax.random.normal(key_base, (MB, TOK_MB, D), jnp.float32) * rising
    return values.astype(jnp.bfloat16)


def draw_new_latent(key, part):
    return shared_latent(key).astype(jnp.bfloat16)


def draw_queries(key, part):
    key = jax.random.fold_in(key, 23)
    key_base = jax.random.fold_in(key, 0)
    values = 2.0 * jnp.clip(jax.random.normal(key_base, (REQ, LAYERS, HEADS, LAT), jnp.float32), -6.0, 6.0)
    return jnp.clip(values, -64.0, 64.0).astype(jnp.bfloat16)


def with_ends(result, own_key, low, high):
    place = [jax.random.randint(jax.random.fold_in(own_key, axis), (), 0, length) for axis, length in enumerate(result.shape)]
    widest = result.shape.index(max(result.shape))
    beside = place[:widest] + [(place[widest] + 1) % result.shape[widest]] + place[widest + 1:]
    return result.at[tuple(place)].set(low).at[tuple(beside)].set(high)


def levels(own_key, extent, cuts, smallest, largest):
    level = 1.0
    for position, blocks in cuts:
        draws = jax.random.uniform(jax.random.fold_in(jax.random.fold_in(own_key, 6), position), (blocks,), jnp.float32, smallest / len(cuts), largest / len(cuts))
        level = level * jnp.repeat(jnp.exp(draws), extent[position] // blocks).reshape((-1,) + (1,) * (len(extent) - 1 - position))
    return level


def deal_out(key, own, number, rows, count, top, most, slope):
    sequence = jax.random.permutation(key, count)
    packed, common = portions_of(count, rows * top, most, slope, True), portions_of(count, rows * top, most, slope, False)
    places = jnp.arange(count)

    def named(sizes, offset_by):
        used = int((sizes > 0).sum())
        fixed = max(1, used // 4)
        shifted = fixed + (places - fixed + offset_by * (used - fixed)) % max(1, count - fixed)
        return jnp.zeros((count,), jnp.int32).at[sequence[jnp.where(places < fixed, places, shifted)]].set(jnp.asarray(sizes, jnp.int32))

    sizes = jnp.where(number % 4 == 0, named(packed, number // 4), named(common, number - number // 4 - 1))
    mixed = jax.random.permutation(jax.random.fold_in(own, 3), count)
    donor, taker = mixed[0:count // 2 * 2:2], mixed[1:count // 2 * 2:2]
    margin = jnp.minimum(sizes[donor] - 1, most - sizes[taker]) // 2
    margin = jnp.where((donor == sequence[0]) | (taker == sequence[0]) | (sizes[taker] == 0), 0, jnp.maximum(margin, 0))
    shifted = jax.random.randint(jax.random.fold_in(own, 4), (count // 2,), 0, 1 << 20) % (margin + 1)
    sizes = sizes.at[donor].add(-shifted).at[taker].add(shifted)
    items = jnp.searchsorted(jnp.cumsum(sizes), jnp.arange(rows * top), side="right").astype(jnp.int32)
    grid = items.reshape(top, rows).T
    grid = grid[jax.random.permutation(jax.random.fold_in(own, 1), rows)]
    offset_by = jax.random.randint(jax.random.fold_in(own, 2), (rows, 1), 0, top)
    return jnp.take_along_axis(grid, (jnp.arange(top)[None, :] + offset_by) % top, axis=1)


def portions_of(count, total, most, slope, full):
    portions = [(1 << 20) // math.isqrt(grade ** slope) + 1 for grade in range(1, count + 1)]
    largest = most if full else min(most, max(-(-total // count), total * portions[0] // sum(portions)))
    least = 1 if total - largest >= count - 1 else 0
    holding, rest = [largest] + [least] * (count - 1), total - largest - least * (count - 1)
    while rest > 0:
        free = [i for i in range(1, count) if holding[i] < largest] or [i for i in range(1, count) if holding[i] < most]
        mass, left = sum([portions[i] for i in free]), rest
        for i in free:
            extra = min(most - holding[i], max(1, left * portions[i] // mass), rest)
            holding[i] = holding[i] + extra
            rest = rest - extra
    return np.array(holding)


def bell_draw(stream_key, dims, scale, most, cuts=(), kind=jnp.bfloat16):
    level = levels(stream_key, dims, cuts, -0.22, 0.18) if cuts else 1.0
    array = jax.random.normal(stream_key, dims, jnp.float32) * scale * level
    return jnp.minimum(jnp.maximum(array, -most), most).astype(kind)


def setup_inputs(seed: int = 0) -> dict:
    splits = jax.random.split(jax.random.key(seed), 9)
    prompt_states = draw_prompt_states(jax.random.fold_in(splits[8], 71), 0)
    norm_gain = jnp.clip(jnp.exp(math.log(3.0) - 2.306499 * jax.random.uniform(splits[1], (LAYERS, D), jnp.float32) ** levels(splits[1], (LAYERS, D), ((0, 8), (1, 16)), -0.2, 0.2)), 0.29882812, 3.0).astype(jnp.bfloat16)
    w_latent = bell_draw(splits[2], (LAYERS, D, LAT), D ** -0.5, 0.0625, ((0, 8), (1, 16)))
    w_back = bell_draw(splits[3], (LAYERS, LAT, D), LAT ** -0.5, 0.25, ((0, 8), (2, 16)))
    page_lists_keys = jax.random.split(jax.random.fold_in(splits[4], 1), LAYERS * PAGES // PAGES)
    page_lists_turns = jax.random.permutation(jax.random.fold_in(splits[4], 3), LAYERS * PAGES // PAGES)
    page_lists = jax.vmap(lambda own, number: deal_out(jax.random.fold_in(splits[4], 2), own, number, PAGES, N_SEGMENT, 1, CAP, 1))(page_lists_keys, page_lists_turns).reshape((LAYERS, PAGES, 1))
    queries = draw_queries(jax.random.fold_in(splits[8], 71), 0)
    new_latent = draw_new_latent(jax.random.fold_in(splits[8], 71), 0)
    context_lengths = with_ends(jax.random.randint(splits[7], (REQ, LAYERS), 0, CAP * PAGE + 1), jax.random.fold_in(splits[7], 1), 0, CAP * PAGE).astype(jnp.int32)
    return {"prompt_states": prompt_states, "norm_gain": norm_gain, "w_latent": w_latent, "w_back": w_back, "page_lists": page_lists, "queries": queries, "new_latent": new_latent, "context_lengths": context_lengths}


eps_norm = 1e-06
score_scale = 192.0 ** (-0.5)

def page_ranks(targets):
    count = targets.shape[-1]
    order = jnp.arange(count, dtype=jnp.int32)
    earlier = order[None, :] < order[:, None]
    same = targets[..., :, None] == targets[..., None, :]
    return lax.optimization_barrier(jnp.sum((same & earlier).astype(jnp.int32), axis=-1))

def latent_layer(state, gain, w_lat, w_out):
    values = state.astype(jnp.float32)
    inverse_rms = lax.rsqrt(lax.optimization_barrier(jnp.mean(values * values, axis=1)) + eps_norm)
    normed = (values * inverse_rms[:, None] * gain.astype(jnp.float32)[None, :]).astype(jnp.bfloat16)
    pieces = normed.reshape(state.shape[0], N_WIDE, D // N_WIDE).astype(jnp.float32)
    blocks = w_lat.reshape(N_WIDE, D // N_WIDE, LAT).astype(jnp.float32)
    partial_terms = jnp.einsum('tnd,ndc->ntc', pieces, blocks)
    latent = lax.optimization_barrier(jnp.sum(partial_terms, axis=0)).astype(jnp.bfloat16)
    activated = jax.nn.silu(latent.astype(jnp.float32)).astype(jnp.bfloat16)
    update = jnp.dot(activated, w_out, preferred_element_type=jnp.float32)
    return ((values + update).astype(jnp.bfloat16), latent)

def decode_block(owner_queries, keys, owner_new, limit):
    positions = jnp.arange(keys.shape[1], dtype=jnp.int32)
    readable = positions[None, None, :] < limit[:, :, None]
    query_values = owner_queries.astype(jnp.float32)
    scores = jnp.einsum('rlhc,lkc->rlhk', query_values, keys.astype(jnp.float32)) * score_scale
    scores = jnp.where(readable[:, :, None, :], scores, -jnp.inf)
    own_score = jnp.einsum('rlhc,rlc->rlh', query_values, owner_new.astype(jnp.float32)) * score_scale
    top = jnp.maximum(lax.optimization_barrier(jnp.max(scores, axis=-1)), own_score)
    weights = jnp.exp(scores - top[..., None])
    own_weight = jnp.exp(own_score - top)
    total = lax.optimization_barrier(jnp.sum(weights, axis=-1)) + own_weight
    weights_b = weights.astype(jnp.bfloat16).astype(jnp.float32)
    numer = jnp.einsum('rlhk,lkc->rlhc', weights_b, keys.astype(jnp.float32))
    numer = numer + own_weight[..., None] * owner_new.astype(jnp.float32)[:, :, None, :]
    return (numer / total[..., None]).astype(jnp.bfloat16)

def reference(prompt_states, norm_gain, w_latent, w_back, page_lists, queries, new_latent, context_lengths):
    state = prompt_states.reshape(MB * TOK_MB, D)
    layer_latents = []
    for layer in range(LAYERS):
        state, latent = latent_layer(state, norm_gain[layer], w_latent[layer], w_back[layer])
        layer_latents.append(latent)
    pages = jnp.stack(layer_latents).reshape(LAYERS, PAGES, PAGE, LAT).astype(jnp.float32)
    targets = page_lists[:, :, 0]
    slot_rank = page_ranks(targets)
    slot_ids = jnp.arange(CAP, dtype=jnp.int32)
    query_groups = queries.reshape(N_SEGMENT, REQ_DEV, LAYERS, HEADS, LAT)
    new_groups = new_latent.reshape(N_SEGMENT, REQ_DEV, LAYERS, LAT)
    length_groups = context_lengths.reshape(N_SEGMENT, REQ_DEV, LAYERS)

    def owner_output(inputs):
        owner, owner_queries, owner_new, owner_lengths = inputs
        mine = targets == owner
        chosen = (mine[:, None, :] & (slot_rank[:, None, :] == slot_ids[None, :, None])).astype(jnp.float32)
        keys = jnp.einsum('ljp,lptc->ljtc', chosen, pages).astype(jnp.bfloat16).reshape(LAYERS, CAP * PAGE, LAT)
        counts = lax.optimization_barrier(jnp.sum(mine.astype(jnp.int32), axis=1))
        limit = jnp.minimum(owner_lengths, counts[None, :] * PAGE)
        return decode_block(owner_queries, keys, owner_new, limit)
    owners = jnp.arange(N_SEGMENT, dtype=jnp.int32)
    results = lax.map(owner_output, (owners, query_groups, new_groups, length_groups))
    return results.reshape(REQ, LAYERS, HEADS, LAT)
```

```python
import jax
import jax.numpy as jnp
from jax import lax
from jax.sharding import PartitionSpec as P

PAGE = 128
LANES = 128

eps_norm = 1e-06
score_scale = 192.0 ** (-0.5)

GROUPS = ((0,), (1,), (2,), (3,), (4,), (5,), (6,), (7,))


def dot(a, b):
    return jnp.dot(a, b, preferred_element_type=jnp.float32)


def dot_t(a, b):
    return lax.dot_general(a, b, (((1,), (1,)), ((), ())), preferred_element_type=jnp.float32)


def square_columns(state):
    values = state.astype(jnp.float32)
    squares = jnp.sum(values * values, axis=1, keepdims=True)
    high = squares.astype(jnp.bfloat16)
    low = (squares - high.astype(jnp.float32)).astype(jnp.bfloat16)
    column = lax.broadcasted_iota(jnp.int32, (state.shape[0], LANES), 1)
    return jnp.where(column == 0, high, jnp.where(column == 1, low, jnp.zeros_like(low)))


def scatter_sum(parts, axis):
    size = lax.axis_size(axis)
    rows = parts.shape[0] // size
    sent = parts.reshape(size, rows, parts.shape[1])
    received = lax.all_to_all(sent, axis, 0, 0, tiled=True)
    return jnp.sum(received.astype(jnp.float32), axis=0)


def gathered(block, axis):
    size = lax.axis_size(axis)
    sent = jnp.broadcast_to(block[None], (size,) + block.shape)
    return lax.all_to_all(sent, axis, 0, 0, tiled=True)


def silu(latent):
    return jax.nn.silu(latent.astype(jnp.float32)).astype(jnp.bfloat16)


def decode_block(owner_queries, keys, owner_new, limit):
    positions = jnp.arange(keys.shape[1], dtype=jnp.int32)
    readable = positions[None, None, :] < limit[:, :, None]
    scores = (
        jnp.einsum("rlhc,lkc->rlhk", owner_queries, keys, preferred_element_type=jnp.float32)
        * score_scale
    )
    scores = jnp.where(readable[:, :, None, :], scores, -jnp.inf)
    own_score = (
        jnp.einsum("rlhc,rlc->rlh", owner_queries, owner_new, preferred_element_type=jnp.float32)
        * score_scale
    )
    top = jnp.maximum(jnp.max(scores, axis=-1), own_score)
    weights = jnp.exp(scores - top[..., None])
    own_weight = jnp.exp(own_score - top)
    total = jnp.sum(weights, axis=-1) + own_weight
    numer = jnp.einsum(
        "rlhk,lkc->rlhc", weights.astype(jnp.bfloat16), keys, preferred_element_type=jnp.float32
    )
    numer = numer + own_weight[..., None] * owner_new.astype(jnp.float32)[:, :, None, :]
    return (numer / total[..., None]).astype(jnp.bfloat16)


def shards(
    prompt_states, norm_gain, w_latent, w_back, page_lists, queries, new_latent, context_lengths
):
    segments = lax.axis_size("segment")
    wide_size = lax.axis_size("wide")
    position = lax.axis_index("segment")
    core = position % 2
    batches, tok_rows, local_width = prompt_states.shape
    width = local_width * wide_size
    tokens = batches * tok_rows
    mine = tokens // segments
    layers = segments
    lat = w_latent.shape[2]

    gained = (
        w_latent[0].astype(jnp.float32) * norm_gain[0].astype(jnp.float32)[:, None]
    ).astype(jnp.bfloat16)
    back = w_back[0]

    first = lax.all_gather(jnp.where(core == 0, back, gained), "segment", axis=0)
    second = lax.all_gather(jnp.where(core == 0, gained, back), "segment", axis=0)

    def latent_weight(layer):
        return (second if layer % 2 == 0 else first)[layer]

    def back_weight(layer):
        return (first if layer % 2 == 0 else second)[layer]

    states = prompt_states.reshape(tokens, local_width)
    state = lax.dynamic_slice_in_dim(states, position * mine, mine, 0)
    lent = lax.ppermute(gained, "segment", [(0, 1)])
    home_weight = jnp.where(position == 0, gained, lent)
    by_core = states.reshape(segments // 2, 2, mine, local_width)
    turn = lax.dynamic_index_in_dim(by_core, core, 1, keepdims=False)
    home = dot(turn.reshape(tokens // 2, local_width), home_weight).astype(jnp.bfloat16)
    home = home.reshape(segments // 2, mine, lat)
    product = jnp.where(position < 2, home[0], jnp.zeros_like(home[0]))
    for hop in range(1, segments // 2):
        product = product + lax.ppermute(
            home[hop], "segment", [(0, 2 * hop), (1, 2 * hop + 1)]
        )

    pages = []
    for number, group in enumerate(GROUPS):
        last = number == len(GROUPS) - 1
        (layer,) = group
        if number > 0:
            update = dot(activated, back_weight(layer - 1))
            state = (state.astype(jnp.float32) + update).astype(jnp.bfloat16)
            product = dot(state, latent_weight(layer)).astype(jnp.bfloat16)
        summed = scatter_sum(jnp.concatenate([product, square_columns(state)], axis=1), "wide")
        squares = summed[:, lat : lat + 1] + summed[:, lat + 1 : lat + 2]
        inverse_rms = lax.rsqrt(squares / width + eps_norm)
        latent = (summed[:, :lat] * inverse_rms).astype(jnp.bfloat16)
        if not last:
            whole = gathered(latent, "wide").reshape(mine, lat)
            activated = silu(whole)
            pages.append(lax.all_gather(whole, "segment", axis=0))

    targets = page_lists[:, :, 0]
    owned = targets == position
    counts = jnp.sum(owned.astype(jnp.int32), axis=1)
    order = jnp.arange(targets.shape[1], dtype=jnp.int32)[None, :]
    none = targets.shape[1]
    slot0 = jnp.min(jnp.where(owned, order, none), axis=1)
    slot1 = jnp.min(jnp.where(owned & (order > slot0[:, None]), order, none), axis=1)
    slot0 = jnp.minimum(slot0, none - 1)
    slot1 = jnp.minimum(slot1, none - 1)

    keys = []
    for layer in range(layers - 1):
        here = pages[layer]
        keys.append(jnp.concatenate([here[slot0[layer]], here[slot1[layer]]], axis=0))
    spread = gathered(latent, "segment")
    chosen = jnp.concatenate(
        [spread[slot0[layers - 1]], spread[slot1[layers - 1]]], axis=1
    )
    ends = gathered(chosen, "wide").reshape(mine, 2 * lat)
    keys.append(jnp.concatenate([ends[:, :lat], ends[:, lat:]], axis=0))
    keys = jnp.stack(keys)
    limit = jnp.minimum(context_lengths, counts[None, :] * PAGE)
    return decode_block(queries, keys, new_latent, limit)


def solution(mesh):
    in_specs = (
        P(None, None, "wide"),
        P("segment", "wide"),
        P("segment", "wide", None),
        P("segment", None, "wide"),
        P(),
        P("segment", None, "wide", None),
        P("segment", None, None),
        P("segment", None),
    )
    out_specs = P("segment", None, "wide", None)
    return jax.shard_map(shards, mesh=mesh, in_specs=in_specs, out_specs=out_specs, check_vma=False)
```

```python
import functools

import jax
import jax.numpy as jnp
from jax import lax
from jax.experimental import pallas as pl
from jax.experimental.pallas import tpu as pltpu
from jax.sharding import PartitionSpec as P

PAGE = 128
LANES = 128

eps_norm = 1e-06
score_scale = 192.0 ** (-0.5)


def dot(a, b):
    return jnp.dot(a, b, preferred_element_type=jnp.float32)


def dot_t(a, b):
    return lax.dot_general(a, b, (((1,), (1,)), ((), ())), preferred_element_type=jnp.float32)


def square_columns(state):
    values = state.astype(jnp.float32)
    squares = jnp.sum(values * values, axis=1, keepdims=True)
    high = squares.astype(jnp.bfloat16)
    low = (squares - high.astype(jnp.float32)).astype(jnp.bfloat16)
    column = lax.broadcasted_iota(jnp.int32, (state.shape[0], LANES), 1)
    return jnp.where(column == 0, high, jnp.where(column == 1, low, jnp.zeros_like(low)))


def scatter_sum(parts, axis):
    size = lax.axis_size(axis)
    rows = parts.shape[0] // size
    sent = parts.reshape(size, rows, parts.shape[1])
    received = lax.all_to_all(sent, axis, 0, 0, tiled=True)
    return jnp.sum(received.astype(jnp.float32), axis=0)


def gathered(block, axis):
    size = lax.axis_size(axis)
    sent = jnp.broadcast_to(block[None], (size,) + block.shape)
    return lax.all_to_all(sent, axis, 0, 0, tiled=True)


def silu(latent):
    return jax.nn.silu(latent.astype(jnp.float32)).astype(jnp.bfloat16)


def core_swap(x):
    length = lax.axis_size("segment")
    return lax.ppermute(x, "segment", [(i, i ^ 1) for i in range(length)])


def along_x(x):
    length = lax.axis_size("segment")
    groups = [list(range(core, length, 2)) for core in range(2)]
    return lax.all_gather(x, "segment", axis=0, axis_index_groups=groups)


def decode_kernel(slots, q_ref, new_ref, limit_ref, first_ref, second_ref, *rest):
    out_ref = rest[-1]
    requests, _, heads, lat = q_ref.shape
    rows = requests * heads
    q = q_ref[...].reshape(rows, lat)
    row = lax.broadcasted_iota(jnp.int32, (rows, requests), 0)
    start = lax.broadcasted_iota(jnp.int32, (rows, requests), 1) * heads
    pick = jnp.where((row >= start) & (row < start + heads), 1.0, 0.0).astype(jnp.bfloat16)
    own = dot(pick, new_ref[...].reshape(requests, lat))
    keys = jnp.concatenate([first_ref[0], second_ref[0]], axis=0)
    scores = dot_t(q, keys) * score_scale
    place = lax.broadcasted_iota(jnp.int32, scores.shape, 1)
    scores = jnp.where(place < limit_ref[0], scores, -jnp.inf)
    own_score = jnp.sum(q.astype(jnp.float32) * own, axis=1, keepdims=True) * score_scale
    top = jnp.maximum(jnp.max(scores, axis=1, keepdims=True), own_score)
    weights = jnp.exp(scores - top)
    own_weight = jnp.exp(own_score - top)
    total = jnp.sum(weights, axis=1, keepdims=True) + own_weight
    numer = dot(weights.astype(jnp.bfloat16), keys) + own_weight * own
    out_ref[...] = (numer / total).astype(jnp.bfloat16).reshape(out_ref.shape)


def decode_pair(layer, slots, queries, new, limit, pages, carried, in_order):
    requests, _, heads, lat = queries.shape

    def page(which):
        if in_order:
            return pl.BlockSpec((1, PAGE, lat), lambda i, s: (which, 0, i))
        return pl.BlockSpec((1, PAGE, lat), lambda i, s: (s[2 * (layer + i) + which], 0, i))

    in_specs = [
        pl.BlockSpec((requests, 1, heads, lat), lambda i, s: (0, layer + i, 0, 0)),
        pl.BlockSpec((1, requests, lat), lambda i, s: (layer + i, 0, 0)),
        pl.BlockSpec((1, requests * heads, 1), lambda i, s: (layer + i, 0, 0)),
        page(0),
        page(1),
    ]
    operands = [slots, queries, new, limit, pages, pages]
    aliases = {}
    if carried is not None:
        in_specs.append(pl.BlockSpec(memory_space=pl.ANY))
        aliases = {len(operands): 0}
        operands.append(carried)
    return pl.pallas_call(
        decode_kernel,
        grid_spec=pltpu.PrefetchScalarGridSpec(
            num_scalar_prefetch=1,
            grid=(2,),
            in_specs=in_specs,
            out_specs=pl.BlockSpec((requests, 1, heads, lat), lambda i, s: (0, layer + i, 0, 0)),
        ),
        out_shape=jax.ShapeDtypeStruct(queries.shape, jnp.bfloat16),
        input_output_aliases=aliases,
        compiler_params=pltpu.CompilerParams(vmem_limit_bytes=16 * 1024 * 1024),
        cost_estimate=pl.CostEstimate(
            flops=2 * 4 * requests * heads * 2 * PAGE * lat,
            bytes_accessed=2 * 2 * (2 * requests * heads + 2 * PAGE) * lat,
            transcendentals=2 * requests * heads * 2 * PAGE,
        ),
    )(*operands)


def shards(
    prompt_states, norm_gain, w_latent, w_back, page_lists, queries, new_latent, context_lengths
):
    segments = lax.axis_size("segment")
    wide_size = lax.axis_size("wide")
    position = lax.axis_index("segment")
    core = position & 1
    batches, tok_rows, local_width = prompt_states.shape
    width = local_width * wide_size
    tokens = batches * tok_rows
    mine = tokens // segments
    layers = segments
    lat = w_latent.shape[2]

    gained = (
        w_latent[0].astype(jnp.float32) * norm_gain[0].astype(jnp.float32)[:, None]
    ).astype(jnp.bfloat16)
    back = w_back[0]

    first = along_x(jnp.where(core == 0, back, gained))
    second = along_x(jnp.where(core == 0, gained, back))
    first_swapped = core_swap(first)
    second_swapped = core_swap(second)

    def latent_weight(layer):
        a, b = (second, second_swapped) if layer % 2 == 0 else (first_swapped, first)
        return jnp.where(core == 0, a[layer // 2], b[layer // 2])

    def back_weight(layer):
        a, b = (first, first_swapped) if layer % 2 == 0 else (second_swapped, second)
        return jnp.where(core == 0, a[layer // 2], b[layer // 2])

    states = prompt_states.reshape(tokens, local_width)
    state = lax.dynamic_slice_in_dim(states, position * mine, mine, 0)
    lent = lax.ppermute(
        jnp.where(position == 0, gained, back),
        "segment",
        [(i, i + 1) for i in range(0, segments, 2)],
    )
    home_weight = jnp.where(position == 0, gained, lent)
    by_core = states.reshape(segments // 2, 2, mine, local_width)
    turn = lax.dynamic_index_in_dim(by_core, core, 1, keepdims=False)
    home = dot(turn.reshape(tokens // 2, local_width), home_weight).astype(jnp.bfloat16)
    home = home.reshape(segments // 2, mine, lat)
    product = jnp.where(position < 2, home[0], jnp.zeros_like(home[0]))
    for hop in range(1, segments // 2):
        product = product + lax.ppermute(
            home[hop], "segment", [(0, 2 * hop), (1, 2 * hop + 1)]
        )

    cross = jnp.where(core == 0, dot_t(back, back), dot(lent, gained)).astype(jnp.bfloat16)
    share = lat // wide_size // (mine // wide_size)
    cross = cross.reshape(wide_size, share, mine // wide_size, lat)
    cross = [cross[:, part].reshape(mine, lat) for part in range(share)]

    def normed(total, squares):
        return (total * lax.rsqrt(squares / width + eps_norm)).astype(jnp.bfloat16)

    summed = scatter_sum(jnp.concatenate([product, square_columns(state)] + cross, axis=1), "wide")
    squares = summed[:, lat : lat + 1] + summed[:, lat + 1 : lat + 2]
    latent = normed(summed[:, :lat], squares)
    block = jnp.concatenate([latent, summed[:, lat + LANES :].astype(jnp.bfloat16)], axis=1)
    got = gathered(block, "wide")
    whole0 = got[:, :, :lat].reshape(mine, lat)
    cross = got[:, :, lat:].reshape(wide_size, mine // wide_size, share, lat)
    cross = along_x(cross.transpose(0, 2, 1, 3).reshape(lat, lat))
    cross_swapped = core_swap(cross)
    state = (state.astype(jnp.float32) + dot(silu(whole0), back_weight(0))).astype(jnp.bfloat16)

    product = dot(state, latent_weight(1)).astype(jnp.bfloat16)
    summed = scatter_sum(jnp.concatenate([product, square_columns(state)], axis=1), "wide")
    squares = summed[:, lat : lat + 1] + summed[:, lat + 1 : lat + 2]
    latent = normed(summed[:, :lat], squares)
    whole1 = gathered(latent, "wide").reshape(mine, lat)
    state = (state.astype(jnp.float32) + dot(silu(whole1), back_weight(1))).astype(jnp.bfloat16)
    pages = [lax.all_gather(jnp.concatenate([whole0, whole1], axis=1), "segment", axis=0)]

    for pair in range(1, layers // 2):
        even, odd = 2 * pair, 2 * pair + 1
        back_even = back_weight(even)
        mixing = jnp.where(core == 0, cross_swapped[pair], cross[pair])
        gram = jnp.where(core == 0, cross[pair], cross_swapped[pair])
        parts = [
            dot(state, latent_weight(even)).astype(jnp.bfloat16),
            dot(state, latent_weight(odd)).astype(jnp.bfloat16),
            dot_t(state, back_even).astype(jnp.bfloat16),
            square_columns(state),
        ]
        summed = scatter_sum(jnp.concatenate(parts, axis=1), "wide")
        squares = summed[:, 3 * lat : 3 * lat + 1] + summed[:, 3 * lat + 1 : 3 * lat + 2]
        latent_even = normed(summed[:, :lat], squares)
        activated = silu(latent_even)
        values = activated.astype(jnp.float32)
        towards = 2.0 * summed[:, 2 * lat : 3 * lat] + dot(activated, gram)
        squares = squares + jnp.sum(values * towards, axis=1, keepdims=True)
        latent_odd = normed(summed[:, lat : 2 * lat] + dot(activated, mixing), squares)
        latent = jnp.concatenate([latent_even, latent_odd], axis=1)
        if odd < layers - 1:
            whole = gathered(latent, "wide").reshape(mine, 2 * lat)
            activated = silu(whole)
            update = dot(activated[:, :lat], back_even) + dot(activated[:, lat:], back_weight(odd))
            state = (state.astype(jnp.float32) + update).astype(jnp.bfloat16)
            pages.append(lax.all_gather(whole, "segment", axis=0))

    targets = page_lists[:, :, 0]
    owned = targets == position
    counts = jnp.sum(owned.astype(jnp.int32), axis=1)
    none = targets.shape[1]
    order = jnp.arange(none, dtype=jnp.int32)[None, :]
    slot0 = jnp.min(jnp.where(owned, order, none), axis=1)
    slot1 = jnp.min(jnp.where(owned & (order > slot0[:, None]), order, none), axis=1)
    slots = jnp.minimum(jnp.stack([slot0, slot1], axis=1), none - 1)
    limit = jnp.minimum(context_lengths, counts[None, :] * PAGE)
    limit = jnp.repeat(limit.T, queries.shape[2], axis=1)[:, :, None]
    new = new_latent.transpose(1, 0, 2)

    flat_slots = slots.reshape(-1)
    out = None
    for pair, held in enumerate(pages):
        out = decode_pair(2 * pair, flat_slots, queries, new, limit, held, out, False)

    spread = gathered(latent, "segment")
    chosen = [
        lax.dynamic_index_in_dim(spread, slots[layers - 2 + i, which], 0, keepdims=False)[
            :, i * lat : (i + 1) * lat
        ]
        for which in range(2)
        for i in range(2)
    ]
    ends = gathered(jnp.concatenate(chosen, axis=1), "wide").reshape(mine, 4 * lat)
    ends = jnp.stack([ends[:, : 2 * lat], ends[:, 2 * lat :]])
    return decode_pair(layers - 2, flat_slots, queries, new, limit, ends, out, True)


def solution(mesh):
    in_specs = (
        P(None, None, "wide"),
        P("segment", "wide"),
        P("segment", "wide", None),
        P("segment", None, "wide"),
        P(),
        P("segment", None, "wide", None),
        P("segment", None, None),
        P("segment", None),
    )
    out_specs = P("segment", None, "wide", None)
    return jax.shard_map(shards, mesh=mesh, in_specs=in_specs, out_specs=out_specs, check_vma=False)
```

```python
import functools

import jax
import jax.numpy as jnp
from jax import lax
from jax.experimental import pallas as pl
from jax.experimental.pallas import tpu as pltpu
from jax.sharding import PartitionSpec as P

PAGE = 128
LANES = 128

eps_norm = 1e-06
score_scale = 192.0 ** (-0.5)

params = pltpu.CompilerParams(vmem_limit_bytes=24 * 1024 * 1024)
anywhere = pl.BlockSpec(memory_space=pl.ANY)
bf16 = jnp.bfloat16
f32 = jnp.float32


def dot(a, b):
    return jnp.dot(a, b, preferred_element_type=jnp.float32)


def dot_t(a, b):
    return lax.dot_general(a, b, (((1,), (1,)), ((), ())), preferred_element_type=jnp.float32)


def square_columns(values):
    squares = jnp.sum(values * values, axis=1, keepdims=True)
    high = squares.astype(bf16).astype(f32)
    column = lax.broadcasted_iota(jnp.int32, (values.shape[0], LANES), 1)
    return jnp.where(column == 0, high, jnp.where(column == 1, squares - high, 0.0))


def silu(latent):
    values = latent.astype(f32)
    return (values / (1.0 + jnp.exp(-values))).astype(bf16)


def exchanged(sent, axis):
    return lax.all_to_all(sent, axis, 0, 0, tiled=True)


def whole(shape):
    return pl.BlockSpec(shape, lambda i, *s: (0,) * len(shape))


def call(body, in_specs, out_specs, out_shape, operands, scalars=(), scratch=(), flops=0):
    moved = sum(o.size * 2 for o in out_shape)
    return pl.pallas_call(
        body,
        grid_spec=pltpu.PrefetchScalarGridSpec(
            num_scalar_prefetch=len(scalars),
            grid=(1,),
            in_specs=in_specs,
            out_specs=out_specs,
            scratch_shapes=scratch,
        ),
        out_shape=out_shape,
        compiler_params=params,
        cost_estimate=pl.CostEstimate(flops=flops, bytes_accessed=2 * moved, transcendentals=0),
    )(*scalars, *operands)


def weights_kernel(where, latent_ref, gain_ref, back_ref, both_ref, lent_ref):
    size = latent_ref.shape[1]
    row = lax.broadcasted_iota(jnp.int32, (size, size), 0)
    column = lax.broadcasted_iota(jnp.int32, (size, size), 1)
    gains = jnp.where(row == column, gain_ref[...].astype(f32), 0.0).astype(bf16)
    gained = dot(gains, latent_ref[0]).astype(bf16)
    both_ref[0] = gained
    both_ref[1] = back_ref[0]

    @pl.when(where[0] == 0)
    def _():
        lent_ref[...] = gained

    @pl.when(where[0] != 0)
    def _():
        lent_ref[...] = back_ref[0]


def home_kernel(where, states_ref, both_ref, lent_ref, out_ref, weight, cross):
    groups, _, rows, width = states_ref.shape
    lat = both_ref.shape[2]
    wide = out_ref.shape[0]

    @pl.when(where[0] == 0)
    def _():
        weight[...] = both_ref[0]

    @pl.when(where[0] != 0)
    def _():
        weight[...] = lent_ref[...]

    @pl.when(where[1] == 0)
    def _():
        cross[...] = dot_t(both_ref[1], both_ref[1])

    @pl.when(where[1] != 0)
    def _():
        cross[...] = dot(lent_ref[...], both_ref[0])

    share = rows // wide
    for group in range(groups):
        tokens = states_ref[group, 0]
        at = slice(group * share, (group + 1) * share)
        out_ref[:, at, :lat] = dot(tokens, weight[...]).reshape(wide, share, lat).astype(bf16)
        squares = square_columns(tokens.astype(f32))
        out_ref[:, at, lat : lat + LANES] = squares.reshape(wide, share, LANES).astype(bf16)
    out_ref[:, :, lat + LANES :] = cross[...].reshape(wide, lat // wide, lat).astype(bf16)


def home_sum_kernel(width, got_ref, latent_ref, cross_ref):
    lat = cross_ref.shape[1]
    summed = jnp.sum(got_ref[...].astype(f32), axis=0)
    squares = summed[:, lat : lat + 1] + summed[:, lat + 1 : lat + 2]
    latent = summed[:, :lat] * lax.rsqrt(squares / width + eps_norm)
    latent_ref[...] = latent.reshape(latent_ref.shape).astype(bf16)
    cross_ref[...] = summed[:, lat + LANES :].astype(bf16)


def home_send_kernel(where, mine_ref, a_ref, b_ref, c_ref, cross_ref, out_ref):
    wide = out_ref.shape[0]
    high = cross_ref.shape[0]
    taken = a_ref[...].astype(f32) + b_ref[...].astype(f32) + c_ref[...].astype(f32)
    latent = jnp.where(where[0] < 2, mine_ref[0].astype(f32), taken).astype(bf16)
    block = cross_ref[...]
    for place in range(wide):
        out_ref[place, :high] = block
        out_ref[place, high:] = latent


def advance_kernel(before, layers, first, where, got_ref, *refs):
    if first:
        states_ref, both_ref, out_ref, state_ref, held_ref, weights, sems = refs
    elif len(before) < len(layers):
        earlier_ref, states_ref, both_ref, out_ref, state_ref, held_ref, weights, sems = refs
    else:
        states_ref, both_ref, out_ref, state_ref, weights, sems = refs
    needed = [(layer, 1) for layer in before] + [(layer, 0) for layer in layers]
    if len(layers) == 2:
        needed.append((layers[0], 1))
    copies = [
        pltpu.make_async_copy(both_ref.at[layer, kind], weights.at[i], sems.at[i])
        for i, (layer, kind) in enumerate(needed)
    ]
    for copy in copies:
        copy.start()
    wide = out_ref.shape[0]
    share = out_ref.shape[1]
    rows = wide * share
    lat = weights.shape[2]
    got = got_ref[...]
    if first:
        held_ref[...] = got[:, : got.shape[1] - share]
        got = got[:, got.shape[1] - share :]
    latents = got.astype(f32).reshape(rows, got.shape[2])
    if not first and len(before) < len(layers):
        earlier = earlier_ref[:, earlier_ref.shape[1] - share :]
        held_ref[:, :lat] = earlier.astype(f32).reshape(rows, lat).astype(bf16)
        held_ref[:, lat:] = latents.astype(bf16)
    activated = silu(latents)
    state = states_ref[...].reshape(rows, lat).astype(f32)
    for i in range(len(before)):
        copies[i].wait()
        state = state + dot(activated[:, i * lat : (i + 1) * lat], weights[i])
    state = state.astype(bf16)
    state_ref[...] = state
    squares = square_columns(state.astype(f32))
    out_ref[:, :, :LANES] = squares.reshape(wide, share, LANES).astype(bf16)
    for i in range(len(before), len(needed)):
        copies[i].wait()
        product = (dot_t if needed[i][1] else dot)(state, weights[i])
        at = LANES + (i - len(before)) * lat
        out_ref[:, :, at : at + lat] = product.reshape(wide, share, lat).astype(bf16)


def single_kernel(width, got_ref, out_ref):
    summed = jnp.sum(got_ref[...].astype(f32), axis=0)
    squares = summed[:, 0:1] + summed[:, 1:2]
    latent = (summed[:, LANES:] * lax.rsqrt(squares / width + eps_norm)).astype(bf16)
    for place in range(out_ref.shape[0]):
        out_ref[place] = latent


def pair_kernel(width, even, got_ref, cross_ref, out_ref, crosses, sems):
    copies = [
        pltpu.make_async_copy(cross_ref.at[even + i], crosses.at[i], sems.at[i]) for i in range(2)
    ]
    for copy in copies:
        copy.start()
    lat = crosses.shape[2]
    summed = jnp.sum(got_ref[...].astype(f32), axis=0)
    squares = summed[:, 0:1] + summed[:, 1:2]
    at = [LANES + i * lat for i in range(4)]
    first = (summed[:, at[0] : at[1]] * lax.rsqrt(squares / width + eps_norm)).astype(bf16)
    activated = silu(first)
    copies[0].wait()
    towards = 2.0 * summed[:, at[2] : at[3]] + dot(activated, crosses[0])
    squares = squares + jnp.sum(activated.astype(f32) * towards, axis=1, keepdims=True)
    copies[1].wait()
    second = summed[:, at[1] : at[2]] + dot(activated, crosses[1])
    second = (second * lax.rsqrt(squares / width + eps_norm)).astype(bf16)
    for place in range(out_ref.shape[0]):
        out_ref[place, :, :lat] = first
        out_ref[place, :, lat:] = second


def choose_kernel(layer, slots, got_ref, out_ref):
    lat = got_ref.shape[2] // 2
    parts = []
    for i in range(2):
        for which in range(2):
            shard = got_ref[slots[2 * (layer + i) + which]]
            parts.append(shard[:, i * lat : (i + 1) * lat])
    for place in range(out_ref.shape[0]):
        for i, part in enumerate(parts):
            out_ref[place, :, i * lat : (i + 1) * lat] = part


def decode_kernel(slots, q_ref, new_ref, limit_ref, first_ref, second_ref, *rest):
    out_ref = rest[-1]
    requests, _, heads, lat = q_ref.shape
    rows = requests * heads
    q = q_ref[...].reshape(rows, lat)
    row = lax.broadcasted_iota(jnp.int32, (rows, requests), 0)
    start = lax.broadcasted_iota(jnp.int32, (rows, requests), 1) * heads
    pick = jnp.where((row >= start) & (row < start + heads), 1.0, 0.0).astype(bf16)
    own = dot(pick, new_ref[...].reshape(requests, lat))
    pages = [ref[...].astype(f32).reshape(PAGE, lat) for ref in (first_ref, second_ref)]
    keys = jnp.concatenate(pages, axis=0).astype(bf16)
    scores = dot_t(q, keys) * score_scale
    place = lax.broadcasted_iota(jnp.int32, scores.shape, 1)
    scores = jnp.where(place < limit_ref[0], scores, -jnp.inf)
    own_score = jnp.sum(q.astype(f32) * own, axis=1, keepdims=True) * score_scale
    top = jnp.maximum(jnp.max(scores, axis=1, keepdims=True), own_score)
    weights = jnp.exp(scores - top)
    own_weight = jnp.exp(own_score - top)
    total = jnp.sum(weights, axis=1, keepdims=True) + own_weight
    numer = dot(weights.astype(bf16), keys) + own_weight * own
    out_ref[...] = (numer / total).astype(bf16).reshape(out_ref.shape)


def decode_pair(layer, slots, queries, new, limit, pages, carried):
    requests, _, heads, lat = queries.shape

    def page(which):
        if pages.shape[0] * pages.shape[1] == PAGE:
            return pl.BlockSpec(pages.shape[:2] + (lat,), lambda i, s: (0, 0, 2 * i + which))
        return pl.BlockSpec((1, PAGE, lat), lambda i, s: (s[2 * (layer + i) + which], 0, i))

    in_specs = [
        pl.BlockSpec((requests, 1, heads, lat), lambda i, s: (0, layer + i, 0, 0)),
        pl.BlockSpec((1, requests, lat), lambda i, s: (layer + i, 0, 0)),
        pl.BlockSpec((1, requests * heads, 1), lambda i, s: (layer + i, 0, 0)),
        page(0),
        page(1),
    ]
    operands = [slots, queries, new, limit, pages, pages]
    aliases = {}
    if carried is not None:
        in_specs.append(anywhere)
        aliases = {len(operands): 0}
        operands.append(carried)
    return pl.pallas_call(
        decode_kernel,
        grid_spec=pltpu.PrefetchScalarGridSpec(
            num_scalar_prefetch=1,
            grid=(2,),
            in_specs=in_specs,
            out_specs=pl.BlockSpec((requests, 1, heads, lat), lambda i, s: (0, layer + i, 0, 0)),
        ),
        out_shape=jax.ShapeDtypeStruct(queries.shape, bf16),
        input_output_aliases=aliases,
        compiler_params=params,
        cost_estimate=pl.CostEstimate(
            flops=2 * 4 * requests * heads * 2 * PAGE * lat,
            bytes_accessed=2 * 2 * (2 * requests * heads + 2 * PAGE) * lat,
            transcendentals=2 * requests * heads * 2 * PAGE,
        ),
    )(*operands)


def shards(
    prompt_states, norm_gain, w_latent, w_back, page_lists, queries, new_latent, context_lengths
):
    segments = lax.axis_size("segment")
    wide = lax.axis_size("wide")
    position = lax.axis_index("segment")
    core = position & 1
    batches, tok_rows, local_width = prompt_states.shape
    width = local_width * wide
    tokens = batches * tok_rows
    mine = tokens // segments
    share = mine // wide
    layers = segments
    lat = w_latent.shape[2]
    where = jnp.stack([position, core]).astype(jnp.int32)

    def array(*shape):
        return jax.ShapeDtypeStruct(shape, bf16)

    both, lent = call(
        weights_kernel,
        [whole(w_latent.shape), whole(norm_gain.shape), whole(w_back.shape)],
        [whole((2, local_width, lat)), whole((local_width, lat))],
        [array(2, local_width, lat), array(local_width, lat)],
        [w_latent, norm_gain, w_back],
        [where],
        flops=2 * local_width**3,
    )
    every = lax.all_gather(both, "segment", axis=0)
    lent = lax.ppermute(lent, "segment", [(i, i + 1) for i in range(0, segments, 2)])

    states = prompt_states.reshape(segments // 2, 2, mine, local_width)
    high = lat // wide
    columns = 2 * lat + LANES
    (sent,) = call(
        home_kernel,
        [
            pl.BlockSpec((segments // 2, 1, mine, local_width), lambda i, s: (0, s[1], 0, 0)),
            whole(both.shape),
            whole(lent.shape),
        ],
        [whole((wide, high, columns))],
        [array(wide, high, columns)],
        [states, both, lent],
        [where],
        [pltpu.VMEM((local_width, lat), bf16), pltpu.VMEM((lat, lat), f32)],
        flops=2 * 2 * local_width**3,
    )
    got = exchanged(sent, "wide")
    latent, cross = call(
        functools.partial(home_sum_kernel, width),
        [whole(got.shape)],
        [whole((segments // 2, share, lat)), whole((high, lat))],
        [array(segments // 2, share, lat), array(high, lat)],
        [got],
    )
    taken = [
        lax.ppermute(latent[hop], "segment", [(0, 2 * hop), (1, 2 * hop + 1)])
        for hop in range(1, segments // 2)
    ]
    (sent,) = call(
        home_send_kernel,
        [whole((1, share, lat))] + [whole((share, lat))] * 3 + [whole((high, lat))],
        [whole((wide, high + share, lat))],
        [array(wide, high + share, lat)],
        [latent] + taken + [cross],
        [where],
    )
    got = exchanged(sent, "wide")

    def advance(before, following, got, state, extra=None):
        first = before == (0,)
        in_specs, operands = [whole(got.shape)], [got]
        if extra is not None:
            in_specs.append(whole(extra.shape))
            operands.append(extra)
        if first:
            in_specs.append(
                pl.BlockSpec((1, 1, mine, local_width), lambda i, s: (s[0] >> 1, s[1], 0, 0))
            )
        else:
            in_specs.append(whole(state.shape))
        operands += [state, every]
        in_specs.append(anywhere)
        count = len(following) + (len(following) == 2)
        shapes = [array(wide, share, LANES + count * lat), array(mine, local_width)]
        if first:
            shapes.append(array(wide, high, lat))
        elif extra is not None:
            shapes.append(array(mine, 2 * lat))
        needed = len(before) + count
        return call(
            functools.partial(advance_kernel, before, following, first),
            in_specs,
            [whole(s.shape) for s in shapes],
            shapes,
            operands,
            [where],
            [pltpu.VMEM((needed, local_width, lat), bf16), pltpu.SemaphoreType.DMA((needed,))],
            flops=2 * needed * mine * lat * local_width,
        )

    sent, state, cross = advance((0,), (1,), got, states)
    crosses = lax.all_gather(cross.reshape(lat, lat), "segment", axis=0)
    earlier = got
    got = exchanged(sent, "wide")
    (sent,) = call(
        functools.partial(single_kernel, width),
        [whole(got.shape)],
        [whole((wide, share, lat))],
        [array(wide, share, lat)],
        [got],
    )
    got = exchanged(sent, "wide")

    def pair_step(even, got):
        (sent,) = call(
            functools.partial(pair_kernel, width, even),
            [whole(got.shape), anywhere],
            [whole((wide, share, 2 * lat))],
            [array(wide, share, 2 * lat)],
            [got, crosses],
            [],
            [pltpu.VMEM((2, lat, lat), bf16), pltpu.SemaphoreType.DMA((2,))],
            flops=2 * 2 * share * lat * lat,
        )
        return sent

    targets = page_lists[:, :, 0]
    owned = targets == position
    counts = jnp.sum(owned.astype(jnp.int32), axis=1)
    none = targets.shape[1]
    order = jnp.arange(none, dtype=jnp.int32)[None, :]
    slot0 = jnp.min(jnp.where(owned, order, none), axis=1)
    slot1 = jnp.min(jnp.where(owned & (order > slot0[:, None]), order, none), axis=1)
    slots = jnp.minimum(jnp.stack([slot0, slot1], axis=1), none - 1).reshape(-1)
    limit = jnp.minimum(context_lengths, counts[None, :] * PAGE)
    limit = jnp.repeat(limit.T, queries.shape[2], axis=1)[:, :, None]
    new = new_latent.transpose(1, 0, 2)

    def decode(layer, pages, carried):
        return decode_pair(layer, slots, queries, new, limit, pages, carried)

    sent, state, held = advance((1,), (2, 3), got, state, earlier)
    pages01 = lax.all_gather(held, "segment", axis=0)
    got = exchanged(sent, "wide")
    sent = pair_step(2, got)
    got = exchanged(sent, "wide")

    pages23 = lax.all_gather(got.reshape(mine, 2 * lat), "segment", axis=0)
    sent, state = advance((2, 3), (4, 5), got, state)
    got = exchanged(sent, "wide")
    sent = pair_step(4, got)
    got = exchanged(sent, "wide")

    pages45 = lax.all_gather(got.reshape(mine, 2 * lat), "segment", axis=0)
    sent, state = advance((4, 5), (6, 7), got, state)
    got = exchanged(sent, "wide")
    out = decode(0, pages01, None)
    got, out = lax.optimization_barrier((got, out))
    sent = pair_step(6, got)

    got = exchanged(sent[:segments], "segment")
    out = decode(2, pages23, out)
    got, out = lax.optimization_barrier((got, out))
    (sent,) = call(
        functools.partial(choose_kernel, layers - 2),
        [whole(got.shape)],
        [whole((wide, share, 4 * lat))],
        [array(wide, share, 4 * lat)],
        [got],
        [slots],
    )
    got = exchanged(sent, "wide")
    out = decode(4, pages45, out)
    got, out = lax.optimization_barrier((got, out))
    return decode(layers - 2, got, out)


def solution(mesh):
    in_specs = (
        P(None, None, "wide"),
        P("segment", "wide"),
        P("segment", "wide", None),
        P("segment", None, "wide"),
        P(),
        P("segment", None, "wide", None),
        P("segment", None, None),
        P("segment", None),
    )
    out_specs = P("segment", None, "wide", None)
    return jax.shard_map(shards, mesh=mesh, in_specs=in_specs, out_specs=out_specs, check_vma=False)
```

```python
import functools

import jax
import jax.numpy as jnp
from jax import lax
from jax.experimental import pallas as pl
from jax.experimental.pallas import tpu as pltpu
from jax.sharding import PartitionSpec as P

PAGE = 128
LANES = 128

eps_norm = 1e-06
score_scale = 192.0 ** (-0.5)

params = pltpu.CompilerParams(vmem_limit_bytes=24 * 1024 * 1024)
in_hbm = pl.BlockSpec(memory_space=pltpu.HBM)
bf16 = jnp.bfloat16
f32 = jnp.float32


def dot(a, b):
    return jnp.dot(a, b, preferred_element_type=jnp.float32)


def dot_t(a, b):
    return lax.dot_general(a, b, (((1,), (1,)), ((), ())), preferred_element_type=jnp.float32)


def square_columns(values):
    squares = jnp.sum(values * values, axis=1, keepdims=True)
    high = squares.astype(bf16).astype(f32)
    column = lax.broadcasted_iota(jnp.int32, (values.shape[0], LANES), 1)
    return jnp.where(column == 0, high, jnp.where(column == 1, squares - high, 0.0))


def silu(latent):
    values = latent.astype(f32)
    return (values / (1.0 + jnp.exp(-values))).astype(bf16)


def exchanged(sent, axis):
    return lax.all_to_all(sent, axis, 0, 0, tiled=True)


def core_swap(x):
    length = lax.axis_size("segment")
    return lax.ppermute(x, "segment", [(i, i ^ 1) for i in range(length)])


def whole(shape):
    return pl.BlockSpec(shape, lambda i, *s: (0,) * len(shape))


def call(body, in_specs, out_specs, out_shape, operands, scalars=(), scratch=(), flops=0):
    moved = sum(o.size * 2 for o in out_shape)
    return pl.pallas_call(
        body,
        grid_spec=pltpu.PrefetchScalarGridSpec(
            num_scalar_prefetch=len(scalars),
            grid=(1,),
            in_specs=in_specs,
            out_specs=out_specs,
            scratch_shapes=scratch,
        ),
        out_shape=out_shape,
        compiler_params=params,
        cost_estimate=pl.CostEstimate(flops=flops, bytes_accessed=2 * moved, transcendentals=0),
    )(*scalars, *operands)


def weights_kernel(latent_ref, gain_ref, back_ref, both_ref, latent, sems):
    copies = [
        pltpu.make_async_copy(latent_ref.at[0], latent, sems.at[0]),
        pltpu.make_async_copy(back_ref.at[0], both_ref.at[1], sems.at[1]),
    ]
    for copy in copies:
        copy.start()
    size = latent.shape[0]
    row = lax.broadcasted_iota(jnp.int32, (size, size), 0)
    column = lax.broadcasted_iota(jnp.int32, (size, size), 1)
    gains = jnp.where(row == column, gain_ref[...].astype(f32), 0.0).astype(bf16)
    copies[0].wait()
    both_ref[0] = dot(gains, latent[...]).astype(bf16)
    copies[1].wait()


def home_kernel(where, states_ref, both_ref, other_ref, out_ref):
    groups, _, rows, width = states_ref.shape
    lat = both_ref.shape[2]
    wide = out_ref.shape[0]
    share = rows // wide
    tokens = states_ref[...].reshape(groups * rows, width)

    def put(product, at):
        for group in range(groups):
            part = product[group * rows : (group + 1) * rows]
            part = part.reshape(wide, share, part.shape[1]).astype(bf16)
            out_ref[:, group * share : (group + 1) * share, at : at + part.shape[2]] = part

    def partials(even_ref, odd_ref):
        put(dot(tokens, even_ref[0]), LANES)
        put(dot(tokens, odd_ref[0]), LANES + lat)
        put(dot_t(tokens, even_ref[1]), LANES + 2 * lat)

    def put_cross(cross):
        cross = cross.reshape(wide, lat // wide, lat).astype(bf16)
        out_ref[:, :, LANES + 3 * lat :] = cross

    put(square_columns(tokens.astype(f32)), 0)

    @pl.when(where[1] == 0)
    def _():
        put_cross(dot_t(both_ref[1], both_ref[1]))
        partials(both_ref, other_ref)

    @pl.when(where[1] != 0)
    def _():
        put_cross(dot(other_ref[1], both_ref[0]))
        partials(other_ref, both_ref)


def home_sum_kernel(got_ref, sums_ref, cross_ref):
    summed = jnp.sum(got_ref[...].astype(f32), axis=0)
    sums_ref[...] = summed[:, : sums_ref.shape[1]]
    cross = summed[:, sums_ref.shape[1] :].astype(bf16)
    for place in range(cross_ref.shape[0]):
        cross_ref[place] = cross


def chain(width, summed, gram, mixing):
    lat = gram().shape[1]
    squares = summed[:, 0:1] + summed[:, 1:2]
    at = [LANES + i * lat for i in range(4)]
    first = (summed[:, at[0] : at[1]] * lax.rsqrt(squares / width + eps_norm)).astype(bf16)
    activated = silu(first)
    towards = 2.0 * summed[:, at[2] : at[3]] + dot(activated, gram())
    squares = squares + jnp.sum(activated.astype(f32) * towards, axis=1, keepdims=True)
    second = summed[:, at[1] : at[2]] + dot(activated, mixing())
    second = (second * lax.rsqrt(squares / width + eps_norm)).astype(bf16)
    return first, second


def home_pair_kernel(width, where, sums_ref, mine_ref, other_ref, out_ref):
    def run(gram_ref, mixing_ref):
        parts = chain(width, sums_ref[...], lambda: gram_ref[...], lambda: mixing_ref[...])
        lat = parts[0].shape[1]
        for i, part in enumerate(parts):
            part = part.astype(f32).reshape(out_ref.shape[:2] + (lat,)).astype(bf16)
            out_ref[:, :, i * lat : (i + 1) * lat] = part

    @pl.when(where[1] == 0)
    def _():
        run(mine_ref, other_ref)

    @pl.when(where[1] != 0)
    def _():
        run(other_ref, mine_ref)


def home_send_kernel(where, mine_ref, a_ref, b_ref, c_ref, out_ref):
    taken = a_ref[...].astype(f32) + b_ref[...].astype(f32) + c_ref[...].astype(f32)
    latent = jnp.where(where[0] < 2, mine_ref[0].astype(f32), taken).astype(bf16)
    for place in range(out_ref.shape[0]):
        out_ref[place] = latent


def advance_kernel(before, layers, where, got_ref, states_ref, both_ref, out_ref, state_ref, *rest):
    got, weights, sems = rest
    needed = [(layer, 1) for layer in before] + [(layer, 0) for layer in layers] + [(layers[0], 1)]
    taking = pltpu.make_async_copy(got_ref, got, sems.at[len(needed)])
    taking.start()
    copies = [
        pltpu.make_async_copy(both_ref.at[layer, kind], weights.at[i], sems.at[i])
        for i, (layer, kind) in enumerate(needed)
    ]
    for copy in copies:
        copy.start()
    wide, share, _ = out_ref.shape
    rows = wide * share
    lat = weights.shape[2]
    state = states_ref[...].reshape(rows, weights.shape[1]).astype(f32)
    taking.wait()
    activated = silu(got[...].astype(f32).reshape(rows, got.shape[2]))
    for i in range(len(before)):
        copies[i].wait()
        state = state + dot(activated[:, i * lat : (i + 1) * lat], weights[i])
    state = state.astype(bf16)
    state_ref[...] = state
    squares = square_columns(state.astype(f32))
    out_ref[:, :, :LANES] = squares.reshape(wide, share, LANES).astype(bf16)
    for i in range(len(before), len(needed)):
        copies[i].wait()
        product = (dot_t if needed[i][1] else dot)(state, weights[i])
        at = LANES + (i - len(before)) * lat
        out_ref[:, :, at : at + lat] = product.reshape(wide, share, lat).astype(bf16)


def pair_kernel(width, even, got_ref, cross_ref, out_ref, crosses, sems):
    copies = [
        pltpu.make_async_copy(cross_ref.at[even + i], crosses.at[i], sems.at[i]) for i in range(2)
    ]
    for copy in copies:
        copy.start()

    def fetched(i):
        def read():
            return crosses[i]

        return read

    summed = jnp.sum(got_ref[...].astype(f32), axis=0)
    for copy in copies:
        copy.wait()
    first, second = chain(width, summed, fetched(0), fetched(1))
    lat = first.shape[1]
    for place in range(out_ref.shape[0]):
        out_ref[place, :, :lat] = first
        out_ref[place, :, lat:] = second


def choose_kernel(layer, slots, got_ref, out_ref):
    lat = got_ref.shape[2] // 2
    parts = []
    for i in range(2):
        for which in range(2):
            shard = got_ref[slots[2 * (layer + i) + which]]
            parts.append(shard[:, i * lat : (i + 1) * lat])
    for place in range(out_ref.shape[0]):
        for i, part in enumerate(parts):
            out_ref[place, :, i * lat : (i + 1) * lat] = part


def attend(q, new, keys, limit, heads):
    rows = q.shape[0]
    requests = new.shape[0]
    row = lax.broadcasted_iota(jnp.int32, (rows, requests), 0)
    start = lax.broadcasted_iota(jnp.int32, (rows, requests), 1) * heads
    pick = jnp.where((row >= start) & (row < start + heads), 1.0, 0.0).astype(bf16)
    own = dot(pick, new)
    scores = dot_t(q, keys) * score_scale
    place = lax.broadcasted_iota(jnp.int32, scores.shape, 1)
    scores = jnp.where(place < limit, scores, -jnp.inf)
    own_score = jnp.sum(q.astype(f32) * own, axis=1, keepdims=True) * score_scale
    top = jnp.maximum(jnp.max(scores, axis=1, keepdims=True), own_score)
    weights = jnp.exp(scores - top)
    own_weight = jnp.exp(own_score - top)
    total = jnp.sum(weights, axis=1, keepdims=True) + own_weight
    numer = dot(weights.astype(bf16), keys) + own_weight * own
    return (numer / total).astype(bf16)


def decode_kernel(layer, slots, q_ref, new_ref, limit_ref, pages_ref, *rest):
    out_ref, keys, sems = rest[-3:]
    requests, count, heads, lat = q_ref.shape
    copies = []
    for i in range(count):
        for which in range(2):
            page = pages_ref.at[slots[2 * (layer + i) + which], :, pl.ds(i * lat, lat)]
            at = keys.at[i, pl.ds(which * PAGE, PAGE)]
            copies.append(pltpu.make_async_copy(page, at, sems.at[2 * i + which]))
    for copy in copies:
        copy.start()
    for i in range(count):
        q = q_ref[:, i].reshape(requests * heads, lat)
        copies[2 * i].wait()
        copies[2 * i + 1].wait()
        result = attend(q, new_ref[i], keys[i], limit_ref[i], heads)
        out_ref[:, i] = result.reshape(requests, heads, lat)


def last_decode_kernel(q_ref, new_ref, limit_ref, pages_ref, carried_ref, out_ref):
    requests, count, heads, lat = q_ref.shape
    for i in range(count):
        q = q_ref[:, i].reshape(requests * heads, lat)
        at = 2 * i * lat
        pages = pages_ref[:, :, at : at + 2 * lat].astype(f32).reshape(PAGE, 2 * lat)
        keys = jnp.concatenate([pages[:, :lat], pages[:, lat:]], axis=0).astype(bf16)
        result = attend(q, new_ref[i], keys, limit_ref[i], heads)
        out_ref[:, i] = result.reshape(requests, heads, lat)


def decode_pair(layer, slots, queries, new, limit, pages, carried, last=False):
    requests, _, heads, lat = queries.shape
    half = layer // 2
    in_specs = [
        pl.BlockSpec((requests, 2, heads, lat), lambda i, *s: (0, half, 0, 0)),
        pl.BlockSpec((2, requests, lat), lambda i, *s: (half, 0, 0)),
        pl.BlockSpec((2, requests * heads, 1), lambda i, *s: (half, 0, 0)),
        whole(pages.shape) if last else in_hbm,
    ]
    scalars = [] if last else [slots]
    operands = scalars + [queries, new, limit, pages]
    aliases = {}
    if carried is not None:
        in_specs.append(in_hbm)
        aliases = {len(operands): 0}
        operands.append(carried)
    scratch = [pltpu.VMEM((2, 2 * PAGE, lat), bf16), pltpu.SemaphoreType.DMA((4,))]
    return pl.pallas_call(
        last_decode_kernel if last else functools.partial(decode_kernel, layer),
        grid_spec=pltpu.PrefetchScalarGridSpec(
            num_scalar_prefetch=len(scalars),
            grid=(1,),
            in_specs=in_specs,
            out_specs=pl.BlockSpec((requests, 2, heads, lat), lambda i, *s: (0, half, 0, 0)),
            scratch_shapes=[] if last else scratch,
        ),
        out_shape=jax.ShapeDtypeStruct(queries.shape, bf16),
        input_output_aliases=aliases,
        compiler_params=params,
        cost_estimate=pl.CostEstimate(
            flops=2 * 4 * requests * heads * 2 * PAGE * lat,
            bytes_accessed=2 * 2 * (2 * requests * heads + 2 * PAGE) * lat,
            transcendentals=2 * requests * heads * 2 * PAGE,
        ),
    )(*operands)


def shards(
    prompt_states, norm_gain, w_latent, w_back, page_lists, queries, new_latent, context_lengths
):
    segments = lax.axis_size("segment")
    wide = lax.axis_size("wide")
    position = lax.axis_index("segment")
    core = position & 1
    batches, tok_rows, local_width = prompt_states.shape
    width = local_width * wide
    tokens = batches * tok_rows
    mine = tokens // segments
    share = mine // wide
    layers = segments
    lat = w_latent.shape[2]
    where = jnp.stack([position, core]).astype(jnp.int32)

    def array(*shape):
        return jax.ShapeDtypeStruct(shape, bf16)

    size = (2, local_width, lat)
    (both,) = call(
        weights_kernel,
        [in_hbm, whole(norm_gain.shape), in_hbm],
        [whole(size)],
        [array(*size)],
        [w_latent, norm_gain, w_back],
        scratch=[pltpu.VMEM(size[1:], bf16), pltpu.SemaphoreType.DMA((2,))],
        flops=2 * local_width**3,
    )
    every = lax.all_gather(both, "segment", axis=0)
    other = core_swap(both)

    states = prompt_states.reshape(segments // 2, 2, mine, local_width)
    high = lat // wide
    partial_columns = LANES + 3 * lat
    columns = partial_columns + lat
    (sent,) = call(
        home_kernel,
        [
            pl.BlockSpec((segments // 2, 1, mine, local_width), lambda i, s: (0, s[1], 0, 0)),
            whole(size),
            whole(size),
        ],
        [whole((wide, high, columns))],
        [array(wide, high, columns)],
        [states, both, other],
        [where],
        flops=4 * 2 * local_width**3,
    )
    got = exchanged(sent, "wide")
    sums, sent = call(
        home_sum_kernel,
        [whole(got.shape)],
        [whole((high, partial_columns)), whole((wide, high, lat))],
        [jax.ShapeDtypeStruct((high, partial_columns), f32), array(wide, high, lat)],
        [got],
    )
    cross = exchanged(sent, "wide").reshape(lat, lat)
    crosses = lax.all_gather(cross, "segment", axis=0)
    (latent,) = call(
        functools.partial(home_pair_kernel, width),
        [whole(sums.shape), whole(cross.shape), whole(cross.shape)],
        [whole((segments // 2, share, 2 * lat))],
        [array(segments // 2, share, 2 * lat)],
        [sums, cross, core_swap(cross)],
        [where],
        flops=2 * 2 * high * lat * lat,
    )
    taken = [
        lax.ppermute(latent[hop], "segment", [(0, 2 * hop), (1, 2 * hop + 1)])
        for hop in range(1, segments // 2)
    ]
    (sent,) = call(
        home_send_kernel,
        [whole((1, share, 2 * lat))] + [whole((share, 2 * lat))] * 3,
        [whole((wide, share, 2 * lat))],
        [array(wide, share, 2 * lat)],
        [latent] + taken,
        [where],
    )
    got = exchanged(sent, "wide")

    def advance(before, following, got, state):
        if state.ndim == 4:
            spec = pl.BlockSpec((1, 1, mine, local_width), lambda i, s: (s[0] >> 1, s[1], 0, 0))
        else:
            spec = whole(state.shape)
        shapes = [array(wide, share, partial_columns), array(mine, local_width)]
        return call(
            functools.partial(advance_kernel, before, following),
            [in_hbm, spec, in_hbm],
            [whole(s.shape) for s in shapes],
            shapes,
            [got, state, every],
            [where],
            [
                pltpu.VMEM(got.shape, bf16),
                pltpu.VMEM((5, local_width, lat), bf16),
                pltpu.SemaphoreType.DMA((6,)),
            ],
            flops=2 * 5 * mine * lat * local_width,
        )

    def pair_step(even, got, copies):
        (sent,) = call(
            functools.partial(pair_kernel, width, even),
            [whole(got.shape), in_hbm],
            [whole((copies, share, 2 * lat))],
            [array(copies, share, 2 * lat)],
            [got, crosses],
            [],
            [pltpu.VMEM((2, lat, lat), bf16), pltpu.SemaphoreType.DMA((2,))],
            flops=2 * 2 * share * lat * lat,
        )
        return sent

    targets = page_lists[:, :, 0]
    owned = targets == position
    counts = jnp.sum(owned.astype(jnp.int32), axis=1)
    none = targets.shape[1]
    order = jnp.arange(none, dtype=jnp.int32)[None, :]
    slot0 = jnp.min(jnp.where(owned, order, none), axis=1)
    slot1 = jnp.min(jnp.where(owned & (order > slot0[:, None]), order, none), axis=1)
    slots = jnp.minimum(jnp.stack([slot0, slot1], axis=1), none - 1).reshape(-1)
    limit = jnp.minimum(context_lengths, counts[None, :] * PAGE)
    limit = jnp.repeat(limit.T, queries.shape[2], axis=1)[:, :, None]
    new = new_latent.transpose(1, 0, 2)

    def decode(layer, pages, carried, last=False):
        return decode_pair(layer, slots, queries, new, limit, pages, carried, last)

    pages = []
    state = states
    for even in range(2, layers, 2):
        pages.append(lax.all_gather(got.reshape(mine, 2 * lat), "segment", axis=0))
        sent, state = advance((even - 2, even - 1), (even, even + 1), got, state)
        got = exchanged(sent, "wide")
        if even < layers - 2:
            got = exchanged(pair_step(even, got, wide), "wide")
    out = decode(0, pages[0], None)
    got, out = lax.optimization_barrier((got, out))

    got = exchanged(pair_step(layers - 2, got, segments), "segment")
    out = decode(2, pages[1], out)
    got, out = lax.optimization_barrier((got, out))
    (sent,) = call(
        functools.partial(choose_kernel, layers - 2),
        [whole(got.shape)],
        [whole((wide, share, 4 * lat))],
        [array(wide, share, 4 * lat)],
        [got],
        [slots],
    )
    got = exchanged(sent, "wide")
    out = decode(4, pages[2], out)
    got, out = lax.optimization_barrier((got, out))
    return decode(layers - 2, got, out, True)


def solution(mesh):
    in_specs = (
        P(None, None, "wide"),
        P("segment", "wide"),
        P("segment", "wide", None),
        P("segment", None, "wide"),
        P(),
        P("segment", None, "wide", None),
        P("segment", None, None),
        P("segment", None),
    )
    out_specs = P("segment", None, "wide", None)
    return jax.shard_map(shards, mesh=mesh, in_specs=in_specs, out_specs=out_specs, check_vma=False)
```

```python
import functools

import jax
import jax.numpy as jnp
from jax import lax
from jax.experimental import pallas as pl
from jax.experimental.pallas import tpu as pltpu
from jax.sharding import PartitionSpec as P

PAGE = 128
LANES = 128

eps_norm = 1e-06
score_scale = 192.0 ** (-0.5)

params = pltpu.CompilerParams(vmem_limit_bytes=24 * 1024 * 1024)
in_hbm = pl.BlockSpec(memory_space=pltpu.HBM)
bf16 = jnp.bfloat16
f32 = jnp.float32


def dot(a, b):
    return jnp.dot(a, b, preferred_element_type=jnp.float32)


def dot_t(a, b):
    return lax.dot_general(a, b, (((1,), (1,)), ((), ())), preferred_element_type=jnp.float32)


def square_columns(values):
    squares = jnp.sum(values * values, axis=1, keepdims=True)
    high = squares.astype(bf16).astype(f32)
    column = lax.broadcasted_iota(jnp.int32, (values.shape[0], LANES), 1)
    return jnp.where(column == 0, high, jnp.where(column == 1, squares - high, 0.0))


def silu(latent):
    values = latent.astype(f32)
    return (values / (1.0 + jnp.exp(-values))).astype(bf16)


def exchanged(sent, axis):
    return lax.all_to_all(sent, axis, 0, 0, tiled=True)


def core_swap(x):
    length = lax.axis_size("segment")
    return lax.ppermute(x, "segment", [(i, i ^ 1) for i in range(length)])


def held_in_hbm(x):
    return pltpu.with_memory_space_constraint(x, pltpu.HBM)


def whole(shape):
    return pl.BlockSpec(shape, lambda i, *s: (0,) * len(shape))


def call(body, in_specs, out_specs, out_shape, operands, scalars=(), scratch=(), flops=0):
    moved = sum(o.size * 2 for o in out_shape)
    return pl.pallas_call(
        body,
        grid_spec=pltpu.PrefetchScalarGridSpec(
            num_scalar_prefetch=len(scalars),
            grid=(1,),
            in_specs=in_specs,
            out_specs=out_specs,
            scratch_shapes=scratch,
        ),
        out_shape=out_shape,
        compiler_params=params,
        cost_estimate=pl.CostEstimate(flops=flops, bytes_accessed=2 * moved, transcendentals=0),
    )(*scalars, *operands)


def weights_kernel(where, latent_ref, gain_ref, back_ref, both_ref, lent_ref, latent, sems):
    copies = [
        pltpu.make_async_copy(latent_ref.at[0], latent, sems.at[0]),
        pltpu.make_async_copy(back_ref.at[0], both_ref.at[1], sems.at[1]),
    ]
    for copy in copies:
        copy.start()
    size = latent.shape[0]
    row = lax.broadcasted_iota(jnp.int32, (size, size), 0)
    column = lax.broadcasted_iota(jnp.int32, (size, size), 1)
    gains = jnp.where(row == column, gain_ref[...].astype(f32), 0.0).astype(bf16)
    copies[0].wait()
    both_ref[0] = dot(gains, latent[...]).astype(bf16)
    copies[1].wait()

    @pl.when(where[0] == 0)
    def _():
        lent_ref[...] = both_ref[0]

    @pl.when(where[0] != 0)
    def _():
        lent_ref[...] = both_ref[1]


def home_kernel(where, states_ref, both_ref, lent_ref, *out_refs):
    groups, _, rows, width = states_ref.shape
    tokens = states_ref[...].reshape(groups * rows, width)

    def products(weight):
        product = dot(tokens, weight).astype(bf16)
        for group in range(groups):
            out_refs[group][...] = product[group * rows : (group + 1) * rows]

    @pl.when(where[0] == 0)
    def _():
        products(both_ref[0])

    @pl.when(where[0] != 0)
    def _():
        products(lent_ref[...])

    @pl.when(where[1] == 0)
    def _():
        out_refs[groups][...] = dot_t(both_ref[1], both_ref[1]).astype(bf16)

    @pl.when(where[1] != 0)
    def _():
        out_refs[groups][...] = dot(lent_ref[...], both_ref[0]).astype(bf16)


def home_send_kernel(where, home_ref, a_ref, b_ref, c_ref, cross_ref, states_ref, out_ref):
    wide, share, _ = out_ref.shape
    rows, lat = home_ref.shape
    taken = a_ref[...].astype(f32) + b_ref[...].astype(f32) + c_ref[...].astype(f32)
    product = jnp.where(where[0] < 2, home_ref[...].astype(f32), taken)
    squares = square_columns(states_ref[...].reshape(rows, states_ref.shape[3]).astype(f32))
    out_ref[:, :, :LANES] = squares.reshape(wide, share, LANES).astype(bf16)
    out_ref[:, :, LANES : LANES + lat] = product.reshape(wide, share, lat).astype(bf16)
    parts = cross_ref.shape[0] // rows
    cross = cross_ref[...].astype(f32).reshape(wide, parts, share, lat)
    for part in range(parts):
        at = LANES + (1 + part) * lat
        out_ref[:, :, at : at + lat] = cross[:, part].astype(bf16)


def home_sum_kernel(width, got_ref, out_ref):
    wide, high, lat = out_ref.shape
    summed = jnp.sum(got_ref[...].astype(f32), axis=0)
    squares = summed[:, 0:1] + summed[:, 1:2]
    latent = summed[:, LANES : LANES + lat] * lax.rsqrt(squares / width + eps_norm)
    parts = [summed[:, at : at + lat] for at in range(LANES + lat, summed.shape[1], lat)]
    block = jnp.concatenate(parts + [latent], axis=0).astype(bf16)
    for place in range(wide):
        out_ref[place] = block


def single_kernel(width, got_ref, out_ref):
    summed = jnp.sum(got_ref[...].astype(f32), axis=0)
    squares = summed[:, 0:1] + summed[:, 1:2]
    latent = (summed[:, LANES:] * lax.rsqrt(squares / width + eps_norm)).astype(bf16)
    for place in range(out_ref.shape[0]):
        out_ref[place] = latent


def chain(width, summed, gram, mixing):
    lat = gram().shape[1]
    squares = summed[:, 0:1] + summed[:, 1:2]
    at = [LANES + i * lat for i in range(4)]
    first = (summed[:, at[0] : at[1]] * lax.rsqrt(squares / width + eps_norm)).astype(bf16)
    activated = silu(first)
    towards = 2.0 * summed[:, at[2] : at[3]] + dot(activated, gram())
    squares = squares + jnp.sum(activated.astype(f32) * towards, axis=1, keepdims=True)
    second = summed[:, at[1] : at[2]] + dot(activated, mixing())
    second = (second * lax.rsqrt(squares / width + eps_norm)).astype(bf16)
    return first, second


def advance_kernel(before, layers, held, where, got_ref, states_ref, both_ref, *rest):
    got, weights, sems = rest[-3:]
    out_ref, state_ref = rest[held : held + 2]
    needed = [(layer, 1) for layer in before] + [(layer, 0) for layer in layers]
    if len(layers) == 2:
        needed.append((layers[0], 1))
    taking = pltpu.make_async_copy(got_ref, got, sems.at[len(needed)])
    taking.start()
    copies = [
        pltpu.make_async_copy(both_ref.at[layer, kind], weights.at[i], sems.at[i])
        for i, (layer, kind) in enumerate(needed)
    ]
    for copy in copies:
        copy.start()
    wide, share, _ = out_ref.shape
    rows = wide * share
    lat = weights.shape[2]
    state = states_ref[...].reshape(rows, weights.shape[1]).astype(f32)
    taking.wait()
    latents = got[...].astype(f32).reshape(rows, got.shape[2])
    if held:
        earlier_ref, held_ref = rest[0], rest[3]
        held_ref[:, :lat] = earlier_ref[...].astype(f32).reshape(rows, lat).astype(bf16)
        held_ref[:, lat:] = latents.astype(bf16)
    activated = silu(latents)
    for i in range(len(before)):
        copies[i].wait()
        state = state + dot(activated[:, i * lat : (i + 1) * lat], weights[i])
    state = state.astype(bf16)
    state_ref[...] = state
    squares = square_columns(state.astype(f32))
    out_ref[:, :, :LANES] = squares.reshape(wide, share, LANES).astype(bf16)
    for i in range(len(before), len(needed)):
        copies[i].wait()
        product = (dot_t if needed[i][1] else dot)(state, weights[i])
        at = LANES + (i - len(before)) * lat
        out_ref[:, :, at : at + lat] = product.reshape(wide, share, lat).astype(bf16)


def pair_kernel(width, even, got_ref, cross_ref, out_ref, crosses, sems):
    copies = [
        pltpu.make_async_copy(cross_ref.at[even + i], crosses.at[i], sems.at[i]) for i in range(2)
    ]
    for copy in copies:
        copy.start()

    def fetched(i):
        def read():
            return crosses[i]

        return read

    summed = jnp.sum(got_ref[...].astype(f32), axis=0)
    for copy in copies:
        copy.wait()
    first, second = chain(width, summed, fetched(0), fetched(1))
    lat = first.shape[1]
    for place in range(out_ref.shape[0]):
        out_ref[place, :, :lat] = first
        out_ref[place, :, lat:] = second


def choose_kernel(layer, slots, got_ref, out_ref):
    lat = got_ref.shape[2] // 2
    parts = []
    for i in range(2):
        for which in range(2):
            shard = got_ref[slots[2 * (layer + i) + which]]
            parts.append(shard[:, i * lat : (i + 1) * lat])
    for place in range(out_ref.shape[0]):
        for i, part in enumerate(parts):
            out_ref[place, :, i * lat : (i + 1) * lat] = part


def attend(q, new, keys, limit, heads):
    rows = q.shape[0]
    requests = new.shape[0]
    row = lax.broadcasted_iota(jnp.int32, (rows, requests), 0)
    start = lax.broadcasted_iota(jnp.int32, (rows, requests), 1) * heads
    pick = jnp.where((row >= start) & (row < start + heads), 1.0, 0.0).astype(bf16)
    own = dot(pick, new)
    scores = dot_t(q, keys) * score_scale
    place = lax.broadcasted_iota(jnp.int32, scores.shape, 1)
    scores = jnp.where(place < limit, scores, -jnp.inf)
    own_score = jnp.sum(q.astype(f32) * own, axis=1, keepdims=True) * score_scale
    top = jnp.maximum(jnp.max(scores, axis=1, keepdims=True), own_score)
    weights = jnp.exp(scores - top)
    own_weight = jnp.exp(own_score - top)
    total = jnp.sum(weights, axis=1, keepdims=True) + own_weight
    numer = dot(weights.astype(bf16), keys) + own_weight * own
    return (numer / total).astype(bf16)


def decode_kernel(layer, slots, q_ref, new_ref, limit_ref, pages_ref, *rest):
    out_ref, keys, sems = rest[-3:]
    requests, count, heads, lat = q_ref.shape
    copies = []
    for i in range(count):
        for which in range(2):
            page = pages_ref.at[slots[2 * (layer + i) + which], :, pl.ds(i * lat, lat)]
            at = keys.at[i, pl.ds(which * PAGE, PAGE)]
            copies.append(pltpu.make_async_copy(page, at, sems.at[2 * i + which]))
    for copy in copies:
        copy.start()
    for i in range(count):
        q = q_ref[:, i].reshape(requests * heads, lat)
        copies[2 * i].wait()
        copies[2 * i + 1].wait()
        result = attend(q, new_ref[i], keys[i], limit_ref[i], heads)
        out_ref[:, i] = result.reshape(requests, heads, lat)


def last_decode_kernel(q_ref, new_ref, limit_ref, pages_ref, carried_ref, out_ref):
    requests, count, heads, lat = q_ref.shape
    for i in range(count):
        q = q_ref[:, i].reshape(requests * heads, lat)
        at = 2 * i * lat
        pages = pages_ref[:, :, at : at + 2 * lat].astype(f32).reshape(PAGE, 2 * lat)
        keys = jnp.concatenate([pages[:, :lat], pages[:, lat:]], axis=0).astype(bf16)
        result = attend(q, new_ref[i], keys, limit_ref[i], heads)
        out_ref[:, i] = result.reshape(requests, heads, lat)


def decode_pair(layer, slots, queries, new, limit, pages, carried, last=False):
    requests, _, heads, lat = queries.shape
    half = layer // 2
    in_specs = [
        pl.BlockSpec((requests, 2, heads, lat), lambda i, *s: (0, half, 0, 0)),
        pl.BlockSpec((2, requests, lat), lambda i, *s: (half, 0, 0)),
        pl.BlockSpec((2, requests * heads, 1), lambda i, *s: (half, 0, 0)),
        whole(pages.shape) if last else in_hbm,
    ]
    scalars = [] if last else [slots]
    operands = scalars + [queries, new, limit, pages if last else held_in_hbm(pages)]
    aliases = {}
    if carried is not None:
        in_specs.append(in_hbm)
        aliases = {len(operands): 0}
        operands.append(carried)
    scratch = [pltpu.VMEM((2, 2 * PAGE, lat), bf16), pltpu.SemaphoreType.DMA((4,))]
    return pl.pallas_call(
        last_decode_kernel if last else functools.partial(decode_kernel, layer),
        grid_spec=pltpu.PrefetchScalarGridSpec(
            num_scalar_prefetch=len(scalars),
            grid=(1,),
            in_specs=in_specs,
            out_specs=pl.BlockSpec((requests, 2, heads, lat), lambda i, *s: (0, half, 0, 0)),
            scratch_shapes=[] if last else scratch,
        ),
        out_shape=jax.ShapeDtypeStruct(queries.shape, bf16),
        input_output_aliases=aliases,
        compiler_params=params,
        cost_estimate=pl.CostEstimate(
            flops=2 * 4 * requests * heads * 2 * PAGE * lat,
            bytes_accessed=2 * 2 * (2 * requests * heads + 2 * PAGE) * lat,
            transcendentals=2 * requests * heads * 2 * PAGE,
        ),
    )(*operands)


def shards(
    prompt_states, norm_gain, w_latent, w_back, page_lists, queries, new_latent, context_lengths
):
    segments = lax.axis_size("segment")
    wide = lax.axis_size("wide")
    position = lax.axis_index("segment")
    core = position & 1
    batches, tok_rows, local_width = prompt_states.shape
    width = local_width * wide
    tokens = batches * tok_rows
    mine = tokens // segments
    share = mine // wide
    layers = segments
    lat = w_latent.shape[2]
    where = jnp.stack([position, core]).astype(jnp.int32)

    def array(*shape):
        return jax.ShapeDtypeStruct(shape, bf16)

    size = (2, local_width, lat)
    both, lent = call(
        weights_kernel,
        [in_hbm, whole(norm_gain.shape), in_hbm],
        [whole(size), whole(size[1:])],
        [array(*size), array(*size[1:])],
        [held_in_hbm(w_latent), norm_gain, held_in_hbm(w_back)],
        [where],
        [pltpu.VMEM(size[1:], bf16), pltpu.SemaphoreType.DMA((2,))],
        flops=2 * local_width**3,
    )
    every = held_in_hbm(lax.all_gather(both, "segment", axis=0))
    lent = lax.ppermute(lent, "segment", [(i, i + 1) for i in range(0, segments, 2)])

    states = prompt_states.reshape(segments // 2, 2, mine, local_width)
    groups = segments // 2
    own_states = pl.BlockSpec((1, 1, mine, local_width), lambda i, s: (s[0] >> 1, s[1], 0, 0))
    *home, cross = call(
        home_kernel,
        [
            pl.BlockSpec((groups, 1, mine, local_width), lambda i, s: (0, s[1], 0, 0)),
            whole(size),
            whole(size[1:]),
        ],
        [whole((mine, lat))] * groups + [whole((lat, lat))],
        [array(mine, lat)] * groups + [array(lat, lat)],
        [states, both, lent],
        [where],
        flops=2 * 2 * local_width**3,
    )
    taken = [
        lax.ppermute(home[hop], "segment", [(0, 2 * hop), (1, 2 * hop + 1)])
        for hop in range(1, groups)
    ]
    high = lat // wide
    columns = LANES + lat + high // share * lat
    (sent,) = call(
        home_send_kernel,
        [whole((mine, lat))] * groups + [whole((lat, lat)), own_states],
        [whole((wide, share, columns))],
        [array(wide, share, columns)],
        [home[0]] + taken + [cross, states],
        [where],
    )
    got = exchanged(sent, "wide")
    (sent,) = call(
        functools.partial(home_sum_kernel, width),
        [whole(got.shape)],
        [whole((wide, high + share, lat))],
        [array(wide, high + share, lat)],
        [got],
    )
    got = exchanged(sent, "wide")
    crosses = lax.all_gather(got[:, :high].reshape(lat, lat), "segment", axis=0)
    crosses = held_in_hbm(crosses)
    got = got[:, high:]

    def advance(before, following, got, state, earlier=None):
        held = earlier is not None
        count = len(following) + (len(following) == 2)
        shapes = [array(wide, share, LANES + count * lat), array(mine, local_width)]
        in_specs = [in_hbm, own_states if state.ndim == 4 else whole(state.shape), in_hbm]
        operands = [held_in_hbm(got), state, every]
        if held:
            shapes.append(array(mine, 2 * lat))
            in_specs.append(whole(earlier.shape))
            operands.append(earlier)
        needed = len(before) + count
        return call(
            functools.partial(advance_kernel, before, following, held),
            in_specs,
            [whole(s.shape) for s in shapes],
            shapes,
            operands,
            [where],
            [
                pltpu.VMEM(got.shape, bf16),
                pltpu.VMEM((needed, local_width, lat), bf16),
                pltpu.SemaphoreType.DMA((needed + 1,)),
            ],
            flops=2 * needed * mine * lat * local_width,
        )

    earlier = got
    sent, state = advance((0,), (1,), got, states)
    got = exchanged(sent, "wide")
    (sent,) = call(
        functools.partial(single_kernel, width),
        [whole(got.shape)],
        [whole((wide, share, lat))],
        [array(wide, share, lat)],
        [got],
    )
    got = exchanged(sent, "wide")

    def pair_step(even, got, copies):
        (sent,) = call(
            functools.partial(pair_kernel, width, even),
            [whole(got.shape), in_hbm],
            [whole((copies, share, 2 * lat))],
            [array(copies, share, 2 * lat)],
            [got, crosses],
            [],
            [pltpu.VMEM((2, lat, lat), bf16), pltpu.SemaphoreType.DMA((2,))],
            flops=2 * 2 * share * lat * lat,
        )
        return sent

    targets = page_lists[:, :, 0]
    owned = targets == position
    counts = jnp.sum(owned.astype(jnp.int32), axis=1)
    none = targets.shape[1]
    order = jnp.arange(none, dtype=jnp.int32)[None, :]
    slot0 = jnp.min(jnp.where(owned, order, none), axis=1)
    slot1 = jnp.min(jnp.where(owned & (order > slot0[:, None]), order, none), axis=1)
    slots = jnp.minimum(jnp.stack([slot0, slot1], axis=1), none - 1).reshape(-1)
    limit = jnp.minimum(context_lengths, counts[None, :] * PAGE)
    limit = jnp.repeat(limit.T, queries.shape[2], axis=1)[:, :, None]
    new = new_latent.transpose(1, 0, 2)

    def decode(layer, pages, carried, last=False):
        return decode_pair(layer, slots, queries, new, limit, pages, carried, last)

    pages = []
    for even in range(2, layers, 2):
        if even == 2:
            sent, state, held = advance((1,), (2, 3), got, state, earlier)
        else:
            held = got.reshape(mine, 2 * lat)
            sent, state = advance((even - 2, even - 1), (even, even + 1), got, state)
        pages.append(lax.all_gather(held, "segment", axis=0))
        got = exchanged(sent, "wide")
        if even < layers - 2:
            got = exchanged(pair_step(even, got, wide), "wide")
    out = decode(0, pages[0], None)
    got, out = lax.optimization_barrier((got, out))

    got = exchanged(pair_step(layers - 2, got, segments), "segment")
    out = decode(2, pages[1], out)
    got, out = lax.optimization_barrier((got, out))
    (sent,) = call(
        functools.partial(choose_kernel, layers - 2),
        [whole(got.shape)],
        [whole((wide, share, 4 * lat))],
        [array(wide, share, 4 * lat)],
        [got],
        [slots],
    )
    got = exchanged(sent, "wide")
    out = decode(4, pages[2], out)
    got, out = lax.optimization_barrier((got, out))
    return decode(layers - 2, got, out, True)


def solution(mesh):
    in_specs = (
        P(None, None, "wide"),
        P("segment", "wide"),
        P("segment", "wide", None),
        P("segment", None, "wide"),
        P(),
        P("segment", None, "wide", None),
        P("segment", None, None),
        P("segment", None),
    )
    out_specs = P("segment", None, "wide", None)
    return jax.shard_map(shards, mesh=mesh, in_specs=in_specs, out_specs=out_specs, check_vma=False)
```

```python
import functools
import math

import jax
import jax.numpy as jnp
from jax import lax
from jax.experimental import pallas as pl
from jax.experimental.pallas import tpu as pltpu
from jax.sharding import PartitionSpec as P

PAGE = 128
LANES = 128

eps_norm = 1e-06
score_scale = 192.0 ** (-0.5)

params = pltpu.CompilerParams(vmem_limit_bytes=24 * 1024 * 1024)
in_hbm = pl.BlockSpec(memory_space=pltpu.HBM)
bf16 = jnp.bfloat16
f32 = jnp.float32


def dot(a, b):
    return jnp.dot(a, b, preferred_element_type=jnp.float32)


def dot_t(a, b):
    return lax.dot_general(a, b, (((1,), (1,)), ((), ())), preferred_element_type=jnp.float32)


def square_columns(values):
    squares = jnp.sum(values * values, axis=1, keepdims=True)
    high = squares.astype(bf16).astype(f32)
    column = lax.broadcasted_iota(jnp.int32, (values.shape[0], LANES), 1)
    return jnp.where(column == 0, high, jnp.where(column == 1, squares - high, 0.0))


def silu(latent):
    values = latent.astype(f32)
    return (values / (1.0 + jnp.exp(-values))).astype(bf16)


def exchanged(sent, axis):
    return lax.all_to_all(sent, axis, 0, 0, tiled=True)


def core_swap(x):
    length = lax.axis_size("segment")
    return lax.ppermute(x, "segment", [(i, i ^ 1) for i in range(length)])


def held_in_hbm(x):
    return pltpu.with_memory_space_constraint(x, pltpu.HBM)


def in_vmem(x):
    return pltpu.with_memory_space_constraint(x, pltpu.VMEM)


def whole(shape):
    return pl.BlockSpec(shape, lambda i, *s: (0,) * len(shape))


def call(body, in_specs, out_specs, out_shape, operands, scalars=(), scratch=(), flops=0):
    moved = sum(2 * math.prod(o.shape) for o in out_shape)
    return pl.pallas_call(
        body,
        grid_spec=pltpu.PrefetchScalarGridSpec(
            num_scalar_prefetch=len(scalars),
            grid=(1,),
            in_specs=in_specs,
            out_specs=out_specs,
            scratch_shapes=scratch,
        ),
        out_shape=out_shape,
        compiler_params=params,
        cost_estimate=pl.CostEstimate(flops=flops, bytes_accessed=2 * moved, transcendentals=0),
    )(*scalars, *operands)


def weights_kernel(where, latent_ref, gain_ref, back_ref, both_ref, lent_ref, *scratch):
    latent, gain, pair, sems = scratch
    copies = [
        pltpu.make_async_copy(latent_ref.at[0], latent, sems.at[0]),
        pltpu.make_async_copy(gain_ref, gain, sems.at[1]),
        pltpu.make_async_copy(back_ref.at[0], pair.at[1], sems.at[2]),
    ]
    for copy in copies:
        copy.start()
    size = latent.shape[0]
    row = lax.broadcasted_iota(jnp.int32, (size, size), 0)
    column = lax.broadcasted_iota(jnp.int32, (size, size), 1)
    copies[1].wait()
    gains = jnp.where(row == column, gain[...].astype(f32), 0.0).astype(bf16)
    copies[2].wait()
    sending = [pltpu.make_async_copy(pair.at[i], both_ref.at[i], sems.at[3 + i]) for i in range(2)]
    sending[1].start()

    @pl.when(where[0] != 0)
    def _():
        pltpu.make_async_copy(pair.at[1], lent_ref, sems.at[5]).start()

    copies[0].wait()
    pair[0] = dot(gains, latent[...]).astype(bf16)
    sending[0].start()

    @pl.when(where[0] == 0)
    def _():
        pltpu.make_async_copy(pair.at[0], lent_ref, sems.at[5]).start()

    pltpu.make_async_copy(pair.at[0], lent_ref, sems.at[5]).wait()
    for copy in sending:
        copy.wait()


def home_kernel(where, states_ref, both_ref, lent_ref, *rest):
    out_refs, (tokens, weight, sems) = rest[:-3], rest[-3:]
    groups, rows, width = tokens.shape
    loading = pltpu.make_async_copy(states_ref.at[:, where[1]], tokens, sems.at[0])
    loading.start()

    def products(weight_ref):
        loading.wait()
        product = dot(tokens[...].reshape(groups * rows, width), weight_ref[...]).astype(bf16)
        for group in range(groups):
            out_refs[group][...] = product[group * rows : (group + 1) * rows]

    @pl.when(where[0] == 0)
    def _():
        fetching = pltpu.make_async_copy(both_ref.at[0], weight, sems.at[1])
        fetching.start()
        fetching.wait()
        products(weight)

    @pl.when(where[0] != 0)
    def _():
        products(lent_ref)


def cross_kernel(where, both_ref, lent_ref, out_ref):
    @pl.when(where[0] & 1 == 0)
    def _():
        out_ref[...] = dot_t(both_ref[1], both_ref[1]).astype(bf16)

    @pl.when(where[0] & 1 != 0)
    def _():
        out_ref[...] = dot(lent_ref[...], both_ref[0]).astype(bf16)


def home_send_kernel(where, home_ref, a_ref, b_ref, c_ref, cross_ref, states_ref, out_ref):
    wide, share, _ = out_ref.shape
    rows, lat = home_ref.shape
    taken = a_ref[...].astype(f32) + b_ref[...].astype(f32) + c_ref[...].astype(f32)
    product = jnp.where(where[0] < 2, home_ref[...].astype(f32), taken)
    squares = square_columns(states_ref[...].reshape(rows, states_ref.shape[3]).astype(f32))
    out_ref[:, :, :LANES] = squares.reshape(wide, share, LANES).astype(bf16)
    out_ref[:, :, LANES : LANES + lat] = product.reshape(wide, share, lat).astype(bf16)
    parts = cross_ref.shape[0] // rows
    cross = cross_ref[...].astype(f32).reshape(wide, parts, share, lat)
    for part in range(parts):
        at = LANES + (1 + part) * lat
        out_ref[:, :, at : at + lat] = cross[:, part].astype(bf16)


def home_sum_kernel(width, got_ref, out_ref):
    wide, high, lat = out_ref.shape
    summed = jnp.sum(got_ref[...].astype(f32), axis=0)
    squares = summed[:, 0:1] + summed[:, 1:2]
    latent = summed[:, LANES : LANES + lat] * lax.rsqrt(squares / width + eps_norm)
    parts = [summed[:, at : at + lat] for at in range(LANES + lat, summed.shape[1], lat)]
    block = jnp.concatenate(parts + [latent], axis=0).astype(bf16)
    for place in range(wide):
        out_ref[place] = block


def single_kernel(width, got_ref, out_ref):
    summed = jnp.sum(got_ref[...].astype(f32), axis=0)
    squares = summed[:, 0:1] + summed[:, 1:2]
    latent = (summed[:, LANES:] * lax.rsqrt(squares / width + eps_norm)).astype(bf16)
    for place in range(out_ref.shape[0]):
        out_ref[place] = latent


def chain(width, summed, gram, mixing):
    lat = (summed.shape[1] - LANES) // 3
    squares = summed[:, 0:1] + summed[:, 1:2]
    at = [LANES + i * lat for i in range(4)]
    first = (summed[:, at[0] : at[1]] * lax.rsqrt(squares / width + eps_norm)).astype(bf16)
    activated = silu(first)
    towards = 2.0 * summed[:, at[2] : at[3]] + dot(activated, gram())
    squares = squares + jnp.sum(activated.astype(f32) * towards, axis=1, keepdims=True)
    second = summed[:, at[1] : at[2]] + dot(activated, mixing())
    second = (second * lax.rsqrt(squares / width + eps_norm)).astype(bf16)
    return first, second


def reside_kernel(lists, source_ref, *rest):
    out_refs, sems = rest[:-1], rest[-1]
    copies = []
    for out_ref, slots in zip(out_refs, lists):
        for i, slot in enumerate(slots):
            sem = sems.at[len(copies)]
            copies.append(pltpu.make_async_copy(source_ref.at[slot], out_ref.at[i], sem))
    for copy in copies:
        copy.start()
    for copy in copies:
        copy.wait()


def advance_kernel(before, layers, mode, where, got_ref, states_ref, *rest):
    refs = rest[: 1 + len(layers)]
    back_ref, latent_ref = refs[:2]
    outs = rest[len(refs) :]
    if mode == "later":
        earlier_ref, outs = outs[0], outs[1:]
    out_ref, state_ref, held_ref = outs[:3]
    wide, share, _ = out_ref.shape
    rows = wide * share
    lat = back_ref.shape[2]

    def latents_of(ref):
        block = ref[:, ref.shape[1] - share :]
        return block.astype(f32).reshape(rows, ref.shape[2])

    latents = latents_of(got_ref)
    activated = silu(latents)
    state = states_ref[...].reshape(rows, states_ref.shape[-1]).astype(f32)
    for i in range(len(before)):
        state = state + dot(activated[:, i * lat : (i + 1) * lat], back_ref[i])
    state = state.astype(bf16)
    state_ref[...] = state
    squares = square_columns(state.astype(f32))
    out_ref[:, :, :LANES] = squares.reshape(wide, share, LANES).astype(bf16)
    products = [dot(state, latent_ref[i]) for i in range(len(layers))]
    if len(layers) == 2:
        products.append(dot_t(state, refs[2][0]))
    for i, product in enumerate(products):
        at = LANES + i * lat
        out_ref[:, :, at : at + lat] = product.reshape(wide, share, lat).astype(bf16)
    if mode == "first":
        held_ref[...] = got_ref[:, : got_ref.shape[1] - share]
    elif mode == "later":
        held_ref[:, :lat] = latents_of(earlier_ref).astype(bf16)
        held_ref[:, lat:] = latents.astype(bf16)
    else:
        held_ref[...] = latents.astype(bf16)


def pair_kernel(width, got_ref, cross_ref, out_ref):
    summed = jnp.sum(got_ref[...].astype(f32), axis=0)
    first, second = chain(width, summed, lambda: cross_ref[0], lambda: cross_ref[1])
    lat = first.shape[1]
    for place in range(out_ref.shape[0]):
        out_ref[place, :, :lat] = first
        out_ref[place, :, lat:] = second


def choose_kernel(layer, slots, got_ref, out_ref):
    lat = got_ref.shape[2] // 2
    parts = []
    for i in range(2):
        for which in range(2):
            shard = got_ref[slots[2 * (layer + i) + which]]
            parts.append(shard[:, i * lat : (i + 1) * lat])
    for place in range(out_ref.shape[0]):
        for i, part in enumerate(parts):
            out_ref[place, :, i * lat : (i + 1) * lat] = part


def attend(q, new, keys, limit, heads):
    rows = q.shape[0]
    requests = new.shape[0]
    row = lax.broadcasted_iota(jnp.int32, (rows, requests), 0)
    start = lax.broadcasted_iota(jnp.int32, (rows, requests), 1) * heads
    pick = jnp.where((row >= start) & (row < start + heads), 1.0, 0.0).astype(bf16)
    own = dot(pick, new)
    scores = dot_t(q, keys) * score_scale
    place = lax.broadcasted_iota(jnp.int32, scores.shape, 1)
    scores = jnp.where(place < limit, scores, -jnp.inf)
    own_score = jnp.sum(q.astype(f32) * own, axis=1, keepdims=True) * score_scale
    top = jnp.maximum(jnp.max(scores, axis=1, keepdims=True), own_score)
    weights = jnp.exp(scores - top)
    own_weight = jnp.exp(own_score - top)
    total = jnp.sum(weights, axis=1, keepdims=True) + own_weight
    numer = dot(weights.astype(bf16), keys) + own_weight * own
    return (numer / total).astype(bf16)


def decode_kernel(layer, slots, q_ref, new_ref, limit_ref, pages_ref, *rest):
    out_ref, keys, sems = rest[-3:]
    requests, count, heads, lat = q_ref.shape
    copies = []
    for i in range(count):
        for which in range(2):
            page = pages_ref.at[slots[2 * (layer + i) + which], :, pl.ds(i * lat, lat)]
            at = keys.at[i, pl.ds(which * PAGE, PAGE)]
            copies.append(pltpu.make_async_copy(page, at, sems.at[2 * i + which]))
    for copy in copies:
        copy.start()
    for i in range(count):
        q = q_ref[:, i].reshape(requests * heads, lat)
        copies[2 * i].wait()
        copies[2 * i + 1].wait()
        result = attend(q, new_ref[i], keys[i], limit_ref[i], heads)
        out_ref[:, i] = result.reshape(requests, heads, lat)


def last_decode_kernel(q_ref, new_ref, limit_ref, pages_ref, carried_ref, out_ref):
    requests, count, heads, lat = q_ref.shape
    for i in range(count):
        q = q_ref[:, i].reshape(requests * heads, lat)
        at = 2 * i * lat
        pages = pages_ref[:, :, at : at + 2 * lat].astype(f32).reshape(PAGE, 2 * lat)
        keys = jnp.concatenate([pages[:, :lat], pages[:, lat:]], axis=0).astype(bf16)
        result = attend(q, new_ref[i], keys, limit_ref[i], heads)
        out_ref[:, i] = result.reshape(requests, heads, lat)


def decode_pair(layer, slots, queries, new, limit, pages, carried, last=False):
    requests, _, heads, lat = queries.shape
    half = layer // 2
    in_specs = [
        pl.BlockSpec((requests, 2, heads, lat), lambda i, *s: (0, half, 0, 0)),
        pl.BlockSpec((2, requests, lat), lambda i, *s: (half, 0, 0)),
        pl.BlockSpec((2, requests * heads, 1), lambda i, *s: (half, 0, 0)),
        whole(pages.shape) if last else in_hbm,
    ]
    scalars = [] if last else [slots]
    operands = scalars + [queries, new, limit, pages if last else held_in_hbm(pages)]
    aliases = {}
    if carried is not None:
        in_specs.append(in_hbm)
        aliases = {len(operands): 0}
        operands.append(carried)
    scratch = [pltpu.VMEM((2, 2 * PAGE, lat), bf16), pltpu.SemaphoreType.DMA((4,))]
    return pl.pallas_call(
        last_decode_kernel if last else functools.partial(decode_kernel, layer),
        grid_spec=pltpu.PrefetchScalarGridSpec(
            num_scalar_prefetch=len(scalars),
            grid=(1,),
            in_specs=in_specs,
            out_specs=pl.BlockSpec((requests, 2, heads, lat), lambda i, *s: (0, half, 0, 0)),
            scratch_shapes=[] if last else scratch,
        ),
        out_shape=jax.ShapeDtypeStruct(queries.shape, bf16),
        input_output_aliases=aliases,
        compiler_params=params,
        cost_estimate=pl.CostEstimate(
            flops=2 * 4 * requests * heads * 2 * PAGE * lat,
            bytes_accessed=2 * 2 * (2 * requests * heads + 2 * PAGE) * lat,
            transcendentals=2 * requests * heads * 2 * PAGE,
        ),
    )(*operands)


def shards(
    prompt_states, norm_gain, w_latent, w_back, page_lists, queries, new_latent, context_lengths
):
    segments = lax.axis_size("segment")
    wide = lax.axis_size("wide")
    position = lax.axis_index("segment")
    core = position & 1
    batches, tok_rows, local_width = prompt_states.shape
    width = local_width * wide
    tokens = batches * tok_rows
    mine = tokens // segments
    share = mine // wide
    layers = segments
    lat = w_latent.shape[2]
    where = jnp.stack([position, core]).astype(jnp.int32)

    def array(*shape):
        return jax.ShapeDtypeStruct(shape, bf16)

    def near(*shape):
        return pltpu.VMEM(shape, bf16)

    def far(*shape):
        return pltpu.HBM(shape, bf16)

    size = (2, local_width, lat)
    both, lent = call(
        weights_kernel,
        [in_hbm] * 3,
        [in_hbm] * 2,
        [far(*size), far(*size[1:])],
        [held_in_hbm(w_latent), held_in_hbm(norm_gain), held_in_hbm(w_back)],
        [where],
        [
            pltpu.VMEM(size[1:], bf16),
            pltpu.VMEM(norm_gain.shape, bf16),
            pltpu.VMEM(size, bf16),
            pltpu.SemaphoreType.DMA((6,)),
        ],
        flops=2 * local_width**3,
    )
    every = lax.all_gather(both, "segment", axis=0)
    lent = lax.ppermute(lent, "segment", [(i, i + 1) for i in range(0, segments, 2)])

    states = prompt_states.reshape(segments // 2, 2, mine, local_width)
    groups = segments // 2
    own_states = pl.BlockSpec((1, 1, mine, local_width), lambda i, s: (s[0] >> 1, s[1], 0, 0))
    home = call(
        home_kernel,
        [in_hbm, in_hbm, whole(size[1:])],
        [whole((mine, lat))] * groups,
        [near(mine, lat)] * groups,
        [held_in_hbm(states), held_in_hbm(both), lent],
        [where],
        [
            pltpu.VMEM((groups, mine, local_width), bf16),
            pltpu.VMEM((local_width, lat), bf16),
            pltpu.SemaphoreType.DMA((2,)),
        ],
        flops=2 * local_width**3,
    )
    (cross,) = call(
        cross_kernel,
        [whole(size), whole(size[1:])],
        [whole((lat, lat))],
        [near(lat, lat)],
        [both, lent],
        [where],
        flops=2 * local_width**3,
    )
    taken = [
        lax.ppermute(home[hop], "segment", [(0, 2 * hop), (1, 2 * hop + 1)])
        for hop in range(1, groups)
    ]
    high = lat // wide
    columns = LANES + lat + high // share * lat
    (sent,) = call(
        home_send_kernel,
        [whole((mine, lat))] * groups + [whole((lat, lat)), own_states],
        [whole((wide, share, columns))],
        [array(wide, share, columns)],
        [home[0]] + taken + [cross, states],
        [where],
    )
    got = exchanged(sent, "wide")
    (sent,) = call(
        functools.partial(home_sum_kernel, width),
        [whole(got.shape)],
        [whole((wide, high + share, lat))],
        [array(wide, high + share, lat)],
        [got],
    )
    def resident(source, *lists):
        parts = source.reshape((-1,) + source.shape[-2:])
        count = sum(len(slots) for slots in lists)
        return pl.pallas_call(
            functools.partial(reside_kernel, lists),
            in_specs=[in_hbm],
            out_specs=[pl.BlockSpec(memory_space=pltpu.VMEM)] * len(lists),
            out_shape=[pltpu.VMEM((len(slots),) + parts.shape[1:], bf16) for slots in lists],
            scratch_shapes=[pltpu.SemaphoreType.DMA((count,))],
            compiler_params=params,
            cost_estimate=pl.CostEstimate(
                flops=0, bytes_accessed=2 * count * parts.shape[1] * lat, transcendentals=0
            ),
        )(held_in_hbm(parts))

    def resident_weights(before, following):
        backs = [2 * layer + 1 for layer in before]
        latents = [2 * layer for layer in following]
        if len(following) == 1:
            return resident(every, backs, latents)
        return resident(every, backs, latents, [2 * following[0] + 1])

    def tied(*values):
        return lax.optimization_barrier(values)

    def advance(before, following, got, state, weights, earlier=None):
        mode = "first" if before == (0,) else "later" if earlier is not None else "pair"
        count = len(following) + (len(following) == 2)
        shapes = [
            array(wide, share, LANES + count * lat),
            near(mine, local_width),
            far(wide, high, lat) if mode == "first" else far(mine, 2 * lat),
        ]
        operands = [got, state] + [in_vmem(weight) for weight in weights]
        in_specs = [whole(got.shape), own_states if mode == "first" else whole(state.shape)]
        in_specs += [whole(weight.shape) for weight in weights]
        if mode == "later":
            in_specs.append(whole(earlier.shape))
            operands.append(earlier)
        return call(
            functools.partial(advance_kernel, before, following, mode),
            in_specs,
            [whole(s.shape) for s in shapes],
            shapes,
            operands,
            [where],
            flops=2 * (len(before) + count) * mine * lat * local_width,
        )

    def pair_step(got, crosses, copies):
        (sent,) = call(
            functools.partial(pair_kernel, width),
            [whole(got.shape), whole(crosses[0].shape)],
            [whole((copies, share, 2 * lat))],
            [array(copies, share, 2 * lat)],
            [got, in_vmem(crosses[0])],
            flops=2 * 2 * share * lat * lat,
        )
        return sent

    got, weights = tied(exchanged(sent, "wide"), resident_weights((0,), (1,)))

    earlier = got
    sent, state, cross = advance((0,), (1,), got, states, weights)
    crosses = lax.all_gather(cross.reshape(lat, lat), "segment", axis=0)
    got = exchanged(sent, "wide")
    (sent,) = call(
        functools.partial(single_kernel, width),
        [whole(got.shape)],
        [whole((wide, share, lat))],
        [array(wide, share, lat)],
        [got],
    )
    got, weights = tied(exchanged(sent, "wide"), resident_weights((1,), (2, 3)))

    pages = []
    for even in range(2, layers, 2):
        odd = even + 1
        before = (1,) if even == 2 else (even - 2, even - 1)
        extra = earlier if even == 2 else None
        sent, state, held = advance(before, (even, odd), got, state, weights, extra)
        pages.append(lax.all_gather(held, "segment", axis=0))
        got, mixing = tied(exchanged(sent, "wide"), resident(crosses, [even, odd]))
        if odd < layers - 1:
            sent = pair_step(got, mixing, wide)
            following = resident_weights((even, odd), (even + 2, even + 3))
            got, weights = tied(exchanged(sent, "wide"), following)

    targets = page_lists[:, :, 0]
    owned = targets == position
    counts = jnp.sum(owned.astype(jnp.int32), axis=1)
    none = targets.shape[1]
    order = jnp.arange(none, dtype=jnp.int32)[None, :]
    slot0 = jnp.min(jnp.where(owned, order, none), axis=1)
    slot1 = jnp.min(jnp.where(owned & (order > slot0[:, None]), order, none), axis=1)
    slots = jnp.minimum(jnp.stack([slot0, slot1], axis=1), none - 1).reshape(-1)
    limit = jnp.minimum(context_lengths, counts[None, :] * PAGE)
    limit = jnp.repeat(limit.T, queries.shape[2], axis=1)[:, :, None]
    new = new_latent.transpose(1, 0, 2)

    def decode(layer, pages, carried, last=False):
        return decode_pair(layer, slots, queries, new, limit, pages, carried, last)

    out = decode(0, pages[0], None)
    got, out = lax.optimization_barrier((got, out))

    got = exchanged(pair_step(got, mixing, segments), "segment")
    out = decode(2, pages[1], out)
    got, out = lax.optimization_barrier((got, out))
    (sent,) = call(
        functools.partial(choose_kernel, layers - 2),
        [whole(got.shape)],
        [whole((wide, share, 4 * lat))],
        [array(wide, share, 4 * lat)],
        [got],
        [slots],
    )
    got = exchanged(sent, "wide")
    out = decode(4, pages[2], out)
    got, out = lax.optimization_barrier((got, out))
    return decode(layers - 2, got, out, True)


def solution(mesh):
    in_specs = (
        P(None, None, "wide"),
        P("segment", "wide"),
        P("segment", "wide", None),
        P("segment", None, "wide"),
        P(),
        P("segment", None, "wide", None),
        P("segment", None, None),
        P("segment", None),
    )
    out_specs = P("segment", None, "wide", None)
    return jax.shard_map(shards, mesh=mesh, in_specs=in_specs, out_specs=out_specs, check_vma=False)
```

```python
import functools
import math

import jax
import jax.numpy as jnp
from jax import lax
from jax.experimental import pallas as pl
from jax.experimental.pallas import tpu as pltpu
from jax.sharding import PartitionSpec as P

PAGE = 128
LANES = 128

eps_norm = 1e-06
score_scale = 192.0 ** (-0.5)

params = pltpu.CompilerParams(vmem_limit_bytes=24 * 1024 * 1024)
in_hbm = pl.BlockSpec(memory_space=pltpu.HBM)
bf16 = jnp.bfloat16
f32 = jnp.float32


def dot(a, b):
    return jnp.dot(a, b, preferred_element_type=jnp.float32)


def dot_t(a, b):
    return lax.dot_general(a, b, (((1,), (1,)), ((), ())), preferred_element_type=jnp.float32)


def square_columns(values):
    squares = jnp.sum(values * values, axis=1, keepdims=True)
    high = squares.astype(bf16).astype(f32)
    column = lax.broadcasted_iota(jnp.int32, (values.shape[0], LANES), 1)
    return jnp.where(column == 0, high, jnp.where(column == 1, squares - high, 0.0))


def silu(latent):
    values = latent.astype(f32)
    return (values / (1.0 + jnp.exp(-values))).astype(bf16)


def exchanged(sent, axis):
    return lax.all_to_all(sent, axis, 0, 0, tiled=True)


def core_swap(x):
    length = lax.axis_size("segment")
    return lax.ppermute(x, "segment", [(i, i ^ 1) for i in range(length)])


def held_in_hbm(x):
    return pltpu.with_memory_space_constraint(x, pltpu.HBM)


def in_vmem(x):
    return pltpu.with_memory_space_constraint(x, pltpu.VMEM)


def whole(shape):
    return pl.BlockSpec(shape, lambda i, *s: (0,) * len(shape))


def call(body, in_specs, out_specs, out_shape, operands, scalars=(), scratch=(), flops=0):
    moved = sum(2 * math.prod(o.shape) for o in out_shape)
    return pl.pallas_call(
        body,
        grid_spec=pltpu.PrefetchScalarGridSpec(
            num_scalar_prefetch=len(scalars),
            grid=(1,),
            in_specs=in_specs,
            out_specs=out_specs,
            scratch_shapes=scratch,
        ),
        out_shape=out_shape,
        compiler_params=params,
        cost_estimate=pl.CostEstimate(flops=flops, bytes_accessed=2 * moved, transcendentals=0),
    )(*scalars, *operands)


def weights_kernel(where, latent_ref, gain_ref, back_ref, both_ref, lent_ref, *scratch):
    latent, gain, pair, sems = scratch
    copies = [
        pltpu.make_async_copy(latent_ref.at[0], latent, sems.at[0]),
        pltpu.make_async_copy(gain_ref, gain, sems.at[1]),
        pltpu.make_async_copy(back_ref.at[0], pair.at[1], sems.at[2]),
    ]
    for copy in copies:
        copy.start()
    size = latent.shape[0]
    row = lax.broadcasted_iota(jnp.int32, (size, size), 0)
    column = lax.broadcasted_iota(jnp.int32, (size, size), 1)
    copies[1].wait()
    gains = jnp.where(row == column, gain[...].astype(f32), 0.0).astype(bf16)
    copies[2].wait()
    sending = [pltpu.make_async_copy(pair.at[i], both_ref.at[i], sems.at[3 + i]) for i in range(2)]
    sending[1].start()

    @pl.when(where[0] != 0)
    def _():
        pltpu.make_async_copy(pair.at[1], lent_ref, sems.at[5]).start()

    copies[0].wait()
    pair[0] = dot(gains, latent[...]).astype(bf16)
    sending[0].start()

    @pl.when(where[0] == 0)
    def _():
        pltpu.make_async_copy(pair.at[0], lent_ref, sems.at[5]).start()

    pltpu.make_async_copy(pair.at[0], lent_ref, sems.at[5]).wait()
    for copy in sending:
        copy.wait()


def home_kernel(where, states_ref, both_ref, lent_ref, *rest):
    out_refs, (tokens, weight, sems) = rest[:-3], rest[-3:]
    groups, rows, width = tokens.shape
    loading = pltpu.make_async_copy(states_ref.at[:, where[1]], tokens, sems.at[0])
    loading.start()

    def products(weight_ref):
        loading.wait()
        product = dot(tokens[...].reshape(groups * rows, width), weight_ref[...]).astype(bf16)
        for group in range(groups):
            out_refs[group][...] = product[group * rows : (group + 1) * rows]

    @pl.when(where[0] == 0)
    def _():
        fetching = pltpu.make_async_copy(both_ref.at[0], weight, sems.at[1])
        fetching.start()
        fetching.wait()
        products(weight)

    @pl.when(where[0] != 0)
    def _():
        products(lent_ref)


def cross_kernel(where, both_ref, lent_ref, out_ref):
    @pl.when(where[0] & 1 == 0)
    def _():
        out_ref[...] = dot_t(both_ref[1], both_ref[1]).astype(bf16)

    @pl.when(where[0] & 1 != 0)
    def _():
        out_ref[...] = dot(lent_ref[...], both_ref[0]).astype(bf16)


def home_send_kernel(where, home_ref, a_ref, b_ref, c_ref, cross_ref, states_ref, out_ref):
    wide, share, _ = out_ref.shape
    rows, lat = home_ref.shape
    taken = a_ref[...].astype(f32) + b_ref[...].astype(f32) + c_ref[...].astype(f32)
    product = jnp.where(where[0] < 2, home_ref[...].astype(f32), taken)
    squares = square_columns(states_ref[...].reshape(rows, states_ref.shape[3]).astype(f32))
    out_ref[:, :, :LANES] = squares.reshape(wide, share, LANES).astype(bf16)
    out_ref[:, :, LANES : LANES + lat] = product.reshape(wide, share, lat).astype(bf16)
    parts = cross_ref.shape[0] // rows
    cross = cross_ref[...].astype(f32).reshape(wide, parts, share, lat)
    for part in range(parts):
        at = LANES + (1 + part) * lat
        out_ref[:, :, at : at + lat] = cross[:, part].astype(bf16)


def home_sum_kernel(width, got_ref, out_ref):
    wide, high, lat = out_ref.shape
    summed = jnp.sum(got_ref[...].astype(f32), axis=0)
    squares = summed[:, 0:1] + summed[:, 1:2]
    latent = summed[:, LANES : LANES + lat] * lax.rsqrt(squares / width + eps_norm)
    parts = [summed[:, at : at + lat] for at in range(LANES + lat, summed.shape[1], lat)]
    block = jnp.concatenate(parts + [latent], axis=0).astype(bf16)
    for place in range(wide):
        out_ref[place] = block


def single_kernel(width, got_ref, out_ref):
    summed = jnp.sum(got_ref[...].astype(f32), axis=0)
    squares = summed[:, 0:1] + summed[:, 1:2]
    latent = (summed[:, LANES:] * lax.rsqrt(squares / width + eps_norm)).astype(bf16)
    for place in range(out_ref.shape[0]):
        out_ref[place] = latent


def chain(width, summed, gram, mixing):
    lat = (summed.shape[1] - LANES) // 3
    squares = summed[:, 0:1] + summed[:, 1:2]
    at = [LANES + i * lat for i in range(4)]
    first = (summed[:, at[0] : at[1]] * lax.rsqrt(squares / width + eps_norm)).astype(bf16)
    activated = silu(first)
    towards = 2.0 * summed[:, at[2] : at[3]] + dot(activated, gram())
    squares = squares + jnp.sum(activated.astype(f32) * towards, axis=1, keepdims=True)
    second = summed[:, at[1] : at[2]] + dot(activated, mixing())
    second = (second * lax.rsqrt(squares / width + eps_norm)).astype(bf16)
    return first, second


def reside_kernel(lists, source_ref, *rest):
    out_refs, sems = rest[:-1], rest[-1]
    copies = []
    for out_ref, slots in zip(out_refs, lists):
        for i, slot in enumerate(slots):
            sem = sems.at[len(copies)]
            copies.append(pltpu.make_async_copy(source_ref.at[slot], out_ref.at[i], sem))
    for copy in copies:
        copy.start()
    for copy in copies:
        copy.wait()


def advance_kernel(before, layers, mode, where, got_ref, states_ref, *rest):
    refs = rest[: 1 + len(layers)]
    back_ref, latent_ref = refs[:2]
    outs = rest[len(refs) :]
    if mode == "later":
        earlier_ref, outs = outs[0], outs[1:]
    out_ref, state_ref, held_ref = outs[:3]
    wide, share, _ = out_ref.shape
    rows = wide * share
    lat = back_ref.shape[2]

    def latents_of(ref):
        block = ref[:, ref.shape[1] - share :]
        return block.astype(f32).reshape(rows, ref.shape[2])

    latents = latents_of(got_ref)
    activated = silu(latents)
    state = states_ref[...].reshape(rows, states_ref.shape[-1]).astype(f32)
    for i in range(len(before)):
        state = state + dot(activated[:, i * lat : (i + 1) * lat], back_ref[i])
    state = state.astype(bf16)
    state_ref[...] = state
    squares = square_columns(state.astype(f32))
    out_ref[:, :, :LANES] = squares.reshape(wide, share, LANES).astype(bf16)
    products = [dot(state, latent_ref[i]) for i in range(len(layers))]
    if len(layers) == 2:
        products.append(dot_t(state, refs[2][0]))
    for i, product in enumerate(products):
        at = LANES + i * lat
        out_ref[:, :, at : at + lat] = product.reshape(wide, share, lat).astype(bf16)
    if mode == "first":
        held_ref[...] = got_ref[:, : got_ref.shape[1] - share]
    elif mode == "later":
        held_ref[:, :lat] = latents_of(earlier_ref).astype(bf16)
        held_ref[:, lat:] = latents.astype(bf16)
    else:
        held_ref[...] = latents.astype(bf16)


def pair_kernel(width, got_ref, cross_ref, out_ref):
    summed = jnp.sum(got_ref[...].astype(f32), axis=0)
    first, second = chain(width, summed, lambda: cross_ref[0], lambda: cross_ref[1])
    lat = first.shape[1]
    for place in range(out_ref.shape[0]):
        out_ref[place, :, :lat] = first
        out_ref[place, :, lat:] = second


def choose_kernel(layer, slots, got_ref, out_ref):
    lat = got_ref.shape[2] // 2
    parts = []
    for i in range(2):
        for which in range(2):
            shard = got_ref[slots[2 * (layer + i) + which]]
            parts.append(shard[:, i * lat : (i + 1) * lat])
    for place in range(out_ref.shape[0]):
        for i, part in enumerate(parts):
            out_ref[place, :, i * lat : (i + 1) * lat] = part


def attend(q, new, keys, limit, heads):
    rows = q.shape[0]
    requests = new.shape[0]
    row = lax.broadcasted_iota(jnp.int32, (rows, requests), 0)
    start = lax.broadcasted_iota(jnp.int32, (rows, requests), 1) * heads
    pick = jnp.where((row >= start) & (row < start + heads), 1.0, 0.0).astype(bf16)
    own = dot(pick, new)
    scores = dot_t(q, keys) * score_scale
    place = lax.broadcasted_iota(jnp.int32, scores.shape, 1)
    scores = jnp.where(place < limit, scores, -jnp.inf)
    own_score = jnp.sum(q.astype(f32) * own, axis=1, keepdims=True) * score_scale
    top = jnp.maximum(jnp.max(scores, axis=1, keepdims=True), own_score)
    weights = jnp.exp(scores - top)
    own_weight = jnp.exp(own_score - top)
    total = jnp.sum(weights, axis=1, keepdims=True) + own_weight
    numer = dot(weights.astype(bf16), keys) + own_weight * own
    return (numer / total).astype(bf16)


def decode_kernel(layer, slots, q_ref, new_ref, limit_ref, pages_ref, *rest):
    out_ref, keys, sems = rest[-3:]
    requests, count, heads, lat = q_ref.shape
    copies = []
    for i in range(count):
        for which in range(2):
            page = pages_ref.at[slots[2 * (layer + i) + which], :, pl.ds(i * lat, lat)]
            at = keys.at[i, pl.ds(which * PAGE, PAGE)]
            copies.append(pltpu.make_async_copy(page, at, sems.at[2 * i + which]))
    for copy in copies:
        copy.start()
    for i in range(count):
        q = q_ref[:, i].reshape(requests * heads, lat)
        copies[2 * i].wait()
        copies[2 * i + 1].wait()
        result = attend(q, new_ref[i], keys[i], limit_ref[i], heads)
        out_ref[:, i] = result.reshape(requests, heads, lat)


def last_decode_kernel(q_ref, new_ref, limit_ref, pages_ref, carried_ref, out_ref):
    requests, count, heads, lat = q_ref.shape
    for i in range(count):
        q = q_ref[:, i].reshape(requests * heads, lat)
        at = 2 * i * lat
        pages = pages_ref[:, :, at : at + 2 * lat].astype(f32).reshape(PAGE, 2 * lat)
        keys = jnp.concatenate([pages[:, :lat], pages[:, lat:]], axis=0).astype(bf16)
        result = attend(q, new_ref[i], keys, limit_ref[i], heads)
        out_ref[:, i] = result.reshape(requests, heads, lat)


def decode_pair(layer, slots, queries, new, limit, pages, carried, last=False):
    requests, _, heads, lat = queries.shape
    half = layer // 2
    in_specs = [
        pl.BlockSpec((requests, 2, heads, lat), lambda i, *s: (0, half, 0, 0)),
        pl.BlockSpec((2, requests, lat), lambda i, *s: (half, 0, 0)),
        pl.BlockSpec((2, requests * heads, 1), lambda i, *s: (half, 0, 0)),
        whole(pages.shape) if last else in_hbm,
    ]
    scalars = [] if last else [slots]
    operands = scalars + [queries, new, limit, pages if last else held_in_hbm(pages)]
    aliases = {}
    if carried is not None:
        in_specs.append(in_hbm)
        aliases = {len(operands): 0}
        operands.append(carried)
    scratch = [pltpu.VMEM((2, 2 * PAGE, lat), bf16), pltpu.SemaphoreType.DMA((4,))]
    return pl.pallas_call(
        last_decode_kernel if last else functools.partial(decode_kernel, layer),
        grid_spec=pltpu.PrefetchScalarGridSpec(
            num_scalar_prefetch=len(scalars),
            grid=(1,),
            in_specs=in_specs,
            out_specs=pl.BlockSpec((requests, 2, heads, lat), lambda i, *s: (0, half, 0, 0)),
            scratch_shapes=[] if last else scratch,
        ),
        out_shape=jax.ShapeDtypeStruct(queries.shape, bf16),
        input_output_aliases=aliases,
        compiler_params=params,
        cost_estimate=pl.CostEstimate(
            flops=2 * 4 * requests * heads * 2 * PAGE * lat,
            bytes_accessed=2 * 2 * (2 * requests * heads + 2 * PAGE) * lat,
            transcendentals=2 * requests * heads * 2 * PAGE,
        ),
    )(*operands)


def shards(
    prompt_states, norm_gain, w_latent, w_back, page_lists, queries, new_latent, context_lengths
):
    segments = lax.axis_size("segment")
    wide = lax.axis_size("wide")
    position = lax.axis_index("segment")
    core = position & 1
    batches, tok_rows, local_width = prompt_states.shape
    width = local_width * wide
    tokens = batches * tok_rows
    mine = tokens // segments
    share = mine // wide
    layers = segments
    lat = w_latent.shape[2]
    where = jnp.stack([position, core]).astype(jnp.int32)

    def array(*shape):
        return jax.ShapeDtypeStruct(shape, bf16)

    def near(*shape):
        return pltpu.VMEM(shape, bf16)

    def far(*shape):
        return pltpu.HBM(shape, bf16)

    size = (2, local_width, lat)
    both, lent = call(
        weights_kernel,
        [in_hbm] * 3,
        [in_hbm] * 2,
        [far(*size), far(*size[1:])],
        [held_in_hbm(w_latent), held_in_hbm(norm_gain), held_in_hbm(w_back)],
        [where],
        [
            pltpu.VMEM(size[1:], bf16),
            pltpu.VMEM(norm_gain.shape, bf16),
            pltpu.VMEM(size, bf16),
            pltpu.SemaphoreType.DMA((6,)),
        ],
        flops=2 * local_width**3,
    )
    every = lax.all_gather(both, "segment", axis=0)
    lent = lax.ppermute(lent, "segment", [(i, i + 1) for i in range(0, segments, 2)])

    states = prompt_states.reshape(segments // 2, 2, mine, local_width)
    groups = segments // 2
    own_states = pl.BlockSpec((1, 1, mine, local_width), lambda i, s: (s[0] >> 1, s[1], 0, 0))
    home = call(
        home_kernel,
        [in_hbm, in_hbm, whole(size[1:])],
        [whole((mine, lat))] * groups,
        [near(mine, lat)] * groups,
        [held_in_hbm(states), held_in_hbm(both), lent],
        [where],
        [
            pltpu.VMEM((groups, mine, local_width), bf16),
            pltpu.VMEM((local_width, lat), bf16),
            pltpu.SemaphoreType.DMA((2,)),
        ],
        flops=2 * local_width**3,
    )
    (cross,) = call(
        cross_kernel,
        [whole(size), whole(size[1:])],
        [whole((lat, lat))],
        [near(lat, lat)],
        [both, lent],
        [where],
        flops=2 * local_width**3,
    )
    taken = [
        lax.ppermute(home[hop], "segment", [(0, 2 * hop), (1, 2 * hop + 1)])
        for hop in range(1, groups)
    ]
    high = lat // wide
    columns = LANES + lat + high // share * lat
    (sent,) = call(
        home_send_kernel,
        [whole((mine, lat))] * groups + [whole((lat, lat)), own_states],
        [whole((wide, share, columns))],
        [array(wide, share, columns)],
        [home[0]] + taken + [cross, states],
        [where],
    )
    got = exchanged(sent, "wide")
    (sent,) = call(
        functools.partial(home_sum_kernel, width),
        [whole(got.shape)],
        [whole((wide, high + share, lat))],
        [array(wide, high + share, lat)],
        [got],
    )
    def resident(source, *lists):
        parts = source.reshape((-1,) + source.shape[-2:])
        count = sum(len(slots) for slots in lists)
        return pl.pallas_call(
            functools.partial(reside_kernel, lists),
            in_specs=[in_hbm],
            out_specs=[pl.BlockSpec(memory_space=pltpu.VMEM)] * len(lists),
            out_shape=[pltpu.VMEM((len(slots),) + parts.shape[1:], bf16) for slots in lists],
            scratch_shapes=[pltpu.SemaphoreType.DMA((count,))],
            compiler_params=params,
            cost_estimate=pl.CostEstimate(
                flops=0, bytes_accessed=2 * count * parts.shape[1] * lat, transcendentals=0
            ),
        )(held_in_hbm(parts))

    def resident_weights(before, following):
        backs = [2 * layer + 1 for layer in before]
        latents = [2 * layer for layer in following]
        if len(following) == 1:
            return resident(every, backs, latents)
        return resident(every, backs, latents, [2 * following[0] + 1])

    def tied(*values):
        return lax.optimization_barrier(values)

    def advance(before, following, got, state, weights, earlier=None):
        mode = "first" if before == (0,) else "later" if earlier is not None else "pair"
        count = len(following) + (len(following) == 2)
        shapes = [
            (array if mode == "first" else far)(wide, share, LANES + count * lat),
            near(mine, local_width),
            far(wide, high, lat) if mode == "first" else far(mine, 2 * lat),
        ]
        operands = [got, state] + [in_vmem(weight) for weight in weights]
        in_specs = [whole(got.shape), own_states if mode == "first" else whole(state.shape)]
        in_specs += [whole(weight.shape) for weight in weights]
        if mode == "later":
            in_specs.append(whole(earlier.shape))
            operands.append(earlier)
        return call(
            functools.partial(advance_kernel, before, following, mode),
            in_specs,
            [whole(s.shape) for s in shapes],
            shapes,
            operands,
            [where],
            flops=2 * (len(before) + count) * mine * lat * local_width,
        )

    def pair_step(got, crosses, copies):
        (sent,) = call(
            functools.partial(pair_kernel, width),
            [whole(got.shape), whole(crosses[0].shape)],
            [whole((copies, share, 2 * lat))],
            [array(copies, share, 2 * lat)],
            [got, in_vmem(crosses[0])],
            flops=2 * 2 * share * lat * lat,
        )
        return sent

    got, weights = tied(exchanged(sent, "wide"), resident_weights((0,), (1,)))

    earlier = got
    sent, state, cross = advance((0,), (1,), got, states, weights)
    crosses = lax.all_gather(cross.reshape(lat, lat), "segment", axis=0)
    got = exchanged(sent, "wide")
    (sent,) = call(
        functools.partial(single_kernel, width),
        [whole(got.shape)],
        [whole((wide, share, lat))],
        [array(wide, share, lat)],
        [got],
    )
    got, weights = tied(exchanged(sent, "wide"), resident_weights((1,), (2, 3)))

    pages = []
    for even in range(2, layers, 2):
        odd = even + 1
        before = (1,) if even == 2 else (even - 2, even - 1)
        extra = earlier if even == 2 else None
        sent, state, held = advance(before, (even, odd), got, state, weights, extra)
        pages.append(lax.all_gather(held, "segment", axis=0))
        if odd < layers - 1:
            following = resident_weights((even, odd), (even + 2, even + 3))
            mixing = resident(crosses, [even, odd])
            got, mixing, weights = tied(exchanged(sent, "wide"), mixing, following)
            got = exchanged(pair_step(got, mixing, wide), "wide")
        else:
            got, mixing = tied(exchanged(sent, "wide"), resident(crosses, [even, odd]))

    targets = page_lists[:, :, 0]
    owned = targets == position
    counts = jnp.sum(owned.astype(jnp.int32), axis=1)
    none = targets.shape[1]
    order = jnp.arange(none, dtype=jnp.int32)[None, :]
    slot0 = jnp.min(jnp.where(owned, order, none), axis=1)
    slot1 = jnp.min(jnp.where(owned & (order > slot0[:, None]), order, none), axis=1)
    slots = jnp.minimum(jnp.stack([slot0, slot1], axis=1), none - 1).reshape(-1)
    limit = jnp.minimum(context_lengths, counts[None, :] * PAGE)
    limit = jnp.repeat(limit.T, queries.shape[2], axis=1)[:, :, None]
    new = new_latent.transpose(1, 0, 2)

    def decode(layer, pages, carried, last=False):
        return decode_pair(layer, slots, queries, new, limit, pages, carried, last)

    out = decode(0, pages[0], None)
    got, out = lax.optimization_barrier((got, out))

    got = exchanged(pair_step(got, mixing, segments), "segment")
    out = decode(2, pages[1], out)
    got, out = lax.optimization_barrier((got, out))
    (sent,) = call(
        functools.partial(choose_kernel, layers - 2),
        [whole(got.shape)],
        [whole((wide, share, 4 * lat))],
        [array(wide, share, 4 * lat)],
        [got],
        [slots],
    )
    got = exchanged(sent, "wide")
    out = decode(4, pages[2], out)
    got, out = lax.optimization_barrier((got, out))
    return decode(layers - 2, got, out, True)


def solution(mesh):
    in_specs = (
        P(None, None, "wide"),
        P("segment", "wide"),
        P("segment", "wide", None),
        P("segment", None, "wide"),
        P(),
        P("segment", None, "wide", None),
        P("segment", None, None),
        P("segment", None),
    )
    out_specs = P("segment", None, "wide", None)
    return jax.shard_map(shards, mesh=mesh, in_specs=in_specs, out_specs=out_specs, check_vma=False)
```

```python
import functools
import math

import jax
import jax.numpy as jnp
from jax import lax
from jax.experimental import pallas as pl
from jax.experimental.pallas import tpu as pltpu
from jax.sharding import PartitionSpec as P

PAGE = 128
LANES = 128

eps_norm = 1e-06
score_scale = 192.0 ** (-0.5)

params = pltpu.CompilerParams(vmem_limit_bytes=24 * 1024 * 1024)
in_hbm = pl.BlockSpec(memory_space=pltpu.HBM)
bf16 = jnp.bfloat16
f32 = jnp.float32


def dot(a, b):
    return jnp.dot(a, b, preferred_element_type=jnp.float32)


def dot_t(a, b):
    return lax.dot_general(a, b, (((1,), (1,)), ((), ())), preferred_element_type=jnp.float32)


def square_columns(values):
    squares = jnp.sum(values * values, axis=1, keepdims=True)
    high = squares.astype(bf16).astype(f32)
    column = lax.broadcasted_iota(jnp.int32, (values.shape[0], LANES), 1)
    return jnp.where(column == 0, high, jnp.where(column == 1, squares - high, 0.0))


def silu(latent):
    values = latent.astype(f32)
    return (values / (1.0 + jnp.exp(-values))).astype(bf16)


def exchanged(sent, axis):
    return lax.all_to_all(sent, axis, 0, 0, tiled=True)


def core_swap(x):
    length = lax.axis_size("segment")
    return lax.ppermute(x, "segment", [(i, i ^ 1) for i in range(length)])


def held_in_hbm(x):
    return pltpu.with_memory_space_constraint(x, pltpu.HBM)


def in_vmem(x):
    return pltpu.with_memory_space_constraint(x, pltpu.VMEM)


def whole(shape):
    return pl.BlockSpec(shape, lambda i, *s: (0,) * len(shape))


def call(body, in_specs, out_specs, out_shape, operands, scalars=(), scratch=(), flops=0):
    moved = sum(2 * math.prod(o.shape) for o in out_shape)
    return pl.pallas_call(
        body,
        grid_spec=pltpu.PrefetchScalarGridSpec(
            num_scalar_prefetch=len(scalars),
            grid=(1,),
            in_specs=in_specs,
            out_specs=out_specs,
            scratch_shapes=scratch,
        ),
        out_shape=out_shape,
        compiler_params=params,
        cost_estimate=pl.CostEstimate(flops=flops, bytes_accessed=2 * moved, transcendentals=0),
    )(*scalars, *operands)


def weights_kernel(where, latent_ref, gain_ref, back_ref, both_ref, lent_ref, *scratch):
    latent, gain, pair, sems = scratch
    size = latent.shape[0]
    half = size // 2
    halves = [pl.ds(i * half, half) for i in range(2)]
    copies = [
        pltpu.make_async_copy(gain_ref, gain, sems.at[0]),
        pltpu.make_async_copy(latent_ref.at[0, halves[0]], latent.at[halves[0]], sems.at[1]),
        pltpu.make_async_copy(latent_ref.at[0, halves[1]], latent.at[halves[1]], sems.at[2]),
        pltpu.make_async_copy(back_ref.at[0], pair.at[1], sems.at[3]),
    ]
    for copy in copies:
        copy.start()
    copies[0].wait()
    gains = jnp.broadcast_to(gain[...].astype(f32), (8, size)).T[:, :1]
    sending = []
    for i, rows in enumerate(halves):
        copies[1 + i].wait()
        scaled = latent[rows].astype(f32) * gains[i * half : (i + 1) * half]
        pair[0, rows] = scaled.astype(bf16)
        to = both_ref.at[0, rows]
        sending.append(pltpu.make_async_copy(pair.at[0, rows], to, sems.at[4 + i]))
        sending[i].start()
    copies[3].wait()
    sending.append(pltpu.make_async_copy(pair.at[1], both_ref.at[1], sems.at[6]))
    sending[2].start()

    @pl.when(where[0] == 0)
    def _():
        lent_ref[...] = pair[0]

    @pl.when(where[0] != 0)
    def _():
        lent_ref[...] = pair[1]

    for copy in sending:
        copy.wait()


def home_kernel(where, states_ref, mine_ref, lent_ref, *out_refs):
    groups, _, rows, width = states_ref.shape

    def products(weight_ref):
        tokens = states_ref[:, where[1]].reshape(groups * rows, width)
        product = dot(tokens, weight_ref[...]).astype(bf16)
        for group in range(groups):
            out_refs[group][...] = product[group * rows : (group + 1) * rows]

    @pl.when(where[0] == 0)
    def _():
        products(mine_ref)

    @pl.when(where[0] != 0)
    def _():
        products(lent_ref)


def cross_kernel(where, both_ref, lent_ref, out_ref):
    @pl.when(where[0] & 1 == 0)
    def _():
        out_ref[...] = dot_t(both_ref[1], both_ref[1]).astype(bf16)

    @pl.when(where[0] & 1 != 0)
    def _():
        out_ref[...] = dot(lent_ref[...], both_ref[0]).astype(bf16)


def home_send_kernel(where, home_ref, a_ref, b_ref, c_ref, cross_ref, states_ref, out_ref):
    wide, share, _ = out_ref.shape
    rows, lat = home_ref.shape
    taken = a_ref[...].astype(f32) + b_ref[...].astype(f32) + c_ref[...].astype(f32)
    product = jnp.where(where[0] < 2, home_ref[...].astype(f32), taken)
    squares = square_columns(states_ref[...].reshape(rows, states_ref.shape[3]).astype(f32))
    out_ref[:, :, :LANES] = squares.reshape(wide, share, LANES).astype(bf16)
    out_ref[:, :, LANES : LANES + lat] = product.reshape(wide, share, lat).astype(bf16)
    parts = cross_ref.shape[0] // rows
    cross = cross_ref[...].astype(f32).reshape(wide, parts, share, lat)
    for part in range(parts):
        at = LANES + (1 + part) * lat
        out_ref[:, :, at : at + lat] = cross[:, part].astype(bf16)


def home_sum_kernel(width, got_ref, out_ref):
    wide, high, lat = out_ref.shape
    summed = jnp.sum(got_ref[...].astype(f32), axis=0)
    squares = summed[:, 0:1] + summed[:, 1:2]
    latent = summed[:, LANES : LANES + lat] * lax.rsqrt(squares / width + eps_norm)
    parts = [summed[:, at : at + lat] for at in range(LANES + lat, summed.shape[1], lat)]
    block = jnp.concatenate(parts + [latent], axis=0).astype(bf16)
    for place in range(wide):
        out_ref[place] = block


def single_kernel(width, got_ref, out_ref):
    summed = jnp.sum(got_ref[...].astype(f32), axis=0)
    squares = summed[:, 0:1] + summed[:, 1:2]
    latent = (summed[:, LANES:] * lax.rsqrt(squares / width + eps_norm)).astype(bf16)
    for place in range(out_ref.shape[0]):
        out_ref[place] = latent


def chain(width, summed, gram, mixing):
    lat = (summed.shape[1] - LANES) // 3
    squares = summed[:, 0:1] + summed[:, 1:2]
    at = [LANES + i * lat for i in range(4)]
    first = (summed[:, at[0] : at[1]] * lax.rsqrt(squares / width + eps_norm)).astype(bf16)
    activated = silu(first)
    towards = 2.0 * summed[:, at[2] : at[3]] + dot(activated, gram())
    squares = squares + jnp.sum(activated.astype(f32) * towards, axis=1, keepdims=True)
    second = summed[:, at[1] : at[2]] + dot(activated, mixing())
    second = (second * lax.rsqrt(squares / width + eps_norm)).astype(bf16)
    return first, second


def reside_kernel(lists, source_ref, *rest):
    out_refs, sems = rest[:-1], rest[-1]
    copies = []
    for out_ref, slots in zip(out_refs, lists):
        for i, slot in enumerate(slots):
            sem = sems.at[len(copies)]
            copies.append(pltpu.make_async_copy(source_ref.at[slot], out_ref.at[i], sem))
    for copy in copies:
        copy.start()
    for copy in copies:
        copy.wait()


def advance_kernel(before, layers, mode, where, got_ref, states_ref, *rest):
    refs = rest[: 1 + len(layers)]
    back_ref, latent_ref = refs[:2]
    outs = rest[len(refs) :]
    if mode == "later":
        earlier_ref, outs = outs[0], outs[1:]
    out_ref, state_ref, held_ref = outs[:3]
    wide, share, _ = out_ref.shape
    rows = wide * share
    lat = back_ref.shape[2]

    def latents_of(ref):
        block = ref[:, ref.shape[1] - share :]
        return block.astype(f32).reshape(rows, ref.shape[2])

    latents = latents_of(got_ref)
    activated = silu(latents)
    state = states_ref[...].reshape(rows, states_ref.shape[-1]).astype(f32)
    for i in range(len(before)):
        state = state + dot(activated[:, i * lat : (i + 1) * lat], back_ref[i])
    state = state.astype(bf16)
    state_ref[...] = state
    squares = square_columns(state.astype(f32))
    out_ref[:, :, :LANES] = squares.reshape(wide, share, LANES).astype(bf16)
    products = [dot(state, latent_ref[i]) for i in range(len(layers))]
    if len(layers) == 2:
        products.append(dot_t(state, refs[2][0]))
    for i, product in enumerate(products):
        at = LANES + i * lat
        out_ref[:, :, at : at + lat] = product.reshape(wide, share, lat).astype(bf16)
    if mode == "first":
        held_ref[...] = got_ref[:, : got_ref.shape[1] - share]
    elif mode == "later":
        held_ref[:, :lat] = latents_of(earlier_ref).astype(bf16)
        held_ref[:, lat:] = latents.astype(bf16)
    else:
        held_ref[...] = latents.astype(bf16)


def pair_kernel(width, got_ref, cross_ref, out_ref):
    summed = jnp.sum(got_ref[...].astype(f32), axis=0)
    first, second = chain(width, summed, lambda: cross_ref[0], lambda: cross_ref[1])
    lat = first.shape[1]
    for place in range(out_ref.shape[0]):
        out_ref[place, :, :lat] = first
        out_ref[place, :, lat:] = second


def choose_kernel(layer, slots, got_ref, out_ref):
    lat = got_ref.shape[2] // 2
    parts = []
    for i in range(2):
        for which in range(2):
            shard = got_ref[slots[2 * (layer + i) + which]]
            parts.append(shard[:, i * lat : (i + 1) * lat])
    for place in range(out_ref.shape[0]):
        for i, part in enumerate(parts):
            out_ref[place, :, i * lat : (i + 1) * lat] = part


def attend(q, new, keys, limit, heads):
    rows = q.shape[0]
    requests = new.shape[0]
    row = lax.broadcasted_iota(jnp.int32, (rows, requests), 0)
    start = lax.broadcasted_iota(jnp.int32, (rows, requests), 1) * heads
    pick = jnp.where((row >= start) & (row < start + heads), 1.0, 0.0).astype(bf16)
    own = dot(pick, new)
    scores = dot_t(q, keys) * score_scale
    place = lax.broadcasted_iota(jnp.int32, scores.shape, 1)
    scores = jnp.where(place < limit, scores, -jnp.inf)
    own_score = jnp.sum(q.astype(f32) * own, axis=1, keepdims=True) * score_scale
    top = jnp.maximum(jnp.max(scores, axis=1, keepdims=True), own_score)
    weights = jnp.exp(scores - top)
    own_weight = jnp.exp(own_score - top)
    total = jnp.sum(weights, axis=1, keepdims=True) + own_weight
    numer = dot(weights.astype(bf16), keys) + own_weight * own
    return (numer / total).astype(bf16)


def decode_kernel(layer, slots, q_ref, new_ref, limit_ref, pages_ref, *rest):
    out_ref, keys, sems = rest[-3:]
    requests, count, heads, lat = q_ref.shape
    copies = []
    for i in range(count):
        for which in range(2):
            page = pages_ref.at[slots[2 * (layer + i) + which], :, pl.ds(i * lat, lat)]
            at = keys.at[i, pl.ds(which * PAGE, PAGE)]
            copies.append(pltpu.make_async_copy(page, at, sems.at[2 * i + which]))
    for copy in copies:
        copy.start()
    for i in range(count):
        q = q_ref[:, i].reshape(requests * heads, lat)
        copies[2 * i].wait()
        copies[2 * i + 1].wait()
        result = attend(q, new_ref[i], keys[i], limit_ref[i], heads)
        out_ref[:, i] = result.reshape(requests, heads, lat)


def last_decode_kernel(q_ref, new_ref, limit_ref, pages_ref, carried_ref, out_ref):
    requests, count, heads, lat = q_ref.shape
    for i in range(count):
        q = q_ref[:, i].reshape(requests * heads, lat)
        at = 2 * i * lat
        pages = pages_ref[:, :, at : at + 2 * lat].astype(f32).reshape(PAGE, 2 * lat)
        keys = jnp.concatenate([pages[:, :lat], pages[:, lat:]], axis=0).astype(bf16)
        result = attend(q, new_ref[i], keys, limit_ref[i], heads)
        out_ref[:, i] = result.reshape(requests, heads, lat)


def decode_pair(layer, slots, queries, new, limit, pages, carried, last=False):
    requests, _, heads, lat = queries.shape
    half = layer // 2
    in_specs = [
        pl.BlockSpec((requests, 2, heads, lat), lambda i, *s: (0, half, 0, 0)),
        pl.BlockSpec((2, requests, lat), lambda i, *s: (half, 0, 0)),
        pl.BlockSpec((2, requests * heads, 1), lambda i, *s: (half, 0, 0)),
        whole(pages.shape) if last else in_hbm,
    ]
    scalars = [] if last else [slots]
    operands = scalars + [queries, new, limit, pages if last else held_in_hbm(pages)]
    aliases = {}
    if carried is not None:
        in_specs.append(in_hbm)
        aliases = {len(operands): 0}
        operands.append(carried)
    scratch = [pltpu.VMEM((2, 2 * PAGE, lat), bf16), pltpu.SemaphoreType.DMA((4,))]
    return pl.pallas_call(
        last_decode_kernel if last else functools.partial(decode_kernel, layer),
        grid_spec=pltpu.PrefetchScalarGridSpec(
            num_scalar_prefetch=len(scalars),
            grid=(1,),
            in_specs=in_specs,
            out_specs=pl.BlockSpec((requests, 2, heads, lat), lambda i, *s: (0, half, 0, 0)),
            scratch_shapes=[] if last else scratch,
        ),
        out_shape=jax.ShapeDtypeStruct(queries.shape, bf16),
        input_output_aliases=aliases,
        compiler_params=params,
        cost_estimate=pl.CostEstimate(
            flops=2 * 4 * requests * heads * 2 * PAGE * lat,
            bytes_accessed=2 * 2 * (2 * requests * heads + 2 * PAGE) * lat,
            transcendentals=2 * requests * heads * 2 * PAGE,
        ),
    )(*operands)


def shards(
    prompt_states, norm_gain, w_latent, w_back, page_lists, queries, new_latent, context_lengths
):
    segments = lax.axis_size("segment")
    wide = lax.axis_size("wide")
    position = lax.axis_index("segment")
    core = position & 1
    batches, tok_rows, local_width = prompt_states.shape
    width = local_width * wide
    tokens = batches * tok_rows
    mine = tokens // segments
    share = mine // wide
    layers = segments
    lat = w_latent.shape[2]
    where = jnp.stack([position, core]).astype(jnp.int32)

    def array(*shape):
        return jax.ShapeDtypeStruct(shape, bf16)

    def near(*shape):
        return pltpu.VMEM(shape, bf16)

    def far(*shape):
        return pltpu.HBM(shape, bf16)

    size = (2, local_width, lat)
    both, mine_lent = call(
        weights_kernel,
        [in_hbm] * 3,
        [in_hbm, whole(size[1:])],
        [far(*size), near(*size[1:])],
        [held_in_hbm(w_latent), held_in_hbm(norm_gain), held_in_hbm(w_back)],
        [where],
        [
            pltpu.VMEM(size[1:], bf16),
            pltpu.VMEM(norm_gain.shape, bf16),
            pltpu.VMEM(size, bf16),
            pltpu.SemaphoreType.DMA((7,)),
        ],
    )
    every = lax.all_gather(both, "segment", axis=0)
    lent = lax.ppermute(mine_lent, "segment", [(i, i + 1) for i in range(0, segments, 2)])

    states = prompt_states.reshape(segments // 2, 2, mine, local_width)
    groups = segments // 2
    own_states = pl.BlockSpec((1, 1, mine, local_width), lambda i, s: (s[0] >> 1, s[1], 0, 0))
    home = call(
        home_kernel,
        [whole(states.shape), whole(size[1:]), whole(size[1:])],
        [whole((mine, lat))] * groups,
        [near(mine, lat)] * groups,
        [in_vmem(states), in_vmem(mine_lent), lent],
        [where],
        flops=2 * local_width**3,
    )
    (cross,) = call(
        cross_kernel,
        [whole(size), whole(size[1:])],
        [whole((lat, lat))],
        [near(lat, lat)],
        [both, lent],
        [where],
        flops=2 * local_width**3,
    )
    taken = [
        lax.ppermute(home[hop], "segment", [(0, 2 * hop), (1, 2 * hop + 1)])
        for hop in range(1, groups)
    ]
    high = lat // wide
    columns = LANES + lat + high // share * lat
    (sent,) = call(
        home_send_kernel,
        [whole((mine, lat))] * groups + [whole((lat, lat)), own_states],
        [whole((wide, share, columns))],
        [array(wide, share, columns)],
        [home[0]] + taken + [cross, states],
        [where],
    )
    got = exchanged(sent, "wide")
    (sent,) = call(
        functools.partial(home_sum_kernel, width),
        [whole(got.shape)],
        [whole((wide, high + share, lat))],
        [array(wide, high + share, lat)],
        [got],
    )
    def resident(source, *lists):
        parts = source.reshape((-1,) + source.shape[-2:])
        count = sum(len(slots) for slots in lists)
        return pl.pallas_call(
            functools.partial(reside_kernel, lists),
            in_specs=[in_hbm],
            out_specs=[pl.BlockSpec(memory_space=pltpu.VMEM)] * len(lists),
            out_shape=[pltpu.VMEM((len(slots),) + parts.shape[1:], bf16) for slots in lists],
            scratch_shapes=[pltpu.SemaphoreType.DMA((count,))],
            compiler_params=params,
            cost_estimate=pl.CostEstimate(
                flops=0, bytes_accessed=2 * count * parts.shape[1] * lat, transcendentals=0
            ),
        )(held_in_hbm(parts))

    def resident_weights(before, following):
        backs = [2 * layer + 1 for layer in before]
        latents = [2 * layer for layer in following]
        if len(following) == 1:
            return resident(every, backs, latents)
        return resident(every, backs, latents, [2 * following[0] + 1])

    def tied(*values):
        return lax.optimization_barrier(values)

    def advance(before, following, got, state, weights, earlier=None):
        mode = "first" if before == (0,) else "later" if earlier is not None else "pair"
        count = len(following) + (len(following) == 2)
        shapes = [
            (array if mode == "first" else far)(wide, share, LANES + count * lat),
            near(mine, local_width),
            far(wide, high, lat) if mode == "first" else far(mine, 2 * lat),
        ]
        operands = [got, state] + [in_vmem(weight) for weight in weights]
        in_specs = [whole(got.shape), own_states if mode == "first" else whole(state.shape)]
        in_specs += [whole(weight.shape) for weight in weights]
        if mode == "later":
            in_specs.append(whole(earlier.shape))
            operands.append(earlier)
        return call(
            functools.partial(advance_kernel, before, following, mode),
            in_specs,
            [whole(s.shape) for s in shapes],
            shapes,
            operands,
            [where],
            flops=2 * (len(before) + count) * mine * lat * local_width,
        )

    def pair_step(got, crosses, copies):
        (sent,) = call(
            functools.partial(pair_kernel, width),
            [whole(got.shape), whole(crosses[0].shape)],
            [whole((copies, share, 2 * lat))],
            [array(copies, share, 2 * lat)],
            [got, in_vmem(crosses[0])],
            flops=2 * 2 * share * lat * lat,
        )
        return sent

    got, weights = tied(exchanged(sent, "wide"), resident_weights((0,), (1,)))

    earlier = got
    sent, state, cross = advance((0,), (1,), got, states, weights)
    crosses = lax.all_gather(cross.reshape(lat, lat), "segment", axis=0)
    got = exchanged(sent, "wide")
    (sent,) = call(
        functools.partial(single_kernel, width),
        [whole(got.shape)],
        [whole((wide, share, lat))],
        [array(wide, share, lat)],
        [got],
    )
    got, weights = tied(exchanged(sent, "wide"), resident_weights((1,), (2, 3)))

    pages = []
    for even in range(2, layers, 2):
        odd = even + 1
        before = (1,) if even == 2 else (even - 2, even - 1)
        extra = earlier if even == 2 else None
        sent, state, held = advance(before, (even, odd), got, state, weights, extra)
        pages.append(lax.all_gather(held, "segment", axis=0))
        if odd < layers - 1:
            following = resident_weights((even, odd), (even + 2, even + 3))
            mixing = resident(crosses, [even, odd])
            got, mixing, weights = tied(exchanged(sent, "wide"), mixing, following)
            got = exchanged(pair_step(got, mixing, wide), "wide")
        else:
            got, mixing = tied(exchanged(sent, "wide"), resident(crosses, [even, odd]))

    targets = page_lists[:, :, 0]
    owned = targets == position
    counts = jnp.sum(owned.astype(jnp.int32), axis=1)
    none = targets.shape[1]
    order = jnp.arange(none, dtype=jnp.int32)[None, :]
    slot0 = jnp.min(jnp.where(owned, order, none), axis=1)
    slot1 = jnp.min(jnp.where(owned & (order > slot0[:, None]), order, none), axis=1)
    slots = jnp.minimum(jnp.stack([slot0, slot1], axis=1), none - 1).reshape(-1)
    limit = jnp.minimum(context_lengths, counts[None, :] * PAGE)
    limit = jnp.repeat(limit.T, queries.shape[2], axis=1)[:, :, None]
    new = new_latent.transpose(1, 0, 2)

    def decode(layer, pages, carried, last=False):
        return decode_pair(layer, slots, queries, new, limit, pages, carried, last)

    out = decode(0, pages[0], None)
    got, out = lax.optimization_barrier((got, out))

    got = exchanged(pair_step(got, mixing, segments), "segment")
    (sent,) = call(
        functools.partial(choose_kernel, layers - 2),
        [whole(got.shape)],
        [whole((wide, share, 4 * lat))],
        [array(wide, share, 4 * lat)],
        [got],
        [slots],
    )
    got = exchanged(sent, "wide")
    out = decode(4, pages[2], decode(2, pages[1], out))
    got, out = lax.optimization_barrier((got, out))
    return decode(layers - 2, got, out, True)


def solution(mesh):
    in_specs = (
        P(None, None, "wide"),
        P("segment", "wide"),
        P("segment", "wide", None),
        P("segment", None, "wide"),
        P(),
        P("segment", None, "wide", None),
        P("segment", None, None),
        P("segment", None),
    )
    out_specs = P("segment", None, "wide", None)
    return jax.shard_map(shards, mesh=mesh, in_specs=in_specs, out_specs=out_specs, check_vma=False)
```

```python
import functools
import math

import jax
import jax.numpy as jnp
from jax import lax
from jax.experimental import pallas as pl
from jax.experimental.pallas import tpu as pltpu
from jax.sharding import PartitionSpec as P

PAGE = 128
LANES = 128

eps_norm = 1e-06
score_scale = 192.0 ** (-0.5)

params = pltpu.CompilerParams(vmem_limit_bytes=24 * 1024 * 1024)
in_hbm = pl.BlockSpec(memory_space=pltpu.HBM)
bf16 = jnp.bfloat16
f32 = jnp.float32


def dot(a, b):
    return jnp.dot(a, b, preferred_element_type=jnp.float32)


def dot_t(a, b):
    return lax.dot_general(a, b, (((1,), (1,)), ((), ())), preferred_element_type=jnp.float32)


def square_columns(values):
    squares = jnp.sum(values * values, axis=1, keepdims=True)
    high = squares.astype(bf16).astype(f32)
    column = lax.broadcasted_iota(jnp.int32, (values.shape[0], LANES), 1)
    return jnp.where(column == 0, high, jnp.where(column == 1, squares - high, 0.0))


def silu(latent):
    values = latent.astype(f32)
    return (values / (1.0 + jnp.exp(-values))).astype(bf16)


def exchanged(sent, axis):
    return lax.all_to_all(sent, axis, 0, 0, tiled=True)


def core_swap(x):
    length = lax.axis_size("segment")
    return lax.ppermute(x, "segment", [(i, i ^ 1) for i in range(length)])


def held_in_hbm(x):
    return pltpu.with_memory_space_constraint(x, pltpu.HBM)


def in_vmem(x):
    return pltpu.with_memory_space_constraint(x, pltpu.VMEM)


def whole(shape):
    return pl.BlockSpec(shape, lambda i, *s: (0,) * len(shape))


def call(body, in_specs, out_specs, out_shape, operands, scalars=(), scratch=(), flops=0):
    moved = sum(2 * math.prod(o.shape) for o in out_shape)
    return pl.pallas_call(
        body,
        grid_spec=pltpu.PrefetchScalarGridSpec(
            num_scalar_prefetch=len(scalars),
            grid=(1,),
            in_specs=in_specs,
            out_specs=out_specs,
            scratch_shapes=scratch,
        ),
        out_shape=out_shape,
        compiler_params=params,
        cost_estimate=pl.CostEstimate(flops=flops, bytes_accessed=2 * moved, transcendentals=0),
    )(*scalars, *operands)


def weights_kernel(where, latent_ref, gain_ref, back_ref, both_ref, lent_ref, *scratch):
    latent, gain, pair, sems = scratch
    size = latent.shape[0]
    half = size // 2
    halves = [pl.ds(i * half, half) for i in range(2)]
    copies = [
        pltpu.make_async_copy(gain_ref, gain, sems.at[0]),
        pltpu.make_async_copy(latent_ref.at[0, halves[0]], latent.at[halves[0]], sems.at[1]),
        pltpu.make_async_copy(latent_ref.at[0, halves[1]], latent.at[halves[1]], sems.at[2]),
        pltpu.make_async_copy(back_ref.at[0], pair.at[1], sems.at[3]),
    ]
    for copy in copies:
        copy.start()
    copies[0].wait()
    gains = jnp.broadcast_to(gain[...].astype(f32), (8, size)).T[:, :1]
    sending = []
    for i, rows in enumerate(halves):
        copies[1 + i].wait()
        scaled = latent[rows].astype(f32) * gains[i * half : (i + 1) * half]
        pair[0, rows] = scaled.astype(bf16)
        to = both_ref.at[0, rows]
        sending.append(pltpu.make_async_copy(pair.at[0, rows], to, sems.at[4 + i]))
        sending[i].start()
    copies[3].wait()
    sending.append(pltpu.make_async_copy(pair.at[1], both_ref.at[1], sems.at[6]))
    sending[2].start()

    @pl.when(where[0] == 0)
    def _():
        lent_ref[...] = pair[0]

    @pl.when(where[0] != 0)
    def _():
        lent_ref[...] = pair[1]

    for copy in sending:
        copy.wait()


def home_kernel(where, states_ref, mine_ref, lent_ref, *out_refs):
    groups, _, rows, width = states_ref.shape

    def products(weight_ref):
        tokens = states_ref[:, where[1]].reshape(groups * rows, width)
        product = dot(tokens, weight_ref[...]).astype(bf16)
        for group in range(groups):
            out_refs[group][...] = product[group * rows : (group + 1) * rows]

    @pl.when(where[0] == 0)
    def _():
        products(mine_ref)

    @pl.when(where[0] != 0)
    def _():
        products(lent_ref)


def cross_kernel(where, both_ref, lent_ref, out_ref):
    @pl.when(where[0] & 1 == 0)
    def _():
        out_ref[...] = dot_t(both_ref[1], both_ref[1]).astype(bf16)

    @pl.when(where[0] & 1 != 0)
    def _():
        out_ref[...] = dot(lent_ref[...], both_ref[0]).astype(bf16)


def home_send_kernel(
    where, home_ref, a_ref, b_ref, c_ref, cross_ref, states_ref, out_ref, state_ref
):
    wide, share, _ = out_ref.shape
    rows, lat = home_ref.shape
    taken = a_ref[...].astype(f32) + b_ref[...].astype(f32) + c_ref[...].astype(f32)
    product = jnp.where(where[0] < 2, home_ref[...].astype(f32), taken)
    state = states_ref[where[0] >> 1, where[1]]
    state_ref[...] = state
    squares = square_columns(state.astype(f32))
    out_ref[:, :, :LANES] = squares.reshape(wide, share, LANES).astype(bf16)
    out_ref[:, :, LANES : LANES + lat] = product.reshape(wide, share, lat).astype(bf16)
    parts = cross_ref.shape[0] // rows
    cross = cross_ref[...].astype(f32).reshape(wide, parts, share, lat)
    for part in range(parts):
        at = LANES + (1 + part) * lat
        out_ref[:, :, at : at + lat] = cross[:, part].astype(bf16)


def home_sum_kernel(width, got_ref, out_ref):
    wide, high, lat = out_ref.shape
    summed = jnp.sum(got_ref[...].astype(f32), axis=0)
    squares = summed[:, 0:1] + summed[:, 1:2]
    latent = summed[:, LANES : LANES + lat] * lax.rsqrt(squares / width + eps_norm)
    parts = [summed[:, at : at + lat] for at in range(LANES + lat, summed.shape[1], lat)]
    block = jnp.concatenate(parts + [latent], axis=0).astype(bf16)
    for place in range(wide):
        out_ref[place] = block


def single_kernel(width, got_ref, out_ref):
    summed = jnp.sum(got_ref[...].astype(f32), axis=0)
    squares = summed[:, 0:1] + summed[:, 1:2]
    latent = (summed[:, LANES:] * lax.rsqrt(squares / width + eps_norm)).astype(bf16)
    for place in range(out_ref.shape[0]):
        out_ref[place] = latent


def chain(width, summed, gram, mixing):
    lat = (summed.shape[1] - LANES) // 3
    squares = summed[:, 0:1] + summed[:, 1:2]
    at = [LANES + i * lat for i in range(4)]
    first = (summed[:, at[0] : at[1]] * lax.rsqrt(squares / width + eps_norm)).astype(bf16)
    activated = silu(first)
    towards = 2.0 * summed[:, at[2] : at[3]] + dot(activated, gram())
    squares = squares + jnp.sum(activated.astype(f32) * towards, axis=1, keepdims=True)
    squares = jnp.maximum(squares, 0.0)
    second = summed[:, at[1] : at[2]] + dot(activated, mixing())
    second = (second * lax.rsqrt(squares / width + eps_norm)).astype(bf16)
    return first, second


def reside_kernel(lists, source_ref, *rest):
    out_refs, sems = rest[:-1], rest[-1]
    copies = []
    for out_ref, slots in zip(out_refs, lists):
        for i, slot in enumerate(slots):
            sem = sems.at[len(copies)]
            copies.append(pltpu.make_async_copy(source_ref.at[slot], out_ref.at[i], sem))
    for copy in copies:
        copy.start()
    for copy in copies:
        copy.wait()


def advance_kernel(before, layers, mode, got_ref, states_ref, *rest):
    refs = rest[: 1 + len(layers)]
    back_ref, latent_ref = refs[:2]
    outs = rest[len(refs) :]
    if mode == "later":
        earlier_ref, outs = outs[0], outs[1:]
    out_ref, state_ref, held_ref = outs[:3]
    wide, share, _ = out_ref.shape
    rows = wide * share
    lat = back_ref.shape[2]

    def latents_of(ref):
        block = ref[:, ref.shape[1] - share :]
        return block.astype(f32).reshape(rows, ref.shape[2])

    latents = latents_of(got_ref)
    activated = silu(latents)
    state = states_ref[...].astype(f32)
    for i in range(len(before)):
        state = state + dot(activated[:, i * lat : (i + 1) * lat], back_ref[i])
    state = state.astype(bf16)
    state_ref[...] = state
    squares = square_columns(state.astype(f32))
    out_ref[:, :, :LANES] = squares.reshape(wide, share, LANES).astype(bf16)
    products = [dot(state, latent_ref[i]) for i in range(len(layers))]
    if len(layers) == 2:
        products.append(dot_t(state, refs[2][0]))
    for i, product in enumerate(products):
        at = LANES + i * lat
        out_ref[:, :, at : at + lat] = product.reshape(wide, share, lat).astype(bf16)
    if mode == "first":
        held_ref[...] = got_ref[:, : got_ref.shape[1] - share]
    elif mode == "later":
        held_ref[:, :lat] = latents_of(earlier_ref).astype(bf16)
        held_ref[:, lat:] = latents.astype(bf16)
    else:
        held_ref[...] = latents.astype(bf16)


def pair_kernel(width, got_ref, cross_ref, out_ref):
    summed = jnp.sum(got_ref[...].astype(f32), axis=0)
    first, second = chain(width, summed, lambda: cross_ref[0], lambda: cross_ref[1])
    lat = first.shape[1]
    for place in range(out_ref.shape[0]):
        out_ref[place, :, :lat] = first
        out_ref[place, :, lat:] = second


def choose_kernel(got_ref, hot_ref, out_ref):
    pages = got_ref.shape[0]
    lat = got_ref.shape[2] // 2
    parts = []
    for i in range(2):
        for which in range(2):
            at = (2 * i + which) * pages
            part = jnp.zeros((got_ref.shape[1], lat), f32)
            for page in range(pages):
                shard = got_ref[page, :, i * lat : (i + 1) * lat].astype(f32)
                part = jnp.where(hot_ref[at + page : at + page + 1, :1] > 0, shard, part)
            parts.append(part.astype(bf16))
    for place in range(out_ref.shape[0]):
        for i, part in enumerate(parts):
            out_ref[place, :, i * lat : (i + 1) * lat] = part


def attend(q, new, keys, limit, heads):
    rows = q.shape[0]
    requests = new.shape[0]
    row = lax.broadcasted_iota(jnp.int32, (rows, requests), 0)
    start = lax.broadcasted_iota(jnp.int32, (rows, requests), 1) * heads
    pick = jnp.where((row >= start) & (row < start + heads), 1.0, 0.0).astype(bf16)
    own = dot(pick, new)
    scores = dot_t(q, keys) * score_scale
    place = lax.broadcasted_iota(jnp.int32, scores.shape, 1)
    scores = jnp.where(place < limit, scores, -jnp.inf)
    own_score = jnp.sum(q.astype(f32) * own, axis=1, keepdims=True) * score_scale
    top = jnp.maximum(jnp.max(scores, axis=1, keepdims=True), own_score)
    weights = jnp.exp(scores - top)
    own_weight = jnp.exp(own_score - top)
    total = jnp.sum(weights, axis=1, keepdims=True) + own_weight
    numer = dot(weights.astype(bf16), keys) + own_weight * own
    return (numer / total).astype(bf16)


def decode_kernel(layer, slots, q_ref, new_ref, limit_ref, pages_ref, *rest):
    out_ref, keys, sems = rest[-3:]
    requests, count, heads, lat = q_ref.shape
    copies = []
    for i in range(count):
        for which in range(2):
            page = pages_ref.at[slots[2 * (layer + i) + which], :, pl.ds(i * lat, lat)]
            at = keys.at[i, pl.ds(which * PAGE, PAGE)]
            copies.append(pltpu.make_async_copy(page, at, sems.at[2 * i + which]))
    for copy in copies:
        copy.start()
    for i in range(count):
        q = q_ref[:, i].reshape(requests * heads, lat)
        copies[2 * i].wait()
        copies[2 * i + 1].wait()
        result = attend(q, new_ref[i], keys[i], limit_ref[i], heads)
        out_ref[:, i] = result.reshape(requests, heads, lat)


def last_decode_kernel(layer, q_ref, new_ref, limit_ref, pages_ref, carried_ref, out_ref):
    requests, count, heads, lat = out_ref.shape
    for i in range(count):
        q = q_ref[:, layer + i].reshape(requests * heads, lat)
        at = 2 * i * lat
        pages = pages_ref[:, :, at : at + 2 * lat].astype(f32).reshape(PAGE, 2 * lat)
        keys = jnp.concatenate([pages[:, :lat], pages[:, lat:]], axis=0).astype(bf16)
        result = attend(q, new_ref[layer + i], keys, limit_ref[layer + i], heads)
        out_ref[:, i] = result.reshape(requests, heads, lat)


def decode_pair(layer, slots, queries, new, limit, pages, carried, last=False):
    requests, _, heads, lat = queries.shape
    half = layer // 2
    in_specs = [
        pl.BlockSpec((requests, 2, heads, lat), lambda i, *s: (0, half, 0, 0)),
        pl.BlockSpec((2, requests, lat), lambda i, *s: (half, 0, 0)),
        pl.BlockSpec((2, requests * heads, 1), lambda i, *s: (half, 0, 0)),
        whole(pages.shape) if last else in_hbm,
    ]
    scalars = [] if last else [slots]
    operands = scalars + [queries, new, limit, pages if last else held_in_hbm(pages)]
    if last:
        in_specs[:3] = [whole(operand.shape) for operand in operands[:3]]
        operands[:3] = [in_vmem(operand) for operand in operands[:3]]
    aliases = {}
    if carried is not None:
        in_specs.append(in_hbm)
        aliases = {len(operands): 0}
        operands.append(carried)
    scratch = [pltpu.VMEM((2, 2 * PAGE, lat), bf16), pltpu.SemaphoreType.DMA((4,))]
    return pl.pallas_call(
        functools.partial(last_decode_kernel if last else decode_kernel, layer),
        grid_spec=pltpu.PrefetchScalarGridSpec(
            num_scalar_prefetch=len(scalars),
            grid=(1,),
            in_specs=in_specs,
            out_specs=pl.BlockSpec((requests, 2, heads, lat), lambda i, *s: (0, half, 0, 0)),
            scratch_shapes=[] if last else scratch,
        ),
        out_shape=jax.ShapeDtypeStruct(queries.shape, bf16),
        input_output_aliases=aliases,
        compiler_params=params,
        cost_estimate=pl.CostEstimate(
            flops=2 * 4 * requests * heads * 2 * PAGE * lat,
            bytes_accessed=2 * 2 * (2 * requests * heads + 2 * PAGE) * lat,
            transcendentals=2 * requests * heads * 2 * PAGE,
        ),
    )(*operands)


def shards(
    prompt_states, norm_gain, w_latent, w_back, page_lists, queries, new_latent, context_lengths
):
    segments = lax.axis_size("segment")
    wide = lax.axis_size("wide")
    position = lax.axis_index("segment")
    core = position & 1
    batches, tok_rows, local_width = prompt_states.shape
    width = local_width * wide
    tokens = batches * tok_rows
    mine = tokens // segments
    share = mine // wide
    layers = segments
    lat = w_latent.shape[2]
    where = jnp.stack([position, core]).astype(jnp.int32)

    def array(*shape):
        return jax.ShapeDtypeStruct(shape, bf16)

    def near(*shape):
        return pltpu.VMEM(shape, bf16)

    def far(*shape):
        return pltpu.HBM(shape, bf16)

    size = (2, local_width, lat)
    both, mine_lent = call(
        weights_kernel,
        [in_hbm] * 3,
        [in_hbm, whole(size[1:])],
        [far(*size), near(*size[1:])],
        [held_in_hbm(w_latent), held_in_hbm(norm_gain), held_in_hbm(w_back)],
        [where],
        [
            pltpu.VMEM(size[1:], bf16),
            pltpu.VMEM(norm_gain.shape, bf16),
            pltpu.VMEM(size, bf16),
            pltpu.SemaphoreType.DMA((7,)),
        ],
    )
    every = lax.all_gather(both, "segment", axis=0)
    lent = lax.ppermute(mine_lent, "segment", [(i, i + 1) for i in range(0, segments, 2)])

    states = prompt_states.reshape(segments // 2, 2, mine, local_width)
    groups = segments // 2
    home = call(
        home_kernel,
        [whole(states.shape), whole(size[1:]), whole(size[1:])],
        [whole((mine, lat))] * groups,
        [near(mine, lat)] * groups,
        [in_vmem(states), in_vmem(mine_lent), lent],
        [where],
        flops=2 * local_width**3,
    )
    (cross,) = call(
        cross_kernel,
        [whole(size), whole(size[1:])],
        [whole((lat, lat))],
        [near(lat, lat)],
        [both, lent],
        [where],
        flops=2 * local_width**3,
    )
    taken = [
        lax.ppermute(home[hop], "segment", [(0, 2 * hop), (1, 2 * hop + 1)])
        for hop in range(1, groups)
    ]
    high = lat // wide
    columns = LANES + lat + high // share * lat
    sent, state = call(
        home_send_kernel,
        [whole((mine, lat))] * groups + [whole((lat, lat)), whole(states.shape)],
        [whole((wide, share, columns)), whole((mine, local_width))],
        [array(wide, share, columns), near(mine, local_width)],
        [home[0]] + taken + [cross, in_vmem(states)],
        [where],
    )
    got = exchanged(sent, "wide")
    (sent,) = call(
        functools.partial(home_sum_kernel, width),
        [whole(got.shape)],
        [whole((wide, high + share, lat))],
        [array(wide, high + share, lat)],
        [got],
    )
    def resident(source, *lists):
        parts = source.reshape((-1,) + source.shape[-2:])
        count = sum(len(slots) for slots in lists)
        return pl.pallas_call(
            functools.partial(reside_kernel, lists),
            in_specs=[in_hbm],
            out_specs=[pl.BlockSpec(memory_space=pltpu.VMEM)] * len(lists),
            out_shape=[pltpu.VMEM((len(slots),) + parts.shape[1:], bf16) for slots in lists],
            scratch_shapes=[pltpu.SemaphoreType.DMA((count,))],
            compiler_params=params,
            cost_estimate=pl.CostEstimate(
                flops=0, bytes_accessed=2 * count * parts.shape[1] * lat, transcendentals=0
            ),
        )(held_in_hbm(parts))

    def resident_weights(before, following):
        backs = [2 * layer + 1 for layer in before]
        latents = [2 * layer for layer in following]
        if len(following) == 1:
            return resident(every, backs, latents)
        return resident(every, backs, latents, [2 * following[0] + 1])

    def tied(*values):
        return lax.optimization_barrier(values)

    def advance(before, following, got, state, weights, earlier=None):
        mode = "first" if before == (0,) else "later" if earlier is not None else "pair"
        count = len(following) + (len(following) == 2)
        shapes = [
            (array if mode == "first" else far)(wide, share, LANES + count * lat),
            near(mine, local_width),
            far(wide, high, lat) if mode == "first" else far(mine, 2 * lat),
        ]
        operands = [got, state] + [in_vmem(weight) for weight in weights]
        in_specs = [whole(got.shape), whole(state.shape)]
        in_specs += [whole(weight.shape) for weight in weights]
        if mode == "later":
            in_specs.append(whole(earlier.shape))
            operands.append(earlier)
        return call(
            functools.partial(advance_kernel, before, following, mode),
            in_specs,
            [whole(s.shape) for s in shapes],
            shapes,
            operands,
            flops=2 * (len(before) + count) * mine * lat * local_width,
        )

    def pair_step(got, crosses, copies):
        (sent,) = call(
            functools.partial(pair_kernel, width),
            [whole(got.shape), whole(crosses[0].shape)],
            [whole((copies, share, 2 * lat))],
            [array(copies, share, 2 * lat)],
            [got, in_vmem(crosses[0])],
            flops=2 * 2 * share * lat * lat,
        )
        return sent

    got, weights = tied(exchanged(sent, "wide"), resident_weights((0,), (1,)))

    earlier = got
    sent, state, cross = advance((0,), (1,), got, state, weights)
    crosses = lax.all_gather(cross.reshape(lat, lat), "segment", axis=0)
    got = exchanged(sent, "wide")
    (sent,) = call(
        functools.partial(single_kernel, width),
        [whole(got.shape)],
        [whole((wide, share, lat))],
        [array(wide, share, lat)],
        [got],
    )
    got, weights = tied(exchanged(sent, "wide"), resident_weights((1,), (2, 3)))

    pages = []
    for even in range(2, layers, 2):
        odd = even + 1
        before = (1,) if even == 2 else (even - 2, even - 1)
        extra = earlier if even == 2 else None
        sent, state, held = advance(before, (even, odd), got, state, weights, extra)
        pages.append(lax.all_gather(held, "segment", axis=0))
        if odd < layers - 1:
            following = resident_weights((even, odd), (even + 2, even + 3))
            mixing = resident(crosses, [even, odd])
            got, mixing, weights = tied(exchanged(sent, "wide"), mixing, following)
            got = exchanged(pair_step(got, mixing, wide), "wide")
        else:
            got, mixing = tied(exchanged(sent, "wide"), resident(crosses, [even, odd]))

    targets = page_lists[:, :, 0]
    owned = targets == position
    counts = jnp.sum(owned.astype(jnp.int32), axis=1)
    none = targets.shape[1]
    order = jnp.arange(none, dtype=jnp.int32)[None, :]
    slot0 = jnp.min(jnp.where(owned, order, none), axis=1)
    slot1 = jnp.min(jnp.where(owned & (order > slot0[:, None]), order, none), axis=1)
    slots = jnp.minimum(jnp.stack([slot0, slot1], axis=1), none - 1).reshape(-1)
    limit = jnp.minimum(context_lengths, counts[None, :] * PAGE)
    limit = jnp.repeat(limit.T, queries.shape[2], axis=1)[:, :, None]
    new = new_latent.transpose(1, 0, 2)
    hot = slots[2 * layers - 4 :, None] == jnp.arange(none, dtype=jnp.int32)[None, :]
    hot = jnp.broadcast_to(hot.astype(f32).reshape(4 * none, 1), (4 * none, LANES))

    def decode(layer, pages, carried, last=False):
        return decode_pair(layer, slots, queries, new, limit, pages, carried, last)

    out = decode(0, pages[0], None)
    got, out, hot = lax.optimization_barrier((got, out, in_vmem(hot)))

    got = exchanged(pair_step(got, mixing, segments), "segment")
    (sent,) = call(
        choose_kernel,
        [whole(got.shape), whole(hot.shape)],
        [whole((wide, share, 4 * lat))],
        [array(wide, share, 4 * lat)],
        [got, hot],
    )
    got = exchanged(sent, "wide")
    out = decode(4, pages[2], decode(2, pages[1], out))
    got, out = lax.optimization_barrier((got, out))
    return decode(layers - 2, got, out, True)


def solution(mesh):
    in_specs = (
        P(None, None, "wide"),
        P("segment", "wide"),
        P("segment", "wide", None),
        P("segment", None, "wide"),
        P(),
        P("segment", None, "wide", None),
        P("segment", None, None),
        P("segment", None),
    )
    out_specs = P("segment", None, "wide", None)
    return jax.shard_map(shards, mesh=mesh, in_specs=in_specs, out_specs=out_specs, check_vma=False)
```

```python
import functools
import math

import jax
import jax.numpy as jnp
from jax import lax
from jax.experimental import pallas as pl
from jax.experimental.pallas import tpu as pltpu
from jax.sharding import PartitionSpec as P

PAGE = 128
LANES = 128

eps_norm = 1e-06
score_scale = 192.0 ** (-0.5)

params = pltpu.CompilerParams(vmem_limit_bytes=24 * 1024 * 1024)
in_hbm = pl.BlockSpec(memory_space=pltpu.HBM)
bf16 = jnp.bfloat16
f32 = jnp.float32


def dot(a, b):
    return jnp.dot(a, b, preferred_element_type=jnp.float32)


def dot_t(a, b):
    return lax.dot_general(a, b, (((1,), (1,)), ((), ())), preferred_element_type=jnp.float32)


def square_columns(values):
    squares = jnp.sum(values * values, axis=1, keepdims=True)
    high = squares.astype(bf16).astype(f32)
    column = lax.broadcasted_iota(jnp.int32, (values.shape[0], LANES), 1)
    return jnp.where(column == 0, high, jnp.where(column == 1, squares - high, 0.0))


def silu(latent):
    values = latent.astype(f32)
    return (values / (1.0 + jnp.exp(-values))).astype(bf16)


def exchanged(sent, axis):
    return lax.all_to_all(sent, axis, 0, 0, tiled=True)


def core_swap(x):
    length = lax.axis_size("segment")
    return lax.ppermute(x, "segment", [(i, i ^ 1) for i in range(length)])


def held_in_hbm(x):
    return pltpu.with_memory_space_constraint(x, pltpu.HBM)


def in_vmem(x):
    return pltpu.with_memory_space_constraint(x, pltpu.VMEM)


def whole(shape):
    return pl.BlockSpec(shape, lambda i, *s: (0,) * len(shape))


def call(body, in_specs, out_specs, out_shape, operands, scalars=(), scratch=(), flops=0):
    moved = sum(2 * math.prod(o.shape) for o in out_shape)
    return pl.pallas_call(
        body,
        grid_spec=pltpu.PrefetchScalarGridSpec(
            num_scalar_prefetch=len(scalars),
            grid=(1,),
            in_specs=in_specs,
            out_specs=out_specs,
            scratch_shapes=scratch,
        ),
        out_shape=out_shape,
        compiler_params=params,
        cost_estimate=pl.CostEstimate(flops=flops, bytes_accessed=2 * moved, transcendentals=0),
    )(*scalars, *operands)


def weights_kernel(where, latent_ref, gain_ref, back_ref, both_ref, lent_ref, *scratch):
    latent, gain, pair, sems = scratch
    size = latent.shape[0]
    half = size // 2
    halves = [pl.ds(i * half, half) for i in range(2)]
    copies = [
        pltpu.make_async_copy(gain_ref, gain, sems.at[0]),
        pltpu.make_async_copy(latent_ref.at[0, halves[0]], latent.at[halves[0]], sems.at[1]),
        pltpu.make_async_copy(latent_ref.at[0, halves[1]], latent.at[halves[1]], sems.at[2]),
        pltpu.make_async_copy(back_ref.at[0], pair.at[1], sems.at[3]),
    ]
    for copy in copies:
        copy.start()
    copies[0].wait()
    gains = jnp.broadcast_to(gain[...].astype(f32), (8, size)).T[:, :1]
    sending = []
    for i, rows in enumerate(halves):
        copies[1 + i].wait()
        scaled = latent[rows].astype(f32) * gains[i * half : (i + 1) * half]
        pair[0, rows] = scaled.astype(bf16)
        to = both_ref.at[0, rows]
        sending.append(pltpu.make_async_copy(pair.at[0, rows], to, sems.at[4 + i]))
        sending[i].start()
    copies[3].wait()
    sending.append(pltpu.make_async_copy(pair.at[1], both_ref.at[1], sems.at[6]))
    sending[2].start()

    @pl.when(where[0] == 0)
    def _():
        lent_ref[...] = pair[0]

    @pl.when(where[0] != 0)
    def _():
        lent_ref[...] = pair[1]

    for copy in sending:
        copy.wait()


def home_kernel(where, states_ref, mine_ref, lent_ref, *out_refs):
    groups, _, rows, width = states_ref.shape

    def products(weight_ref):
        tokens = states_ref[:, where[1]].reshape(groups * rows, width)
        product = dot(tokens, weight_ref[...]).astype(bf16)
        for group in range(groups):
            out_refs[group][...] = product[group * rows : (group + 1) * rows]

    @pl.when(where[0] == 0)
    def _():
        products(mine_ref)

    @pl.when(where[0] != 0)
    def _():
        products(lent_ref)


def cross_kernel(where, both_ref, lent_ref, out_ref):
    @pl.when(where[0] & 1 == 0)
    def _():
        out_ref[...] = dot_t(both_ref[1], both_ref[1]).astype(bf16)

    @pl.when(where[0] & 1 != 0)
    def _():
        out_ref[...] = dot(lent_ref[...], both_ref[0]).astype(bf16)


def home_send_kernel(
    where, home_ref, a_ref, b_ref, c_ref, cross_ref, states_ref, out_ref, state_ref
):
    wide, share, _ = out_ref.shape
    rows, lat = home_ref.shape
    taken = a_ref[...].astype(f32) + b_ref[...].astype(f32) + c_ref[...].astype(f32)
    product = jnp.where(where[0] < 2, home_ref[...].astype(f32), taken)
    state = states_ref[where[0] >> 1, where[1]]
    state_ref[...] = state
    squares = square_columns(state.astype(f32))
    out_ref[:, :, :LANES] = squares.reshape(wide, share, LANES).astype(bf16)
    out_ref[:, :, LANES : LANES + lat] = product.reshape(wide, share, lat).astype(bf16)
    parts = cross_ref.shape[0] // rows
    cross = cross_ref[...].astype(f32).reshape(wide, parts, share, lat)
    for part in range(parts):
        at = LANES + (1 + part) * lat
        out_ref[:, :, at : at + lat] = cross[:, part].astype(bf16)


def home_sum_kernel(width, got_ref, out_ref):
    wide, high, lat = out_ref.shape
    summed = jnp.sum(got_ref[...].astype(f32), axis=0)
    squares = summed[:, 0:1] + summed[:, 1:2]
    latent = summed[:, LANES : LANES + lat] * lax.rsqrt(squares / width + eps_norm)
    parts = [summed[:, at : at + lat] for at in range(LANES + lat, summed.shape[1], lat)]
    block = jnp.concatenate(parts + [latent], axis=0).astype(bf16)
    for place in range(wide):
        out_ref[place] = block


def single_kernel(width, got_ref, out_ref):
    summed = jnp.sum(got_ref[...].astype(f32), axis=0)
    squares = summed[:, 0:1] + summed[:, 1:2]
    latent = (summed[:, LANES:] * lax.rsqrt(squares / width + eps_norm)).astype(bf16)
    for place in range(out_ref.shape[0]):
        out_ref[place] = latent


def chain(width, summed, gram, mixing):
    lat = (summed.shape[1] - LANES) // 3
    squares = summed[:, 0:1] + summed[:, 1:2]
    at = [LANES + i * lat for i in range(4)]
    first = (summed[:, at[0] : at[1]] * lax.rsqrt(squares / width + eps_norm)).astype(bf16)
    activated = silu(first)
    towards = 2.0 * summed[:, at[2] : at[3]] + dot(activated, gram())
    squares = squares + jnp.sum(activated.astype(f32) * towards, axis=1, keepdims=True)
    squares = jnp.maximum(squares, 0.0)
    second = summed[:, at[1] : at[2]] + dot(activated, mixing())
    second = (second * lax.rsqrt(squares / width + eps_norm)).astype(bf16)
    return first, second


def reside_kernel(lists, source_ref, *rest):
    out_refs, sems = rest[:-1], rest[-1]
    copies = []
    for out_ref, slots in zip(out_refs, lists):
        for i, slot in enumerate(slots):
            sem = sems.at[len(copies)]
            copies.append(pltpu.make_async_copy(source_ref.at[slot], out_ref.at[i], sem))
    for copy in copies:
        copy.start()
    for copy in copies:
        copy.wait()


def advance_kernel(before, layers, mode, got_ref, states_ref, *rest):
    refs = rest[: 1 + len(layers)]
    back_ref, latent_ref = refs[:2]
    outs = rest[len(refs) :]
    if mode == "later":
        earlier_ref, outs = outs[0], outs[1:]
    out_ref, state_ref, held_ref = outs[:3]
    wide, share, _ = out_ref.shape
    rows = wide * share
    lat = back_ref.shape[2]

    def latents_of(ref):
        block = ref[:, ref.shape[1] - share :]
        return block.astype(f32).reshape(rows, ref.shape[2])

    latents = latents_of(got_ref)
    activated = silu(latents)
    state = states_ref[...].astype(f32)
    for i in range(len(before)):
        state = state + dot(activated[:, i * lat : (i + 1) * lat], back_ref[i])
    state = state.astype(bf16)
    state_ref[...] = state
    squares = square_columns(state.astype(f32))
    out_ref[:, :, :LANES] = squares.reshape(wide, share, LANES).astype(bf16)
    products = [dot(state, latent_ref[i]) for i in range(len(layers))]
    if len(layers) == 2:
        products.append(dot_t(state, refs[2][0]))
    for i, product in enumerate(products):
        at = LANES + i * lat
        out_ref[:, :, at : at + lat] = product.reshape(wide, share, lat).astype(bf16)
    if mode == "first":
        held_ref[...] = got_ref[:, : got_ref.shape[1] - share]
    elif mode == "later":
        held_ref[:, :lat] = latents_of(earlier_ref).astype(bf16)
        held_ref[:, lat:] = latents.astype(bf16)
    else:
        held_ref[...] = latents.astype(bf16)


def pair_kernel(width, got_ref, cross_ref, out_ref):
    summed = jnp.sum(got_ref[...].astype(f32), axis=0)
    first, second = chain(width, summed, lambda: cross_ref[0], lambda: cross_ref[1])
    lat = first.shape[1]
    for place in range(out_ref.shape[0]):
        out_ref[place, :, :lat] = first
        out_ref[place, :, lat:] = second


def choose_kernel(got_ref, hot_ref, out_ref):
    pages = got_ref.shape[0]
    lat = got_ref.shape[2] // 2
    parts = []
    for i in range(2):
        for which in range(2):
            at = (2 * i + which) * pages
            part = jnp.zeros((got_ref.shape[1], lat), f32)
            for page in range(pages):
                shard = got_ref[page, :, i * lat : (i + 1) * lat].astype(f32)
                part = jnp.where(hot_ref[at + page : at + page + 1, :1] > 0, shard, part)
            parts.append(part.astype(bf16))
    for place in range(out_ref.shape[0]):
        for i, part in enumerate(parts):
            out_ref[place, :, i * lat : (i + 1) * lat] = part


def attend(q, new, keys, limit, heads):
    rows = q.shape[0]
    requests = new.shape[0]
    row = lax.broadcasted_iota(jnp.int32, (rows, requests), 0)
    start = lax.broadcasted_iota(jnp.int32, (rows, requests), 1) * heads
    pick = jnp.where((row >= start) & (row < start + heads), 1.0, 0.0).astype(bf16)
    own = dot(pick, new)
    scores = dot_t(q, keys) * score_scale
    place = lax.broadcasted_iota(jnp.int32, scores.shape, 1)
    scores = jnp.where(place < limit, scores, -jnp.inf)
    own_score = jnp.sum(q.astype(f32) * own, axis=1, keepdims=True) * score_scale
    top = jnp.maximum(jnp.max(scores, axis=1, keepdims=True), own_score)
    weights = jnp.exp(scores - top)
    own_weight = jnp.exp(own_score - top)
    total = jnp.sum(weights, axis=1, keepdims=True) + own_weight
    numer = dot(weights.astype(bf16), keys) + own_weight * own
    return (numer / total).astype(bf16)


def decode_kernel(layer, slots, q_ref, new_ref, limit_ref, pages_ref, *rest):
    out_ref, keys, sems = rest[-3:]
    requests, count, heads, lat = q_ref.shape
    copies = []
    for i in range(count):
        for which in range(2):
            page = pages_ref.at[slots[2 * (layer + i) + which], :, pl.ds(i * lat, lat)]
            at = keys.at[i, pl.ds(which * PAGE, PAGE)]
            copies.append(pltpu.make_async_copy(page, at, sems.at[2 * i + which]))
    for copy in copies:
        copy.start()
    for i in range(count):
        q = q_ref[:, i].reshape(requests * heads, lat)
        copies[2 * i].wait()
        copies[2 * i + 1].wait()
        result = attend(q, new_ref[i], keys[i], limit_ref[i], heads)
        out_ref[:, i] = result.reshape(requests, heads, lat)


def last_decode_kernel(layer, q_ref, new_ref, limit_ref, pages_ref, carried_ref, out_ref):
    requests, count, heads, lat = out_ref.shape
    for i in range(count):
        q = q_ref[:, layer + i].reshape(requests * heads, lat)
        at = 2 * i * lat
        pages = pages_ref[:, :, at : at + 2 * lat].astype(f32).reshape(PAGE, 2 * lat)
        keys = jnp.concatenate([pages[:, :lat], pages[:, lat:]], axis=0).astype(bf16)
        result = attend(q, new_ref[layer + i], keys, limit_ref[layer + i], heads)
        out_ref[:, i] = result.reshape(requests, heads, lat)


def decode_pair(layer, slots, queries, new, limit, pages, carried, last=False):
    requests, _, heads, lat = queries.shape
    half = layer // 2
    in_specs = [
        pl.BlockSpec((requests, 2, heads, lat), lambda i, *s: (0, half, 0, 0)),
        pl.BlockSpec((2, requests, lat), lambda i, *s: (half, 0, 0)),
        pl.BlockSpec((2, requests * heads, 1), lambda i, *s: (half, 0, 0)),
        whole(pages.shape) if last else in_hbm,
    ]
    scalars = [] if last else [slots]
    operands = scalars + [queries, new, limit, pages if last else held_in_hbm(pages)]
    if last:
        in_specs[:3] = [whole(operand.shape) for operand in operands[:3]]
        operands[:3] = [in_vmem(operand) for operand in operands[:3]]
    aliases = {}
    if carried is not None:
        in_specs.append(in_hbm)
        aliases = {len(operands): 0}
        operands.append(carried)
    scratch = [pltpu.VMEM((2, 2 * PAGE, lat), bf16), pltpu.SemaphoreType.DMA((4,))]
    return pl.pallas_call(
        functools.partial(last_decode_kernel if last else decode_kernel, layer),
        grid_spec=pltpu.PrefetchScalarGridSpec(
            num_scalar_prefetch=len(scalars),
            grid=(1,),
            in_specs=in_specs,
            out_specs=pl.BlockSpec((requests, 2, heads, lat), lambda i, *s: (0, half, 0, 0)),
            scratch_shapes=[] if last else scratch,
        ),
        out_shape=jax.ShapeDtypeStruct(queries.shape, bf16),
        input_output_aliases=aliases,
        compiler_params=params,
        cost_estimate=pl.CostEstimate(
            flops=2 * 4 * requests * heads * 2 * PAGE * lat,
            bytes_accessed=2 * 2 * (2 * requests * heads + 2 * PAGE) * lat,
            transcendentals=2 * requests * heads * 2 * PAGE,
        ),
    )(*operands)


def shards(
    prompt_states, norm_gain, w_latent, w_back, page_lists, queries, new_latent, context_lengths
):
    segments = lax.axis_size("segment")
    wide = lax.axis_size("wide")
    position = lax.axis_index("segment")
    core = position & 1
    batches, tok_rows, local_width = prompt_states.shape
    width = local_width * wide
    tokens = batches * tok_rows
    mine = tokens // segments
    share = mine // wide
    layers = segments
    lat = w_latent.shape[2]
    where = jnp.stack([position, core]).astype(jnp.int32)

    def array(*shape):
        return jax.ShapeDtypeStruct(shape, bf16)

    def near(*shape):
        return pltpu.VMEM(shape, bf16)

    def far(*shape):
        return pltpu.HBM(shape, bf16)

    size = (2, local_width, lat)
    both, mine_lent = call(
        weights_kernel,
        [in_hbm] * 3,
        [in_hbm, whole(size[1:])],
        [far(*size), near(*size[1:])],
        [held_in_hbm(w_latent), held_in_hbm(norm_gain), held_in_hbm(w_back)],
        [where],
        [
            pltpu.VMEM(size[1:], bf16),
            pltpu.VMEM(norm_gain.shape, bf16),
            pltpu.VMEM(size, bf16),
            pltpu.SemaphoreType.DMA((7,)),
        ],
    )
    every = lax.all_gather(both, "segment", axis=0)
    lent = lax.ppermute(mine_lent, "segment", [(i, i + 1) for i in range(0, segments, 2)])

    states = prompt_states.reshape(segments // 2, 2, mine, local_width)
    groups = segments // 2
    home = call(
        home_kernel,
        [whole(states.shape), whole(size[1:]), whole(size[1:])],
        [whole((mine, lat))] * groups,
        [near(mine, lat)] * groups,
        [in_vmem(states), in_vmem(mine_lent), lent],
        [where],
        flops=2 * local_width**3,
    )
    (cross,) = call(
        cross_kernel,
        [whole(size), whole(size[1:])],
        [whole((lat, lat))],
        [near(lat, lat)],
        [both, lent],
        [where],
        flops=2 * local_width**3,
    )
    taken = [
        lax.ppermute(home[hop], "segment", [(0, 2 * hop), (1, 2 * hop + 1)])
        for hop in range(1, groups)
    ]
    high = lat // wide
    columns = LANES + lat + high // share * lat
    sent, state = call(
        home_send_kernel,
        [whole((mine, lat))] * groups + [whole((lat, lat)), whole(states.shape)],
        [whole((wide, share, columns)), whole((mine, local_width))],
        [array(wide, share, columns), near(mine, local_width)],
        [home[0]] + taken + [cross, in_vmem(states)],
        [where],
    )
    got = exchanged(sent, "wide")
    (sent,) = call(
        functools.partial(home_sum_kernel, width),
        [whole(got.shape)],
        [whole((wide, high + share, lat))],
        [array(wide, high + share, lat)],
        [got],
    )
    def resident(source, *lists):
        parts = source.reshape((-1,) + source.shape[-2:])
        count = sum(len(slots) for slots in lists)
        return pl.pallas_call(
            functools.partial(reside_kernel, lists),
            in_specs=[in_hbm],
            out_specs=[pl.BlockSpec(memory_space=pltpu.VMEM)] * len(lists),
            out_shape=[pltpu.VMEM((len(slots),) + parts.shape[1:], bf16) for slots in lists],
            scratch_shapes=[pltpu.SemaphoreType.DMA((count,))],
            compiler_params=params,
            cost_estimate=pl.CostEstimate(
                flops=0, bytes_accessed=2 * count * parts.shape[1] * lat, transcendentals=0
            ),
        )(held_in_hbm(parts))

    def resident_weights(before, following):
        backs = [2 * layer + 1 for layer in before]
        latents = [2 * layer for layer in following]
        if len(following) == 1:
            return resident(every, backs, latents)
        return resident(every, backs, latents, [2 * following[0] + 1])

    def tied(*values):
        return lax.optimization_barrier(values)

    def advance(before, following, got, state, weights, earlier=None):
        mode = "first" if before == (0,) else "later" if earlier is not None else "pair"
        count = len(following) + (len(following) == 2)
        shapes = [
            (array if mode == "first" else far)(wide, share, LANES + count * lat),
            near(mine, local_width),
            far(wide, high, lat) if mode == "first" else far(mine, 2 * lat),
        ]
        operands = [got, state] + [in_vmem(weight) for weight in weights]
        in_specs = [whole(got.shape), whole(state.shape)]
        in_specs += [whole(weight.shape) for weight in weights]
        if mode == "later":
            in_specs.append(whole(earlier.shape))
            operands.append(earlier)
        return call(
            functools.partial(advance_kernel, before, following, mode),
            in_specs,
            [whole(s.shape) for s in shapes],
            shapes,
            operands,
            flops=2 * (len(before) + count) * mine * lat * local_width,
        )

    def pair_step(got, crosses, copies):
        (sent,) = call(
            functools.partial(pair_kernel, width),
            [whole(got.shape), whole(crosses[0].shape)],
            [whole((copies, share, 2 * lat))],
            [array(copies, share, 2 * lat)],
            [got, in_vmem(crosses[0])],
            flops=2 * 2 * share * lat * lat,
        )
        return sent

    got, weights = tied(exchanged(sent, "wide"), resident_weights((0,), (1,)))

    earlier = got
    sent, state, cross = advance((0,), (1,), got, state, weights)
    crosses = lax.all_gather(cross.reshape(lat, lat), "segment", axis=0)
    got, weights = tied(exchanged(sent, "wide"), resident_weights((1,), (2, 3)))
    (sent,) = call(
        functools.partial(single_kernel, width),
        [whole(got.shape)],
        [whole((wide, share, lat))],
        [array(wide, share, lat)],
        [got],
    )
    got = exchanged(sent, "wide")

    pages = []
    for even in range(2, layers, 2):
        odd = even + 1
        before = (1,) if even == 2 else (even - 2, even - 1)
        extra = earlier if even == 2 else None
        sent, state, held = advance(before, (even, odd), got, state, weights, extra)
        pages.append(lax.all_gather(held, "segment", axis=0))
        if odd < layers - 1:
            following = resident_weights((even, odd), (even + 2, even + 3))
            mixing = resident(crosses, [even, odd])
            got, mixing, weights = tied(exchanged(sent, "wide"), mixing, following)
            got = exchanged(pair_step(got, mixing, wide), "wide")
        else:
            got, mixing = tied(exchanged(sent, "wide"), resident(crosses, [even, odd]))

    targets = page_lists[:, :, 0]
    owned = targets == position
    counts = jnp.sum(owned.astype(jnp.int32), axis=1)
    none = targets.shape[1]
    order = jnp.arange(none, dtype=jnp.int32)[None, :]
    slot0 = jnp.min(jnp.where(owned, order, none), axis=1)
    slot1 = jnp.min(jnp.where(owned & (order > slot0[:, None]), order, none), axis=1)
    slots = jnp.minimum(jnp.stack([slot0, slot1], axis=1), none - 1).reshape(-1)
    limit = jnp.minimum(context_lengths, counts[None, :] * PAGE)
    limit = jnp.repeat(limit.T, queries.shape[2], axis=1)[:, :, None]
    new = new_latent.transpose(1, 0, 2)
    hot = slots[2 * layers - 4 :, None] == jnp.arange(none, dtype=jnp.int32)[None, :]
    hot = jnp.broadcast_to(hot.astype(f32).reshape(4 * none, 1), (4 * none, LANES))

    def decode(layer, pages, carried, last=False):
        return decode_pair(layer, slots, queries, new, limit, pages, carried, last)

    out = decode(0, pages[0], None)
    got, out, hot = lax.optimization_barrier((got, out, in_vmem(hot)))

    got = exchanged(pair_step(got, mixing, segments), "segment")
    (sent,) = call(
        choose_kernel,
        [whole(got.shape), whole(hot.shape)],
        [whole((wide, share, 4 * lat))],
        [array(wide, share, 4 * lat)],
        [got, hot],
    )
    got = exchanged(sent, "wide")
    out = decode(4, pages[2], decode(2, pages[1], out))
    got, out = lax.optimization_barrier((got, out))
    return decode(layers - 2, got, out, True)


def solution(mesh):
    in_specs = (
        P(None, None, "wide"),
        P("segment", "wide"),
        P("segment", "wide", None),
        P("segment", None, "wide"),
        P(),
        P("segment", None, "wide", None),
        P("segment", None, None),
        P("segment", None),
    )
    out_specs = P("segment", None, "wide", None)
    return jax.shard_map(shards, mesh=mesh, in_specs=in_specs, out_specs=out_specs, check_vma=False)
```

```python
import functools
import math

import jax
import jax.numpy as jnp
from jax import lax
from jax.experimental import pallas as pl
from jax.experimental.pallas import tpu as pltpu
from jax.sharding import PartitionSpec as P

PAGE = 128
LANES = 128

eps_norm = 1e-06
score_scale = 192.0 ** (-0.5)

params = pltpu.CompilerParams(vmem_limit_bytes=24 * 1024 * 1024)
in_hbm = pl.BlockSpec(memory_space=pltpu.HBM)
bf16 = jnp.bfloat16
f32 = jnp.float32


def dot(a, b):
    return jnp.dot(a, b, preferred_element_type=jnp.float32)


def dot_t(a, b):
    return lax.dot_general(a, b, (((1,), (1,)), ((), ())), preferred_element_type=jnp.float32)


def square_columns(values):
    squares = jnp.sum(values * values, axis=1, keepdims=True)
    high = squares.astype(bf16).astype(f32)
    column = lax.broadcasted_iota(jnp.int32, (values.shape[0], LANES), 1)
    return jnp.where(column == 0, high, jnp.where(column == 1, squares - high, 0.0))


def silu(latent):
    values = latent.astype(f32)
    return (values / (1.0 + jnp.exp(-values))).astype(bf16)


def exchanged(sent, axis):
    return lax.all_to_all(sent, axis, 0, 0, tiled=True)


def core_swap(x):
    length = lax.axis_size("segment")
    return lax.ppermute(x, "segment", [(i, i ^ 1) for i in range(length)])


def held_in_hbm(x):
    return pltpu.with_memory_space_constraint(x, pltpu.HBM)


def in_vmem(x):
    return pltpu.with_memory_space_constraint(x, pltpu.VMEM)


def whole(shape):
    return pl.BlockSpec(shape, lambda i, *s: (0,) * len(shape))


def call(body, in_specs, out_specs, out_shape, operands, scalars=(), scratch=(), flops=0):
    moved = sum(2 * math.prod(o.shape) for o in out_shape)
    return pl.pallas_call(
        body,
        grid_spec=pltpu.PrefetchScalarGridSpec(
            num_scalar_prefetch=len(scalars),
            grid=(1,),
            in_specs=in_specs,
            out_specs=out_specs,
            scratch_shapes=scratch,
        ),
        out_shape=out_shape,
        compiler_params=params,
        cost_estimate=pl.CostEstimate(flops=flops, bytes_accessed=2 * moved, transcendentals=0),
    )(*scalars, *operands)


def weights_kernel(where, latent_ref, gain_ref, back_ref, both_ref, lent_ref, *scratch):
    latent, gain, pair, sems = scratch
    size = latent.shape[0]
    half = size // 2
    halves = [pl.ds(i * half, half) for i in range(2)]
    copies = [
        pltpu.make_async_copy(gain_ref, gain, sems.at[0]),
        pltpu.make_async_copy(latent_ref.at[0, halves[0]], latent.at[halves[0]], sems.at[1]),
        pltpu.make_async_copy(latent_ref.at[0, halves[1]], latent.at[halves[1]], sems.at[2]),
        pltpu.make_async_copy(back_ref.at[0], pair.at[1], sems.at[3]),
    ]
    for copy in copies:
        copy.start()
    copies[0].wait()
    gains = jnp.broadcast_to(gain[...].astype(f32), (8, size)).T[:, :1]
    sending = []
    for i, rows in enumerate(halves):
        copies[1 + i].wait()
        scaled = latent[rows].astype(f32) * gains[i * half : (i + 1) * half]
        pair[0, rows] = scaled.astype(bf16)
        to = both_ref.at[0, rows]
        sending.append(pltpu.make_async_copy(pair.at[0, rows], to, sems.at[4 + i]))
        sending[i].start()
    copies[3].wait()
    sending.append(pltpu.make_async_copy(pair.at[1], both_ref.at[1], sems.at[6]))
    sending[2].start()

    @pl.when(where[0] == 0)
    def _():
        lent_ref[...] = pair[0]

    @pl.when(where[0] != 0)
    def _():
        lent_ref[...] = pair[1]

    for copy in sending:
        copy.wait()


def home_kernel(where, states_ref, mine_ref, lent_ref, *out_refs):
    groups, _, rows, width = states_ref.shape

    def products(weight_ref):
        tokens = states_ref[:, where[1]].reshape(groups * rows, width)
        product = dot(tokens, weight_ref[...]).astype(bf16)
        for group in range(groups):
            out_refs[group][...] = product[group * rows : (group + 1) * rows]

    @pl.when(where[0] == 0)
    def _():
        products(mine_ref)

    @pl.when(where[0] != 0)
    def _():
        products(lent_ref)


def cross_kernel(where, both_ref, lent_ref, out_ref):
    @pl.when(where[0] & 1 == 0)
    def _():
        out_ref[...] = dot_t(both_ref[1], both_ref[1]).astype(bf16)

    @pl.when(where[0] & 1 != 0)
    def _():
        out_ref[...] = dot(lent_ref[...], both_ref[0]).astype(bf16)


def home_send_kernel(
    where, home_ref, a_ref, b_ref, c_ref, cross_ref, states_ref, out_ref, state_ref
):
    wide, share, _ = out_ref.shape
    rows, lat = home_ref.shape
    taken = a_ref[...].astype(f32) + b_ref[...].astype(f32) + c_ref[...].astype(f32)
    product = jnp.where(where[0] < 2, home_ref[...].astype(f32), taken)
    state = states_ref[where[0] >> 1, where[1]]
    state_ref[...] = state
    squares = square_columns(state.astype(f32))
    out_ref[:, :, :LANES] = squares.reshape(wide, share, LANES).astype(bf16)
    out_ref[:, :, LANES : LANES + lat] = product.reshape(wide, share, lat).astype(bf16)
    parts = cross_ref.shape[0] // rows
    cross = cross_ref[...].astype(f32).reshape(wide, parts, share, lat)
    for part in range(parts):
        at = LANES + (1 + part) * lat
        out_ref[:, :, at : at + lat] = cross[:, part].astype(bf16)


def home_sum_kernel(width, got_ref, out_ref):
    wide, high, lat = out_ref.shape
    summed = jnp.sum(got_ref[...].astype(f32), axis=0)
    squares = summed[:, 0:1] + summed[:, 1:2]
    latent = summed[:, LANES : LANES + lat] * lax.rsqrt(squares / width + eps_norm)
    parts = [summed[:, at : at + lat] for at in range(LANES + lat, summed.shape[1], lat)]
    block = jnp.concatenate(parts + [latent], axis=0).astype(bf16)
    for place in range(wide):
        out_ref[place] = block


def single_kernel(width, got_ref, out_ref):
    summed = jnp.sum(got_ref[...].astype(f32), axis=0)
    squares = summed[:, 0:1] + summed[:, 1:2]
    latent = (summed[:, LANES:] * lax.rsqrt(squares / width + eps_norm)).astype(bf16)
    for place in range(out_ref.shape[0]):
        out_ref[place] = latent


def chain(width, summed, gram, mixing):
    lat = (summed.shape[1] - LANES) // 3
    squares = summed[:, 0:1] + summed[:, 1:2]
    at = [LANES + i * lat for i in range(4)]
    first = (summed[:, at[0] : at[1]] * lax.rsqrt(squares / width + eps_norm)).astype(bf16)
    activated = silu(first)
    towards = 2.0 * summed[:, at[2] : at[3]] + dot(activated, gram())
    squares = squares + jnp.sum(activated.astype(f32) * towards, axis=1, keepdims=True)
    squares = jnp.maximum(squares, 0.0)
    second = summed[:, at[1] : at[2]] + dot(activated, mixing())
    second = (second * lax.rsqrt(squares / width + eps_norm)).astype(bf16)
    return first, second


def reside_kernel(lists, source_ref, *rest):
    out_refs, sems = rest[:-1], rest[-1]
    copies = []
    for out_ref, slots in zip(out_refs, lists):
        for i, slot in enumerate(slots):
            sem = sems.at[len(copies)]
            copies.append(pltpu.make_async_copy(source_ref.at[slot], out_ref.at[i], sem))
    for copy in copies:
        copy.start()
    for copy in copies:
        copy.wait()


def advance_kernel(before, layers, mode, got_ref, states_ref, *rest):
    refs = rest[: 1 + len(layers)]
    back_ref, latent_ref = refs[:2]
    outs = rest[len(refs) :]
    if mode == "later":
        earlier_ref, outs = outs[0], outs[1:]
    out_ref, state_ref, held_ref = outs[:3]
    wide, share, _ = out_ref.shape
    rows = wide * share
    lat = back_ref.shape[2]

    def latents_of(ref):
        block = ref[:, ref.shape[1] - share :]
        return block.astype(f32).reshape(rows, ref.shape[2])

    latents = latents_of(got_ref)
    activated = silu(latents)
    state = states_ref[...].astype(f32)
    for i in range(len(before)):
        state = state + dot(activated[:, i * lat : (i + 1) * lat], back_ref[i])
    state = state.astype(bf16)
    state_ref[...] = state
    squares = square_columns(state.astype(f32))
    out_ref[:, :, :LANES] = squares.reshape(wide, share, LANES).astype(bf16)
    products = [dot(state, latent_ref[i]) for i in range(len(layers))]
    if len(layers) == 2:
        products.append(dot_t(state, refs[2][0]))
    for i, product in enumerate(products):
        at = LANES + i * lat
        out_ref[:, :, at : at + lat] = product.reshape(wide, share, lat).astype(bf16)
    if mode == "first":
        held_ref[...] = got_ref[:, : got_ref.shape[1] - share]
    elif mode == "later":
        held_ref[:, :lat] = latents_of(earlier_ref).astype(bf16)
        held_ref[:, lat:] = latents.astype(bf16)
    else:
        held_ref[...] = latents.astype(bf16)


def pair_kernel(width, got_ref, cross_ref, out_ref):
    summed = jnp.sum(got_ref[...].astype(f32), axis=0)
    first, second = chain(width, summed, lambda: cross_ref[0], lambda: cross_ref[1])
    lat = first.shape[1]
    for place in range(out_ref.shape[0]):
        out_ref[place, :, :lat] = first
        out_ref[place, :, lat:] = second


def choose_kernel(got_ref, hot_ref, out_ref):
    pages = got_ref.shape[0]
    lat = got_ref.shape[2] // 2
    parts = []
    for i in range(2):
        for which in range(2):
            at = (2 * i + which) * pages
            part = jnp.zeros((got_ref.shape[1], lat), f32)
            for page in range(pages):
                shard = got_ref[page, :, i * lat : (i + 1) * lat].astype(f32)
                part = jnp.where(hot_ref[at + page : at + page + 1, :1] > 0, shard, part)
            parts.append(part.astype(bf16))
    for place in range(out_ref.shape[0]):
        for i, part in enumerate(parts):
            out_ref[place, :, i * lat : (i + 1) * lat] = part


def own_rows(new, rows, heads):
    requests = new.shape[0]
    row = lax.broadcasted_iota(jnp.int32, (rows, requests), 0)
    start = lax.broadcasted_iota(jnp.int32, (rows, requests), 1) * heads
    pick = jnp.where((row >= start) & (row < start + heads), 1.0, 0.0).astype(bf16)
    return dot(pick, new)


def attend(q, own, keys, limit):
    scores = dot_t(q, keys) * score_scale
    place = lax.broadcasted_iota(jnp.int32, scores.shape, 1)
    scores = jnp.where(place < limit, scores, -jnp.inf)
    own_score = jnp.sum(q.astype(f32) * own, axis=1, keepdims=True) * score_scale
    top = jnp.maximum(jnp.max(scores, axis=1, keepdims=True), own_score)
    weights = jnp.exp(scores - top)
    own_weight = jnp.exp(own_score - top)
    total = jnp.sum(weights, axis=1, keepdims=True) + own_weight
    numer = dot(weights.astype(bf16), keys) + own_weight * own
    return (numer / total).astype(bf16)


def decode_kernel(layer, slots, q_ref, new_ref, limit_ref, pages_ref, *rest):
    out_ref, keys, sems = rest[-3:]
    requests, count, heads, lat = q_ref.shape
    copies = []
    for i in range(count):
        for which in range(2):
            page = pages_ref.at[slots[2 * (layer + i) + which], :, pl.ds(i * lat, lat)]
            at = keys.at[i, pl.ds(which * PAGE, PAGE)]
            copies.append(pltpu.make_async_copy(page, at, sems.at[2 * i + which]))
    for copy in copies:
        copy.start()
    for i in range(count):
        q = q_ref[:, i].reshape(requests * heads, lat)
        copies[2 * i].wait()
        copies[2 * i + 1].wait()
        own = own_rows(new_ref[i], requests * heads, heads)
        result = attend(q, own, keys[i], limit_ref[i])
        out_ref[:, i] = result.reshape(requests, heads, lat)


def last_decode_kernel(layer, q_ref, new_ref, limit_ref, pages_ref, carried_ref, out_ref):
    requests, count, heads, lat = out_ref.shape
    for i in range(count):
        q = q_ref[:, layer + i].reshape(requests * heads, lat)
        at = 2 * i * lat
        pages = pages_ref[:, :, at : at + 2 * lat].astype(f32).reshape(PAGE, 2 * lat)
        keys = jnp.concatenate([pages[:, :lat], pages[:, lat:]], axis=0).astype(bf16)
        own = new_ref[i].astype(f32)
        result = attend(q, own, keys, limit_ref[layer + i])
        out_ref[:, i] = result.reshape(requests, heads, lat)


def decode_pair(layer, slots, queries, new, limit, pages, carried, last=False):
    requests, _, heads, lat = queries.shape
    half = layer // 2
    in_specs = [
        pl.BlockSpec((requests, 2, heads, lat), lambda i, *s: (0, half, 0, 0)),
        pl.BlockSpec((2, requests, lat), lambda i, *s: (half, 0, 0)),
        pl.BlockSpec((2, requests * heads, 1), lambda i, *s: (half, 0, 0)),
        whole(pages.shape) if last else in_hbm,
    ]
    scalars = [] if last else [slots]
    operands = scalars + [queries, new, limit, pages if last else held_in_hbm(pages)]
    if last:
        in_specs[:3] = [whole(operand.shape) for operand in operands[:3]]
        operands[0], operands[2] = in_vmem(queries), in_vmem(limit)
    aliases = {}
    if carried is not None:
        in_specs.append(in_hbm)
        aliases = {len(operands): 0}
        operands.append(carried)
    scratch = [pltpu.VMEM((2, 2 * PAGE, lat), bf16), pltpu.SemaphoreType.DMA((4,))]
    return pl.pallas_call(
        functools.partial(last_decode_kernel if last else decode_kernel, layer),
        grid_spec=pltpu.PrefetchScalarGridSpec(
            num_scalar_prefetch=len(scalars),
            grid=(1,),
            in_specs=in_specs,
            out_specs=pl.BlockSpec((requests, 2, heads, lat), lambda i, *s: (0, half, 0, 0)),
            scratch_shapes=[] if last else scratch,
        ),
        out_shape=jax.ShapeDtypeStruct(queries.shape, bf16),
        input_output_aliases=aliases,
        compiler_params=params,
        cost_estimate=pl.CostEstimate(
            flops=2 * 4 * requests * heads * 2 * PAGE * lat,
            bytes_accessed=2 * 2 * (2 * requests * heads + 2 * PAGE) * lat,
            transcendentals=2 * requests * heads * 2 * PAGE,
        ),
    )(*operands)


def shards(
    prompt_states, norm_gain, w_latent, w_back, page_lists, queries, new_latent, context_lengths
):
    segments = lax.axis_size("segment")
    wide = lax.axis_size("wide")
    position = lax.axis_index("segment")
    core = position & 1
    batches, tok_rows, local_width = prompt_states.shape
    width = local_width * wide
    tokens = batches * tok_rows
    mine = tokens // segments
    share = mine // wide
    layers = segments
    lat = w_latent.shape[2]
    where = jnp.stack([position, core]).astype(jnp.int32)

    def array(*shape):
        return jax.ShapeDtypeStruct(shape, bf16)

    def near(*shape):
        return pltpu.VMEM(shape, bf16)

    def far(*shape):
        return pltpu.HBM(shape, bf16)

    size = (2, local_width, lat)
    both, mine_lent = call(
        weights_kernel,
        [in_hbm] * 3,
        [in_hbm, whole(size[1:])],
        [far(*size), near(*size[1:])],
        [held_in_hbm(w_latent), held_in_hbm(norm_gain), held_in_hbm(w_back)],
        [where],
        [
            pltpu.VMEM(size[1:], bf16),
            pltpu.VMEM(norm_gain.shape, bf16),
            pltpu.VMEM(size, bf16),
            pltpu.SemaphoreType.DMA((7,)),
        ],
    )
    every = lax.all_gather(both, "segment", axis=0)
    lent = lax.ppermute(mine_lent, "segment", [(i, i + 1) for i in range(0, segments, 2)])

    states = prompt_states.reshape(segments // 2, 2, mine, local_width)
    groups = segments // 2
    home = call(
        home_kernel,
        [whole(states.shape), whole(size[1:]), whole(size[1:])],
        [whole((mine, lat))] * groups,
        [near(mine, lat)] * groups,
        [in_vmem(states), in_vmem(mine_lent), lent],
        [where],
        flops=2 * local_width**3,
    )
    (cross,) = call(
        cross_kernel,
        [whole(size), whole(size[1:])],
        [whole((lat, lat))],
        [near(lat, lat)],
        [both, lent],
        [where],
        flops=2 * local_width**3,
    )
    taken = [
        lax.ppermute(home[hop], "segment", [(0, 2 * hop), (1, 2 * hop + 1)])
        for hop in range(1, groups)
    ]
    high = lat // wide
    columns = LANES + lat + high // share * lat
    sent, state = call(
        home_send_kernel,
        [whole((mine, lat))] * groups + [whole((lat, lat)), whole(states.shape)],
        [whole((wide, share, columns)), whole((mine, local_width))],
        [array(wide, share, columns), near(mine, local_width)],
        [home[0]] + taken + [cross, in_vmem(states)],
        [where],
    )
    got = exchanged(sent, "wide")
    (sent,) = call(
        functools.partial(home_sum_kernel, width),
        [whole(got.shape)],
        [whole((wide, high + share, lat))],
        [array(wide, high + share, lat)],
        [got],
    )
    def resident(source, *lists):
        parts = source.reshape((-1,) + source.shape[-2:])
        count = sum(len(slots) for slots in lists)
        return pl.pallas_call(
            functools.partial(reside_kernel, lists),
            in_specs=[in_hbm],
            out_specs=[pl.BlockSpec(memory_space=pltpu.VMEM)] * len(lists),
            out_shape=[pltpu.VMEM((len(slots),) + parts.shape[1:], bf16) for slots in lists],
            scratch_shapes=[pltpu.SemaphoreType.DMA((count,))],
            compiler_params=params,
            cost_estimate=pl.CostEstimate(
                flops=0, bytes_accessed=2 * count * parts.shape[1] * lat, transcendentals=0
            ),
        )(held_in_hbm(parts))

    def resident_weights(before, following):
        backs = [2 * layer + 1 for layer in before]
        latents = [2 * layer for layer in following]
        if len(following) == 1:
            return resident(every, backs, latents)
        return resident(every, backs, latents, [2 * following[0] + 1])

    def tied(*values):
        return lax.optimization_barrier(values)

    def advance(before, following, got, state, weights, earlier=None):
        mode = "first" if before == (0,) else "later" if earlier is not None else "pair"
        count = len(following) + (len(following) == 2)
        shapes = [
            (array if mode == "first" else far)(wide, share, LANES + count * lat),
            near(mine, local_width),
            far(wide, high, lat) if mode == "first" else far(mine, 2 * lat),
        ]
        operands = [got, state] + [in_vmem(weight) for weight in weights]
        in_specs = [whole(got.shape), whole(state.shape)]
        in_specs += [whole(weight.shape) for weight in weights]
        if mode == "later":
            in_specs.append(whole(earlier.shape))
            operands.append(earlier)
        return call(
            functools.partial(advance_kernel, before, following, mode),
            in_specs,
            [whole(s.shape) for s in shapes],
            shapes,
            operands,
            flops=2 * (len(before) + count) * mine * lat * local_width,
        )

    def pair_step(got, crosses, copies):
        (sent,) = call(
            functools.partial(pair_kernel, width),
            [whole(got.shape), whole(crosses[0].shape)],
            [whole((copies, share, 2 * lat))],
            [array(copies, share, 2 * lat)],
            [got, in_vmem(crosses[0])],
            flops=2 * 2 * share * lat * lat,
        )
        return sent

    got, weights = tied(exchanged(sent, "wide"), resident_weights((0,), (1,)))

    earlier = got
    sent, state, cross = advance((0,), (1,), got, state, weights)
    crosses = lax.all_gather(cross.reshape(lat, lat), "segment", axis=0)
    got, weights = tied(exchanged(sent, "wide"), resident_weights((1,), (2, 3)))
    (sent,) = call(
        functools.partial(single_kernel, width),
        [whole(got.shape)],
        [whole((wide, share, lat))],
        [array(wide, share, lat)],
        [got],
    )
    got = exchanged(sent, "wide")

    pages = []
    for even in range(2, layers, 2):
        odd = even + 1
        before = (1,) if even == 2 else (even - 2, even - 1)
        extra = earlier if even == 2 else None
        sent, state, held = advance(before, (even, odd), got, state, weights, extra)
        pages.append(lax.all_gather(held, "segment", axis=0))
        if odd < layers - 1:
            following = resident_weights((even, odd), (even + 2, even + 3))
            mixing = resident(crosses, [even, odd])
            got, mixing, weights = tied(exchanged(sent, "wide"), mixing, following)
            got = exchanged(pair_step(got, mixing, wide), "wide")
        else:
            got, mixing = tied(exchanged(sent, "wide"), resident(crosses, [even, odd]))

    targets = page_lists[:, :, 0]
    owned = targets == position
    counts = jnp.sum(owned.astype(jnp.int32), axis=1)
    none = targets.shape[1]
    order = jnp.arange(none, dtype=jnp.int32)[None, :]
    slot0 = jnp.min(jnp.where(owned, order, none), axis=1)
    slot1 = jnp.min(jnp.where(owned & (order > slot0[:, None]), order, none), axis=1)
    slots = jnp.minimum(jnp.stack([slot0, slot1], axis=1), none - 1).reshape(-1)
    limit = jnp.minimum(context_lengths, counts[None, :] * PAGE)
    limit = jnp.repeat(limit.T, queries.shape[2], axis=1)[:, :, None]
    new = new_latent.transpose(1, 0, 2)
    hot = slots[2 * layers - 4 :, None] == jnp.arange(none, dtype=jnp.int32)[None, :]
    hot = jnp.broadcast_to(hot.astype(f32).reshape(4 * none, 1), (4 * none, LANES))

    def decode(layer, pages, carried, last=False):
        return decode_pair(layer, slots, queries, new, limit, pages, carried, last)

    out = decode(0, pages[0], None)
    rows = jnp.repeat(new[layers - 2 :], queries.shape[2], axis=1)
    got, out, hot, rows = lax.optimization_barrier((got, out, in_vmem(hot), in_vmem(rows)))

    got = exchanged(pair_step(got, mixing, segments), "segment")
    (sent,) = call(
        choose_kernel,
        [whole(got.shape), whole(hot.shape)],
        [whole((wide, share, 4 * lat))],
        [array(wide, share, 4 * lat)],
        [got, hot],
    )
    got = exchanged(sent, "wide")
    out = decode(4, pages[2], decode(2, pages[1], out))
    got, out = lax.optimization_barrier((got, out))
    return decode_pair(layers - 2, slots, queries, rows, limit, got, out, True)


def solution(mesh):
    in_specs = (
        P(None, None, "wide"),
        P("segment", "wide"),
        P("segment", "wide", None),
        P("segment", None, "wide"),
        P(),
        P("segment", None, "wide", None),
        P("segment", None, None),
        P("segment", None),
    )
    out_specs = P("segment", None, "wide", None)
    return jax.shard_map(shards, mesh=mesh, in_specs=in_specs, out_specs=out_specs, check_vma=False)
```
